128 devices in a mesh: dp: 8 (over x, y_lo), section: 4 (over z), tensor: 4 (over y_hi, core).
Axes of the slice: x: 4, y: 4 (y_hi: 2, y_lo: 2; y = y_hi * 2 + y_lo), z: 4, core: 2. Of those that a mesh axis runs over, the one named last changes fastest.
Arguments:
- hidden_in: bfloat16 [16, 1024, 768], P('dp', 'tensor'), may hold values from -6 to 6
- segments: int32 [16, 1024], P('dp'), may hold values from 0 to 1023, as said below
- timestep: int32 [16], P('dp'), may hold values from 0 to 999
- w_qkv: bfloat16 [2, 768, 2304], P(None, None, 'tensor'), may hold values from -0.21875 to 0.21875
- w_out: bfloat16 [2, 768, 768], P(None, 'tensor'), may hold values from -1.75 to 1.75
- w_up: bfloat16 [2, 768, 3072], P(None, None, 'tensor'), may hold values from -0.21875 to 0.21875
- w_down: bfloat16 [2, 3072, 768], P(None, 'tensor'), may hold values from -0.109375 to 0.109375
- w_mod: bfloat16 [2, 128, 4608], replicated, may hold values from -0.375 to 0.375
- b_mod: bfloat16 [2, 4608], replicated, may hold values from -3 to 3
- cotangent: bfloat16 [4, 16, 1024, 768], P('section', 'dp', 'tensor'), may hold values from -6 to 6
Outputs:
- layer_outputs: bfloat16 [4, 16, 1024, 768], P('section', 'dp', 'tensor')
- section_grads: float32 [4, 16, 1024, 768], P('section', 'dp', 'tensor')
- grad_qkv: float32 [2, 768, 2304], P(None, None, 'tensor')
- grad_out: float32 [2, 768, 768], P(None, 'tensor')
- grad_up: float32 [2, 768, 3072], P(None, None, 'tensor')
- grad_down: float32 [2, 3072, 768], P(None, 'tensor')
- grad_mod: float32 [2, 128, 4608], replicated
- grad_bias: float32 [2, 4608], replicated
The draws below stay inside these ranges and needn't reach their ends.
Inputs may be any that keep to these rules, and one draw needn't show every extreme that they name: `segments`: segment numbers of a row start at 0 and never fall; equal numbers mark one document; the last document of every row has the number 1024 - 1.
All inputs are finite; a program needn't handle non-finite values.
Results may differ from the reference program's by a relative error of at most 0.025.
Values may be sent and summed in bfloat16 or wider, within the bound.
A program may use at most 192 MiB of HBM per device.

```python
import math
import jax
import jax.numpy as jnp
from jax import lax

D = 768
HEADS = 12
HEAD_SIZE = 64
FF = 3072
TDIM = 128
SEQ = 1024
LAYERS = 2
ROWS_ALL = 16
APPLICATIONS = 4
N_TENSOR = 4


def draw_segments(key, part):
    key = jax.random.fold_in(key, 11)
    first_key, second_key, third_key = jax.random.split(key, 3)
    local_len = SEQ // N_TENSOR
    doc_start = jax.random.randint(first_key, (ROWS_ALL, 1), 1, local_len)
    doc_stop = jax.random.randint(second_key, (ROWS_ALL, 1), 3 * local_len + 1, SEQ + 1)
    marks = jax.random.randint(third_key, (ROWS_ALL, SEQ), 0, max(SEQ // 32, 2))
    position = jnp.arange(SEQ)[None, :]
    inside = (position > doc_start) & (position < doc_stop)
    edges = (position == doc_start) | (position == doc_stop)
    quiet = inside | (position == 0)
    flags = jnp.where(edges, 1, jnp.where(quiet, 0, (marks == 0).astype(jnp.int32)))
    numbers = jnp.cumsum(flags, axis=1).astype(jnp.int32)
    last_number = numbers[:, SEQ - 1:SEQ]
    return jnp.where(numbers == last_number, SEQ - 1, numbers).astype(jnp.int32)


def set_ends(array, own_key, smallest, high):
    extent = array.shape
    place = [jax.random.randint(jax.random.fold_in(own_key, axis), (), 0, extent[axis]) for axis in range(len(extent))]
    array = array.at[tuple(place)].set(smallest)
    longest = extent.index(max(extent))
    place[longest] = (place[longest] + 1) % extent[longest]
    return array.at[tuple(place)].set(high)


def levels(stream_key, dims, cuts, low, high):
    level, own = 1.0, jax.random.fold_in(stream_key, 6)
    for dim, shards_of in cuts:
        draws = jnp.exp(jax.random.uniform(jax.random.fold_in(own, dim), (shards_of,), jnp.float32, low / len(cuts), high / len(cuts)))
        level = level * jnp.repeat(draws, dims[dim] // shards_of).reshape([-1 if axis == dim else 1 for axis in range(len(dims))])
    return level


def scatter_about(stream_key, dims, scale, limit, pieces=(), kind=jnp.bfloat16):
    result = jax.random.normal(stream_key, dims, jnp.float32) * scale
    if len(pieces) > 0:
        result = levels(stream_key, dims, pieces, -0.22, 0.18) * result
    return jnp.clip(result, min=-limit, max=limit).astype(kind)


def setup_inputs(seed: int = 0) -> dict:
    keys = jax.random.split(jax.random.key(seed), 11)
    return {
        "hidden_in": scatter_about(keys[0], (ROWS_ALL, SEQ, D), 1.0, 6.0, ((0, 8), (1, 4))),
        "segments": draw_segments(jax.random.fold_in(keys[10], 71), 0),
        "timestep": set_ends(jax.random.randint(keys[2], (ROWS_ALL,), 0, 1000), jax.random.fold_in(keys[2], 1), 0, 999).astype(jnp.int32),
        "w_qkv": scatter_about(keys[3], (LAYERS, D, 3 * D), D ** -0.5, 0.21875, ((2, 4),)),
        "w_out": scatter_about(keys[4], (LAYERS, D, D), (D // 64) ** -0.5, 1.75, ((1, 4),)),
        "w_up": scatter_about(keys[5], (LAYERS, D, FF), D ** -0.5, 0.21875, ((2, 4),)),
        "w_down": scatter_about(keys[6], (LAYERS, FF, D), FF ** -0.5, 0.109375, ((1, 4),)),
        "w_mod": scatter_about(keys[7], (LAYERS, TDIM, 6 * D), (TDIM * 2) ** -0.5, 0.375),
        "b_mod": scatter_about(keys[8], (LAYERS, 6 * D), 0.5, 3.0),
        "cotangent": scatter_about(keys[9], (APPLICATIONS, ROWS_ALL, SEQ, D), 1.0, 6.0, ((0, 4), (1, 8), (2, 4))),
    }


@jax.custom_vjp
def low(v):
    return lax.optimization_barrier(v.astype(jnp.bfloat16)).astype(jnp.float32)

@jax.custom_vjp
def low_back(v):
    return v

def low_keep(v):
    return (low(v), None)

def low_pass(kept, grad):
    return (grad,)

def back_keep(v):
    return (v, None)

def back_low(kept, grad):
    return (low(grad),)
low.defvjp(low_keep, low_pass)
low_back.defvjp(back_keep, back_low)
highest = lax.Precision.HIGHEST
norm_epsilon = 1e-06

def time_features(step_values, feature_count):
    half_count = feature_count // 2
    frequency = jnp.exp(-math.log(10000.0) * jnp.arange(half_count, dtype=jnp.float32) / half_count)
    angles = step_values.astype(jnp.float32)[:, None] * frequency[None, :]
    return jnp.concatenate([jnp.cos(angles), jnp.sin(angles)], axis=1)

def rotary_tables(length, table_size):
    half_size = table_size // 2
    frequency = jnp.exp(-math.log(10000.0) * jnp.arange(half_size, dtype=jnp.float32) / half_size)
    angles = jnp.arange(length, dtype=jnp.float32)[:, None] * frequency[None, :]
    return (jnp.cos(angles), jnp.sin(angles))

def rotate(tensor, cosine, sine_table):
    half_size = tensor.shape[-1] // 2
    first_half = tensor[..., :half_size]
    second_half = tensor[..., half_size:]
    cos_part = cosine[:, None, :]
    sin_part = sine_table[:, None, :]
    return jnp.concatenate([first_half * cos_part - second_half * sin_part, second_half * cos_part + first_half * sin_part], axis=-1)

def normalize(values):
    centred = values - lax.optimization_barrier(jnp.mean(values, axis=-1, keepdims=True))
    return centred * lax.rsqrt(lax.optimization_barrier(jnp.mean(centred * centred, axis=-1, keepdims=True)) + norm_epsilon)

def attention(query_rows, key_rows, values, segment_ids):
    block_rows = min(512, SEQ)
    block_count = SEQ // block_rows

    def one_block(operands):
        query_block, segment_block = operands
        scores = low_back(jnp.einsum('qhd,khd->hqk', query_block, key_rows, precision=highest) * HEAD_SIZE ** (-0.5))
        same_doc = segment_block[:, None] == segment_ids[None, :]
        scores = jnp.where(same_doc[None, :, :], scores, -1e+30)
        shifted = jnp.exp(scores - lax.optimization_barrier(jnp.max(scores, axis=-1, keepdims=True)))
        weights = low(shifted / lax.optimization_barrier(jnp.sum(shifted, axis=-1, keepdims=True)))
        return jnp.einsum('hqk,khd->qhd', weights, values, precision=highest)
    stacked = lax.map(jax.checkpoint(one_block), (query_rows.reshape(block_count, block_rows, HEADS, HEAD_SIZE), segment_ids.reshape(block_count, block_rows)))
    return stacked.reshape(SEQ, HEADS * HEAD_SIZE)

def apply_layer(params, which, layer_in, features, segment_ids, cosine, sine_table):
    weight_qkv, weight_out, weight_up, weight_down, weight_mod, bias_mod = params
    modulation = jnp.dot(features, weight_mod[which], precision=highest) + bias_mod[which]
    shift_a, scale_a, gate_a, shift_b, scale_b, gate_b = jnp.split(modulation, 6)
    normed_a = low(normalize(layer_in) * (1.0 + scale_a) + shift_a)
    projected = low_back(jnp.dot(normed_a, weight_qkv[which], precision=highest)).reshape(SEQ, HEADS, 3, HEAD_SIZE)
    query_rows = low(rotate(projected[:, :, 0], cosine, sine_table))
    key_rows = low(rotate(projected[:, :, 1], cosine, sine_table))
    values = low(projected[:, :, 2])
    attended = low_back(low(attention(query_rows, key_rows, values, segment_ids)))
    branch_a = low_back(jnp.dot(attended, weight_out[which], precision=highest))
    middle = layer_in + gate_a * branch_a
    normed_b = low(normalize(middle) * (1.0 + scale_b) + shift_b)
    activated = low(jax.nn.gelu(low_back(jnp.dot(normed_b, weight_up[which], precision=highest)), approximate=True))
    branch_b = low_back(jnp.dot(activated, weight_down[which], precision=highest))
    return middle + gate_b * branch_b

def reference(hidden_in, segments, timestep, w_qkv, w_out, w_up, w_down, w_mod, b_mod, cotangent):
    weights = tuple((argument.astype(jnp.float32) for argument in (w_qkv, w_out, w_up, w_down, w_mod, b_mod)))
    cosine, sine_table = rotary_tables(SEQ, HEAD_SIZE)
    features_all = time_features(timestep, TDIM)

    def self_pass(params, row_input, features, segment_ids):
        first_out = apply_layer(params, 0, row_input, features, segment_ids, cosine, sine_table)
        return apply_layer(params, 1, low(first_out), features, segment_ids, cosine, sine_table)

    def full_pass(params, probes, row_input, features, segment_ids, prediction):
        out_zero = apply_layer(params, 0, row_input + probes[0], features, segment_ids, cosine, sine_table)
        out_one = apply_layer(params, 1, low(out_zero) + probes[1], features, segment_ids, cosine, sine_table)
        out_two = apply_layer(params, 0, row_input + prediction + probes[2], features, segment_ids, cosine, sine_table)
        out_three = apply_layer(params, 1, low(out_two) + probes[3], features, segment_ids, cosine, sine_table)
        return jnp.stack([out_zero, out_one, out_two, out_three])

    def per_row(running, operands):
        row_input, features, segment_ids, row_cot = operands
        prediction = low(self_pass(weights, row_input, features, segment_ids))
        probes = jnp.zeros((2 * LAYERS, SEQ, D), jnp.float32)
        outputs, pullback = jax.vjp(lambda params, probe_in: full_pass(params, probe_in, row_input, features, segment_ids, prediction), weights, probes)
        weight_grads, probe_grads = pullback(row_cot)
        running = tuple((total_part + grad_part for total_part, grad_part in zip(running, weight_grads)))
        return (running, (outputs.astype(jnp.bfloat16), probe_grads))
    initial = tuple((jnp.zeros_like(argument) for argument in weights))
    totals, (outputs, probe_all) = lax.scan(per_row, initial, (hidden_in.astype(jnp.float32), features_all, segments, jnp.transpose(cotangent.astype(jnp.float32), (1, 0, 2, 3))))
    return (jnp.transpose(outputs, (1, 0, 2, 3)), jnp.transpose(probe_all, (1, 0, 2, 3)), totals[0], totals[1], totals[2], totals[3], totals[4], totals[5])
```

```python
import functools

import jax
import jax.numpy as jnp
import numpy as np
from jax import lax
from jax.experimental import pallas as pl
from jax.experimental.pallas import tpu as pltpu
from jax.sharding import PartitionSpec as P

MESH = pl.DeviceIdType.MESH
BF = jnp.bfloat16
F32 = jnp.float32
highest = lax.Precision.HIGHEST
EPS = 1e-06
D = 768
TOK = 128
SEQ = 1024
ANY = pl.BlockSpec(memory_space=pl.ANY)
VM = pl.BlockSpec(memory_space=pltpu.VMEM)
ROWS = 2304
PACK = (0, 6, 1, 7, 2, 8, 3, 4, 5)
UNPACK = tuple(PACK.index(g) for g in range(9))


def here():
    dp = lax.axis_index("dp")
    t = lax.axis_index("tensor")
    return dp // 2, dp % 2, lax.axis_index("section"), t // 2, t % 2


def dev(x, ylo, z, yhi, c):
    return (2 * x + ylo, z, 2 * yhi + c)


def push(src, dst, send_sem, recv_sem, where):
    return pltpu.make_async_remote_copy(
        src_ref=src,
        dst_ref=dst,
        send_sem=send_sem,
        recv_sem=recv_sem,
        device_id=where,
        device_id_type=MESH,
    )


def greet(devices):
    barrier = pltpu.get_barrier_semaphore()
    for where in devices:
        pl.semaphore_signal(barrier, inc=1, device_id=where, device_id_type=MESH)
    return lambda: pl.semaphore_wait(barrier, len(devices))


def nn(a, b):
    return lax.dot_general(a, b, (((1,), (0,)), ((), ())), preferred_element_type=F32)


def nt(a, b):
    return lax.dot_general(a, b, (((1,), (1,)), ((), ())), preferred_element_type=F32)


def tn(a, b):
    return lax.dot_general(a, b, (((0,), (0,)), ((), ())), preferred_element_type=F32)


def normalize(values):
    centred = values - jnp.mean(values, axis=-1, keepdims=True)
    inverse = lax.rsqrt(jnp.mean(centred * centred, axis=-1, keepdims=True) + EPS)
    return centred * inverse, inverse


def norm_back(gradient, normed, inverse):
    return inverse * (
        gradient
        - jnp.mean(gradient, axis=-1, keepdims=True)
        - normed * jnp.mean(gradient * normed, axis=-1, keepdims=True)
    )


def lanes(shape):
    return lax.broadcasted_iota(jnp.int32, shape, len(shape) - 1)


def swap(x):
    return pltpu.roll(x, 64, 1)


def turn(x, cosine, sine):
    low = (lanes(x.shape) % 64) < 32
    other = jnp.where(low, pltpu.roll(x, 96, 1), pltpu.roll(x, 32, 1))
    return x * cosine + other * sine


def spread(buf, ss, rs, between=None):
    x, ylo, z, yhi, c = here()
    everything = slice(None)

    def at(dims, part, by):
        pos = {"y": ylo, "x": x, "z": z}
        for key, value in by.items():
            pos[key] = value
        return buf.at[tuple(everything if key in dims else pos[key] for key in "yxz") + (part,)]

    def peer(dim, o):
        if dim == "y":
            return dev(x, 1 - ylo, z, yhi, c), 1 - ylo
        if dim == "x":
            return dev((x + o) % 4, ylo, z, yhi, c), (x - o + 4) % 4
        return dev(x, ylo, (z + o) % 4, yhi, c), (z - o + 4) % 4

    orders = ("zyx", "xzy", "yxz")
    for phase in range(3):
        sent, got = [], []
        for part in range(3):
            dim, done = orders[part][phase], orders[part][:phase]
            for o in (1,) if dim == "y" else (2, 1, 3):
                where, origin = peer(dim, o)
                n = (phase * 3 + part) * 3 + o - 1
                cp = push(at(done, part, {}), at(done, part, {}), ss.at[n], rs.at[n], where)
                cp.start()
                sent.append(cp)
                back = at(done, part, {dim: origin})
                got.append((push(back, back, ss.at[n], rs.at[n], where), back))
        if between is not None:
            between(phase, [at(orders[p][:phase], p, {}) for p in range(3)], None)
        for cp, back in got:
            cp.wait_recv()
            if between is not None:
                between(phase, None, back)
        for cp in sent:
            cp.wait_send()


def chips_around():
    x, ylo, z, yhi, c = here()
    found = [dev((x + o) % 4, ylo, z, yhi, c) for o in (1, 2, 3)]
    found += [dev(x, ylo, (z + o) % 4, yhi, c) for o in (1, 2, 3)]
    return found + [dev(x, 1 - ylo, z, yhi, c)]


def prepare_kernel(hid, cot, wloc, x0, cots, w_all, hs, hr, cs, cr, ss, rs, ps, pr, lsem):
    x, ylo, z, yhi, c = here()
    t = 2 * yhi + c
    dp = 2 * x + ylo
    cross = dev(x, 1 - ylo, z, 1 - yhi, c)
    partner = dev(x, ylo, z, yhi, 1 - c)
    group = [(dp, (z + a) % 4, (t + b) % 4) for a in range(4) for b in range(4) if a or b]
    greet(group + [dev((x + o) % 4, ylo, z, yhi, c) for o in (1, 2, 3)] + [dev(x, 1 - ylo, z, yhi, c), cross])()

    own = pltpu.make_async_copy(wloc, w_all.at[t], lsem.at[0])
    own.start()
    first = push(wloc.at[1 - ylo, x, z], w_all.at[t, 1 - ylo, x, z], ps.at[0], pr.at[0], cross)
    first.start()
    side = push(wloc, w_all.at[t], ps.at[1], pr.at[1], partner)
    side.start()

    for b in range(4):
        target = (dp, z, b)
        holder = (t == z) & (t != b)

        @pl.when(holder)
        def _(b=b, target=target):
            push(hid.at[b // 2, b % 2], x0, hs.at[b], hr.at[0], target).start()

        @pl.when((t == z) & (t == b))
        def _(b=b):
            pltpu.make_async_copy(hid.at[b // 2, b % 2], x0, lsem.at[1]).start()

        there = (dp, t, b)
        mine = (t == z) & (t == b)

        @pl.when(jnp.logical_not(mine))
        def _(b=b, there=there):
            push(cot.at[b // 2, b % 2], cots.at[z], cs.at[b], cr.at[z], there).start()

        @pl.when(mine)
        def _(b=b):
            pltpu.make_async_copy(cot.at[b // 2, b % 2], cots.at[z], lsem.at[2]).start()

    other = 2 * (1 - yhi) + c
    buf = w_all.at[other]
    landed = buf.at[ylo, x, z]
    push(landed, landed, ps.at[0], pr.at[0], cross).wait_recv()
    handed = []

    def between(phase, held, back):
        if phase < 2:
            return
        for ref in held if held is not None else [back]:
            n = 2 + len(handed)
            cp = push(ref, ref, ps.at[n], pr.at[n], partner)
            cp.start()
            handed.append(cp)

    spread(buf, ss, rs, between)
    for cp in handed:
        cp.wait_send()
        cp.wait_recv()
    first.wait_send()
    side.wait_send()
    side.wait_recv()
    own.wait()

    for b in range(4):

        @pl.when((t == z) & (t != b))
        def _(b=b):
            push(hid.at[b // 2, b % 2], x0, hs.at[b], hr.at[0], (dp, z, b)).wait_send()

        @pl.when(jnp.logical_not((t == z) & (t == b)))
        def _(b=b):
            push(cot.at[b // 2, b % 2], cots.at[z], cs.at[b], cr.at[z], (dp, t, b)).wait_send()

        mine = (t == z) & (z == b)

        @pl.when(jnp.logical_not(mine))
        def _(b=b):
            push(cots.at[b], cots.at[b], cs.at[b], cr.at[b], partner).wait_recv()

        @pl.when(mine)
        def _(b=b):
            pltpu.make_async_copy(cot.at[b // 2, b % 2], cots.at[z], lsem.at[2]).wait()
            pltpu.make_async_copy(hid.at[b // 2, b % 2], x0, lsem.at[1]).wait()

    @pl.when(t != z)
    def _():
        push(x0, x0, hs.at[0], hr.at[0], partner).wait_recv()


def prepare(hid, cot, wloc):
    dma = pltpu.SemaphoreType.DMA
    return pl.pallas_call(
        prepare_kernel,
        out_shape=(
            jax.ShapeDtypeStruct((TOK, D), BF),
            jax.ShapeDtypeStruct((4, TOK, D), BF),
            jax.ShapeDtypeStruct((4,) + wloc.shape, BF),
        ),
        in_specs=[ANY] * 3,
        out_specs=(ANY,) * 3,
        scratch_shapes=[
            dma((4,)),
            dma((1,)),
            dma((4,)),
            dma((4,)),
            dma((27,)),
            dma((27,)),
            dma((16,)),
            dma((16,)),
            dma((3,)),
        ],
        compiler_params=pltpu.CompilerParams(collective_id=1, has_side_effects=True),
        name="prepare",
    )(hid, cot, wloc)


def fetch(layer, w_all, wq, wo, wu, wd, sem):
    def plan(kind):
        moves = []
        for t in range(4):
            src = w_all.at[t, layer]
            if kind == 0:
                moves.append((src.at[pl.ds(0, 512)], wq.at[pl.ds(512 * t, 512)], 2 * t))
                moves.append((src.at[pl.ds(512, 64)], wq.at[pl.ds(2048 + 64 * t, 64)], 2 * t + 1))
            if kind == 1:
                moves.append((src.at[pl.ds(576, 128)], wo.at[pl.ds(128 * t, 128)], 8 + 2 * t))
                moves.append((src.at[pl.ds(704, 64)], wo.at[pl.ds(512 + 64 * t, 64)], 9 + 2 * t))
            if kind == 2:
                moves.append((src.at[pl.ds(768, 768)], wu.at[t], 16 + t))
            if kind == 3:
                moves.append((src.at[pl.ds(1536, 768)], wd.at[t], 20 + t))
        return [pltpu.make_async_copy(a, b, sem.at[n]) for a, b, n in moves]

    plans = [plan(kind) for kind in range(4)]

    def wait(kind):
        for cp in plans[kind]:
            cp.wait()

    def start(kind):
        for cp in plans[kind]:
            cp.start()

    return start, wait


def weight_scratch():
    return [
        pltpu.VMEM((2304, D), BF),
        pltpu.VMEM((D, D), BF),
        pltpu.VMEM((4, D, D), BF),
        pltpu.VMEM((4, D, D), BF),
        pltpu.SemaphoreType.DMA((24,)),
    ]


def row_group():
    x, ylo, z, yhi, c = here()
    return [(2 * a + b, dev(x, ylo, a, yhi, b)) for a in range(4) for b in range(2)], 2 * z + c


def greet_row():
    x, ylo, z, yhi, c = here()
    me = 2 * z + c
    others = []
    for o in range(1, 8):
        j = (me + o) % 8
        others.append(dev(x, ylo, j // 2, yhi, j % 2))
    return greet(others)


def deal(j, where, me, src, dst, ss, rs):
    @pl.when(me != j)
    def _():
        push(src, dst, ss.at[j], rs.at[me], where).start()

    @pl.when(me == j)
    def _():
        pltpu.make_async_copy(src, dst, ss.at[j]).start()


def dealt(j, where, me, src, dst, ss, rs):
    @pl.when(me != j)
    def _():
        cp = push(src, dst, ss.at[j], rs.at[j], where)
        cp.wait_send()
        cp.wait_recv()

    @pl.when(me == j)
    def _():
        pltpu.make_async_copy(src, dst, ss.at[j]).wait()


def forward_kernel(
    layer, a_ref, b_ref, mod, segc, segr, cosine, sine, w_all,
    y_ref, qkv, lse, att, ba, mid, pre, bb,
    sbuf, obuf, rbuf, wq, wo, wu, wd, wsem, ss, rs, ss2, rs2,
):
    x, ylo, z, yhi, c = here()
    places, me = row_group()
    entered = greet_row()
    start, wait = fetch(layer, w_all, wq, wo, wu, wd, wsem)
    for kind in range(4):
        start(kind)

    v = a_ref[...].astype(F32) + b_ref[...].astype(F32)
    hat, _ = normalize(v)
    normed = (hat * (1.0 + mod[1:2, :]) + mod[0:1, :]).astype(BF)
    cos_here, sin_here = cosine[...], sine[...]
    low = lanes((TOK, 128)) < 64
    wait(0)
    entered()
    last = nt(normed, wq[2048:2304, :])
    for t in range(4):
        got = nt(normed, wq[512 * t : 512 * (t + 1), :])
        q02, k02, v02, qk1 = (got[:, 128 * i : 128 * (i + 1)] for i in range(4))
        v1 = last[:, 128 * (t // 2) : 128 * (t // 2) + 128]
        if t % 2:
            v1 = swap(v1)
        for head, (q, k, w) in enumerate(
            (
                (q02, k02, v02),
                (jnp.where(low, qk1, q02), jnp.where(low, swap(qk1), k02), jnp.where(low, v1, v02)),
            )
        ):
            j = 2 * t + head
            sbuf[j, :, 0:128] = (turn(q, cos_here, sin_here).astype(BF).astype(F32) * 0.125).astype(BF)
            sbuf[j, :, 128:256] = turn(k, cos_here, sin_here).astype(BF)
            sbuf[j, :, 256:384] = w.astype(BF)
            deal(j, places[j][1], me, sbuf.at[j], qkv.at[me], ss, rs)
    for j, where in places:
        dealt(j, where, me, sbuf.at[j], qkv.at[j], ss, rs)

    keys = qkv[:, :, 128:256].reshape(SEQ, 128)
    values = qkv[:, :, 256:384].reshape(SEQ, 128)
    seg_keys = segr[...]

    def softmax(q, seg_q):
        scores = jnp.where(seg_q == seg_keys, nt(q, keys), -1e30)
        largest = jnp.max(scores, axis=-1, keepdims=True)
        raised = jnp.exp(scores - largest)
        total = jnp.sum(raised, axis=-1, keepdims=True)
        mixed = nn(raised.astype(BF), values) * (1.0 / total)
        return mixed, largest + jnp.log(total)

    def flat(column):
        wide = jnp.broadcast_to(column, (column.shape[0], 128))
        return jnp.transpose(wide)[0:8, :]

    for a in range(4):
        q = qkv[2 * a : 2 * a + 2, :, 0:128].reshape(256, 128)
        q = jnp.where(lanes((256, 128)) < 64, q, 0).astype(BF)
        mixed, total = softmax(q, segc[256 * a : 256 * (a + 1), :])
        q2 = jnp.where(low, 0, qkv[2 * a + c, :, 0:128]).astype(BF)
        mixed2, total2 = softmax(q2, segc[pl.ds(256 * a + TOK * c, TOK), :])
        lse[a, :, 0:256] = flat(total)
        lse[a, :, 256:384] = flat(total2)
        for b in range(2):
            j = 2 * a + b
            part = mixed[TOK * b : TOK * (b + 1)]
            obuf[j] = jnp.where(low | (c != b), part, mixed2).astype(BF)
            deal(j, places[j][1], me, obuf.at[j], rbuf.at[me], ss2, rs2)
    for j, where in places:
        dealt(j, where, me, obuf.at[j], rbuf.at[j], ss2, rs2)

    shared = []
    for t in range(4):
        first, second = rbuf[2 * t].astype(F32), rbuf[2 * t + 1].astype(F32)
        att[:, 128 * t : 128 * (t + 1)] = jnp.where(low, first, swap(second)).astype(BF)
        shared.append(rbuf[2 * t + c].astype(F32))
    att[:, 512:640] = jnp.where(low, swap(shared[0]), shared[1]).astype(BF)
    att[:, 640:768] = jnp.where(low, swap(shared[2]), shared[3]).astype(BF)
    wait(1)
    branch_a = nn(att[...], wo[...])
    ba[...] = branch_a
    middle = v + mod[2:3, :] * branch_a
    mid[...] = middle
    hat_b, _ = normalize(middle)
    normed_b = (hat_b * (1.0 + mod[4:5, :]) + mod[3:4, :]).astype(BF)
    wait(2)
    wait(3)
    total_b = jnp.zeros((TOK, D), F32)
    for t in range(4):
        before = nn(normed_b, wu[t])
        pre[:, D * t : D * (t + 1)] = before
        total_b = total_b + nn(jax.nn.gelu(before, approximate=True).astype(BF), wd[t])
    bb[...] = total_b
    y_ref[...] = (middle + mod[5:6, :] * total_b).astype(BF)


def forward(layer, a, b, mod, segc, segr, cosine, sine, w_all):
    dma = pltpu.SemaphoreType.DMA
    return pl.pallas_call(
        functools.partial(forward_kernel, layer),
        out_shape=(
            jax.ShapeDtypeStruct((TOK, D), BF),
            jax.ShapeDtypeStruct((8, TOK, 384), BF),
            jax.ShapeDtypeStruct((4, 8, 384), F32),
            jax.ShapeDtypeStruct((TOK, D), BF),
            jax.ShapeDtypeStruct((TOK, D), F32),
            jax.ShapeDtypeStruct((TOK, D), F32),
            jax.ShapeDtypeStruct((TOK, 4 * D), F32),
            jax.ShapeDtypeStruct((TOK, D), F32),
        ),
        in_specs=[VM] * 7 + [ANY],
        out_specs=(VM,) * 8,
        scratch_shapes=[
            pltpu.VMEM((8, TOK, 384), BF),
            pltpu.VMEM((8, TOK, 128), BF),
            pltpu.VMEM((8, TOK, 128), BF),
        ]
        + weight_scratch()
        + [dma((8,)), dma((8,)), dma((8,)), dma((8,))],
        compiler_params=pltpu.CompilerParams(
            collective_id=2 + layer, has_side_effects=True, vmem_limit_bytes=56 * 2**20
        ),
        name="forward",
    )(a, b, mod, segc, segr, cosine, sine, w_all)


def gelu_parts(u):
    k = 0.7978845608028654
    square = u * u
    th = jnp.tanh(k * u * (1.0 + 0.044715 * square))
    half = 0.5 * (1.0 + th)
    slope = half + 0.5 * u * (1.0 - th * th) * (k * (1.0 + 0.134145 * square))
    return u * half, slope


def backward_kernel(
    layer, a0, b0, a1, b1, dy0, dy1, mod, segc, segr, cosine, sine,
    qkv0, qkv1, lse0, lse1, att0, att1, ba0, ba1, mid0, mid1, pre0, pre1, bb0, bb1, w_all,
    din, dmod, na_o, at_o, nb_o, dba_o, dbb_o, act_o, dpre_o, dpj_o, dv1_o,
    na_p, at_p, nb_p, dba_p, dbb_p, act_p, dpre_p, dpj_p, dv1_p,
    sbuf, rbuf, sbig, rbig, dmid, dnb, k_own, k_sh, v_own, v_sh,
    wq, wo, wu, wd, wsem, ss, rs, ss2, rs2, xs, xr,
):
    x, ylo, z, yhi, c = here()
    places, me = row_group()
    partner = dev(x, ylo, z, yhi, 1 - c)
    entered = greet_row()
    start, wait = fetch(layer, w_all, wq, wo, wu, wd, wsem)
    for kind in (3, 2, 1, 0):
        start(kind)
    scale_a, gate_a = mod[1:2, :], mod[2:3, :]
    scale_b, gate_b = mod[4:5, :], mod[5:6, :]
    a_refs, b_refs, dys = (a0, a1), (b0, b1), (dy0, dy1)
    qkvs, lses, bas, mids, pres, bbs = (qkv0, qkv1), (lse0, lse1), (ba0, ba1), (mid0, mid1), (pre0, pre1), (bb0, bb1)
    low = lanes((TOK, 128)) < 64
    exchanged = []

    def hand(src, dst):
        n = len(exchanged)
        cp = push(src, dst, xs.at[n], xr.at[n], partner)
        cp.start()
        exchanged.append(cp)

    dgate_b = jnp.zeros((1, D), F32)
    for e in range(2):
        rows = slice(TOK * e, TOK * (e + 1))
        dy = dys[e][...]
        dgate_b = dgate_b + jnp.sum(dy * bbs[e][...], axis=0, keepdims=True)
        dbb_o[rows, :] = (gate_b * dy).astype(BF)
        hat_b, _ = normalize(mids[e][...])
        nb_o[rows, :] = (hat_b * (1.0 + scale_b) + mod[3:4, :]).astype(BF)
        hat_a, _ = normalize(a_refs[e][...].astype(F32) + b_refs[e][...].astype(F32))
        na_o[rows, :] = (hat_a * (1.0 + scale_a) + mod[0:1, :]).astype(BF)
        at_o[rows, :] = (att0, att1)[e][...]
    entered()
    hand(dbb_o, dbb_p)
    hand(nb_o, nb_p)
    hand(na_o, na_p)
    hand(at_o, at_p)

    wait(3)
    wait(2)
    for t in range(4):
        d_act = nt(dbb_o[...], wd[t])
        for e in range(2):
            rows = slice(TOK * e, TOK * (e + 1))
            act, slope = gelu_parts(pres[e][:, D * t : D * (t + 1)])
            act_o[t, rows, :] = act.astype(BF)
            dpre_o[t, rows, :] = (d_act[rows] * slope).astype(BF)
        more = nt(dpre_o[t], wu[t])
        dnb[...] = more if t == 0 else dnb[...] + more
    for h in range(2):
        hand(act_o.at[2 * h + 1 - c], act_p.at[h])
        hand(dpre_o.at[2 * h + 1 - c], dpre_p.at[h])

    dgate_a = jnp.zeros((1, D), F32)
    dscale_b = jnp.zeros((1, D), F32)
    dshift_b = jnp.zeros((1, D), F32)
    for e in range(2):
        rows = slice(TOK * e, TOK * (e + 1))
        hat_b, inv_b = normalize(mids[e][...])
        g = dnb[rows, :]
        dscale_b = dscale_b + jnp.sum(g * hat_b, axis=0, keepdims=True)
        dshift_b = dshift_b + jnp.sum(g, axis=0, keepdims=True)
        d_middle = dys[e][...] + norm_back(g * (1.0 + scale_b), hat_b, inv_b)
        dmid[rows, :] = d_middle
        dgate_a = dgate_a + jnp.sum(d_middle * bas[e][...], axis=0, keepdims=True)
        dba_o[rows, :] = (gate_a * d_middle).astype(BF)
    hand(dba_o, dba_p)
    wait(1)
    d_att = nt(dba_o[...], wo[...])
    for t in range(4):
        for e in range(2):
            rows = slice(TOK * e, TOK * (e + 1))
            own = d_att[rows, 128 * t : 128 * (t + 1)]
            extra = d_att[rows, 512 + 128 * (t // 2) : 640 + 128 * (t // 2)]
            if t % 2 == 0:
                extra = swap(extra)
            sbuf[2 * t, e] = jnp.where(low, own, extra).astype(BF)
            sbuf[2 * t + 1, e] = jnp.where(low, swap(own), extra).astype(BF)
        for b in range(2):
            j = 2 * t + b
            deal(j, places[j][1], me, sbuf.at[j], rbuf.at[me], ss, rs)
    for j, where in places:
        dealt(j, where, me, sbuf.at[j], rbuf.at[j], ss, rs)

    seg_keys = segc[...]
    wide = lanes((256, 128)) < 64
    for e in range(2):
        qkv, lse = qkvs[e], lses[e]
        for ref in (k_own, k_sh, v_own, v_sh):
            ref[...] = jnp.zeros_like(ref)

        def one(q, go, seg_q, total, k_sum, v_sum, qkv=qkv):
            keys = qkv[:, :, 128:256].reshape(SEQ, 128)
            values = qkv[:, :, 256:384].reshape(SEQ, 128)
            scores = jnp.where(seg_keys == seg_q, nt(keys, q), -1e30)
            p = jnp.exp(scores - total)
            d_p = nt(values, go)
            centre = jnp.sum(d_p * p, axis=0, keepdims=True)
            d_s = (p * (d_p - centre)).astype(BF)
            v_sum[...] += nn(p.astype(BF), go)
            k_sum[...] += nn(d_s, q)
            return tn(d_s, keys) * 0.125

        for a in range(4):
            q = qkv[2 * a : 2 * a + 2, :, 0:128].reshape(256, 128)
            go = rbuf[2 * a : 2 * a + 2, e].reshape(256, 128)
            dq = one(
                jnp.where(wide, q, 0).astype(BF),
                jnp.where(wide, go, 0).astype(BF),
                segr[0:1, 256 * a : 256 * (a + 1)],
                lse[a, 0:1, 0:256],
                k_own,
                v_own,
            )
            q2 = jnp.where(low, 0, qkv[2 * a + c, :, 0:128]).astype(BF)
            go2 = jnp.where(low, 0, rbuf[2 * a + c, e]).astype(BF)
            seg2 = jnp.where(
                c == 0,
                segr[0:1, 256 * a : 256 * a + 128],
                segr[0:1, 256 * a + 128 : 256 * a + 256],
            )
            dq2 = one(q2, go2, seg2, lse[a, 0:1, 256:384], k_sh, v_sh)
            for b in range(2):
                rows = slice(256 * a + TOK * b, 256 * a + TOK * (b + 1))
                whole = jnp.where(low, dq[TOK * b : TOK * (b + 1)], jnp.where(c == b, dq2, 0.0))
                sbig[2 * a + b, e, :, 0:128] = turn(whole, cosine[rows, :], -sine[rows, :]).astype(BF)
        for j in range(8):
            rows = slice(TOK * j, TOK * (j + 1))
            whole = jnp.where(low, k_own[rows, :], k_sh[rows, :])
            sbig[j, e, :, 128:256] = turn(whole, cosine[rows, :], -sine[rows, :]).astype(BF)
            sbig[j, e, :, 256:384] = jnp.where(low, v_own[rows, :], v_sh[rows, :]).astype(BF)
    for j, where in places:
        deal(j, where, me, sbig.at[j], rbig.at[me], ss2, rs2)
    for j, where in places:
        dealt(j, where, me, sbig.at[j], rbig.at[j], ss2, rs2)

    for e in range(2):
        rows = slice(TOK * e, TOK * (e + 1))
        ones = []
        for t in range(4):
            q0, k0, v0 = (rbig[2 * t, e, :, 128 * i : 128 * (i + 1)].astype(F32) for i in range(3))
            q1, k1, v1 = (rbig[2 * t + 1, e, :, 128 * i : 128 * (i + 1)].astype(F32) for i in range(3))
            dpj_o[t, rows, 0:128] = jnp.where(low, q0, q0 + q1).astype(BF)
            dpj_o[t, rows, 128:256] = jnp.where(low, k0, k0 + k1).astype(BF)
            dpj_o[t, rows, 256:384] = jnp.where(low, v0, v0 + v1).astype(BF)
            dpj_o[t, rows, 384:512] = jnp.where(low, q1, swap(k1)).astype(BF)
            ones.append(v1)
        dv1_o[rows, 0:128] = jnp.where(low, ones[0], swap(ones[1])).astype(BF)
        dv1_o[rows, 128:256] = jnp.where(low, ones[2], swap(ones[3])).astype(BF)
    for h in range(2):
        hand(dpj_o.at[2 * h + 1 - c], dpj_p.at[h])
    hand(dv1_o, dv1_p)
    wait(0)
    dna = nn(dv1_o[...], wq[2048:2304, :])
    for t in range(4):
        dna = dna + nn(dpj_o[t], wq[512 * t : 512 * (t + 1), :])
    dscale_a = jnp.zeros((1, D), F32)
    dshift_a = jnp.zeros((1, D), F32)
    for e in range(2):
        rows = slice(TOK * e, TOK * (e + 1))
        hat_a, inv_a = normalize(a_refs[e][...].astype(F32) + b_refs[e][...].astype(F32))
        g = dna[rows]
        dscale_a = dscale_a + jnp.sum(g * hat_a, axis=0, keepdims=True)
        dshift_a = dshift_a + jnp.sum(g, axis=0, keepdims=True)
        din[e] = dmid[rows, :] + norm_back(g * (1.0 + scale_a), hat_a, inv_a)
    for i, part in enumerate((dshift_a, dscale_a, dgate_a, dshift_b, dscale_b, dgate_b)):
        dmod[i : i + 1, :] = part
    dmod[6:8, :] = jnp.zeros((2, D), F32)
    for cp in exchanged:
        cp.wait_send()
        cp.wait_recv()


def backward(layer, *operands):
    dma = pltpu.SemaphoreType.DMA
    both = 2 * TOK

    def shape(*dims):
        return jax.ShapeDtypeStruct(dims, BF)

    own = [shape(both, D)] * 5 + [shape(4, both, D)] * 2 + [shape(4, both, 512), shape(both, 256)]
    got = [shape(both, D)] * 5 + [shape(2, both, D)] * 2 + [shape(2, both, 512), shape(both, 256)]
    outs = [
        jax.ShapeDtypeStruct((2, TOK, D), F32),
        jax.ShapeDtypeStruct((8, D), F32),
    ] + own + got
    return pl.pallas_call(
        functools.partial(backward_kernel, layer),
        out_shape=tuple(outs),
        in_specs=[VM] * 25 + [ANY],
        out_specs=(VM,) * len(outs),
        scratch_shapes=[
            pltpu.VMEM((8, 2, TOK, 128), BF),
            pltpu.VMEM((8, 2, TOK, 128), BF),
            pltpu.VMEM((8, 2, TOK, 384), BF),
            pltpu.VMEM((8, 2, TOK, 384), BF),
            pltpu.VMEM((both, D), F32),
            pltpu.VMEM((both, D), F32),
        ]
        + [pltpu.VMEM((SEQ, 128), F32)] * 4
        + weight_scratch()
        + [dma((8,)), dma((8,)), dma((8,)), dma((8,)), dma((12,)), dma((12,))],
        compiler_params=pltpu.CompilerParams(
            collective_id=4 + layer, has_side_effects=True, vmem_limit_bytes=60 * 2**20
        ),
        name="backward",
    )(*operands)


def weights_kernel(
    na_o, at_o, nb_o, dba_o, dbb_o, act_o, dpre_o, dpj_o, dv1_o,
    na_p, at_p, nb_p, dba_p, dbb_p, act_p, dpre_p, dpj_p, dv1_p,
    grads, tall,
):
    c = lax.axis_index("tensor") % 2
    tall[...] = (tn(dv1_o[...], na_o[...]) + tn(dv1_p[...], na_p[...])).astype(BF)
    for h in range(2):
        t = 2 * h + c
        grads[h, 0:512, :] = (tn(dpj_o[t], na_o[...]) + tn(dpj_p[h], na_p[...])).astype(BF)
        grads[h, 512:576, :] = tall[pl.ds(pl.multiple_of(64 * t, 64), 64), :]
    tall[...] = (tn(at_o[:, 512:768], dba_o[...]) + tn(at_p[:, 512:768], dba_p[...])).astype(BF)
    for h in range(2):
        t = 2 * h + c
        cols = pl.ds(pl.multiple_of(128 * t, 128), 128)
        grads[h, 576:704, :] = (tn(at_o[:, cols], dba_o[...]) + tn(at_p[:, cols], dba_p[...])).astype(BF)
        grads[h, 704:768, :] = tall[pl.ds(pl.multiple_of(64 * t, 64), 64), :]
        grads[h, 768:1536, :] = (tn(nb_o[...], dpre_o[t]) + tn(nb_p[...], dpre_p[h])).astype(BF)
        grads[h, 1536:2304, :] = (tn(act_o[t], dbb_o[...]) + tn(act_p[h], dbb_p[...])).astype(BF)


def weight_grads(*operands):
    return pl.pallas_call(
        weights_kernel,
        out_shape=jax.ShapeDtypeStruct((2, ROWS, D), BF),
        in_specs=[VM] * 18,
        out_specs=VM,
        scratch_shapes=[pltpu.VMEM((256, D), BF)],
        compiler_params=pltpu.CompilerParams(vmem_limit_bytes=56 * 2**20),
        name="weight_grads",
    )(*operands)


def reduce_kernel(
    g0, g1, ys, gs, out, y_out, g_out,
    own0, own1, own2, in0, in1, in2, sum0, sum1, sum2,
    mid0, mid1, mid2, tot0, tot1, tot2, end0, end1, end2, fin,
    osem, ss, rs, ss2, rs2, ss3, rs3, gss, grs, ys_s, ys_r, gs_s, gs_r, fsem,
):
    x, ylo, z, yhi, c = here()
    t = 2 * yhi + c
    dp = 2 * x + ylo
    y = 2 * yhi + ylo
    gl = (g0, g1)
    group = [(dp, (z + a) % 4, (t + b) % 4) for a in range(4) for b in range(4) if a or b]
    ymates = [dev(x, 1 - ylo, z, yhi, c), dev(x, 1 - ylo, z, 1 - yhi, c)]
    greet(group + [dev((x + o) % 4, ylo, z, yhi, c) for o in (1, 2, 3)] + ymates)()

    def xpeer(o):
        return dev((x + o) % 4, ylo, z, yhi, c), (x + o) % 4

    def zpeer(o):
        return dev(x, ylo, (z + o) % 4, yhi, c), (z + o) % 4

    def ypeer(o):
        to = (y + o) % 4
        return dev(x, to % 2, z, to // 2, c), to

    copies = []
    for l in range(2):
        copies.append(pltpu.make_async_copy(gl[l].at[:, x, :, 0], own0.at[l], osem.at[l]))
        copies.append(pltpu.make_async_copy(gl[l].at[:, :, z, 2], own2.at[l], osem.at[2 + l]))
        copies[-1].start()
        copies[-2].start()

        @pl.when(ylo == l)
        def _(l=l):
            pltpu.make_async_copy(gl[l].at[yhi, :, :, 1], own1, osem.at[4]).start()

    def first(o, begin):
        for l in range(2):
            where, to = xpeer(o)
            a = push(gl[l].at[:, to, :, 0], in0.at[o - 1, l], ss.at[0, o - 1, l], rs.at[0, o - 1, l], where)
            where, to = zpeer(o)
            b = push(gl[l].at[:, :, to, 2], in2.at[o - 1, l], ss.at[2, o - 1, l], rs.at[2, o - 1, l], where)
            where, to = ypeer(o)
            d = push(gl[l].at[to // 2, :, :, 1], in1.at[o - 1], ss.at[1, o - 1, 0], rs.at[1, o - 1, 0], where)
            if begin:
                a.start()
                b.start()

                @pl.when(to % 2 == l)
                def _():
                    d.start()
            else:
                a.wait()
                b.wait()
                if l == 0:
                    d.wait()

    for o in (2, 1, 3):
        first(o, True)

    def scatter(src, dst, s_sem, r_sem, begin):
        for s in range(4):
            mine = (z == s) & (t == z)

            @pl.when(jnp.logical_not(mine))
            def _(s=s):
                cp = push(src.at[s], dst.at[yhi, c], s_sem.at[s], r_sem.at[t], (dp, s, z))
                if begin:
                    cp.start()
                else:
                    cp.wait_send()

            @pl.when(mine)
            def _(s=s):
                cp = pltpu.make_async_copy(src.at[s], dst.at[yhi, c], s_sem.at[s])
                if begin:
                    cp.start()
                else:
                    cp.wait()

        if not begin:
            for b in range(4):

                @pl.when(jnp.logical_not((t == z) & (t == b)))
                def _(b=b):
                    spot = dst.at[b // 2, b % 2]
                    push(spot, spot, s_sem.at[b], r_sem.at[b], (dp, z, (t + 1) % 4)).wait_recv()

    scatter(ys, y_out, ys_s, ys_r, True)
    scatter(gs, g_out, gs_s, gs_r, True)

    for cp in copies:
        cp.wait()
    pltpu.make_async_copy(g0.at[yhi, :, :, 1], own1, osem.at[4]).wait()
    for o in (2, 1, 3):
        first(o, False)

    def add(dst, refs, count):
        def body(i, carry):
            total = refs[0](i).astype(F32)
            for ref in refs[1:]:
                total = total + ref(i).astype(F32)
            dst(i, total)
            return carry

        lax.fori_loop(0, count, body, 0)

    def at0(ref):
        return lambda i: ref[i // 8, (i // 4) % 2, i % 4]

    def put(ref, split):
        def store(i, total):
            ref[split(i)] = total.astype(BF)

        return store

    add(
        put(sum0, lambda i: (i // 8, (i // 4) % 2, i % 4)),
        [at0(own0), at0(in0.at[0]), at0(in0.at[1]), at0(in0.at[2])],
        16,
    )
    add(
        put(sum1, lambda i: (i // 4, i % 4)),
        [(lambda i, r=r: r[i // 4, i % 4]) for r in (own1, in1.at[0], in1.at[1], in1.at[2])],
        16,
    )
    add(
        put(sum2, lambda i: (i // 8, (i // 4) % 2, i % 4)),
        [at0(own2), at0(in2.at[0]), at0(in2.at[1]), at0(in2.at[2])],
        16,
    )

    def second(o):
        where, to = ypeer(o)
        a = push(sum0.at[to % 2, to // 2], mid0.at[o - 1], ss2.at[0, o - 1], rs2.at[0, o - 1], where)
        where, to = zpeer(o)
        b = push(sum1.at[:, to], mid1.at[o - 1], ss2.at[1, o - 1], rs2.at[1, o - 1], where)
        where, to = xpeer(o)
        d = push(sum2.at[:, :, to], mid2.at[o - 1], ss2.at[2, o - 1], rs2.at[2, o - 1], where)
        return a, b, d

    moved = [cp for o in (2, 1, 3) for cp in second(o)]
    for cp in moved:
        cp.start()
    for cp in moved:
        cp.wait()
    add(
        put(tot0, lambda i: i),
        [lambda i: sum0[ylo, yhi, i]] + [(lambda i, r=mid0.at[n]: r[i]) for n in range(3)],
        4,
    )
    add(
        put(tot1, lambda i: i),
        [lambda i: sum1[i, z]] + [(lambda i, r=mid1.at[n]: r[i]) for n in range(3)],
        4,
    )
    add(
        put(tot2, lambda i: (i // 2, i % 2)),
        [lambda i: sum2[i // 2, i % 2, x]] + [(lambda i, r=mid2.at[n]: r[i // 2, i % 2]) for n in range(3)],
        4,
    )

    def third(o):
        where, to = zpeer(o)
        a = push(tot0.at[to], end0.at[o - 1], ss3.at[0, o - 1], rs3.at[0, o - 1], where)
        where, to = xpeer(o)
        b = push(tot1.at[to], end1.at[o - 1], ss3.at[1, o - 1], rs3.at[1, o - 1], where)
        where, to = ypeer(o)
        d = push(tot2.at[to % 2, to // 2], end2.at[o - 1], ss3.at[2, o - 1], rs3.at[2, o - 1], where)
        return a, b, d

    moved = [cp for o in (2, 1, 3) for cp in third(o)]
    for cp in moved:
        cp.start()
    for cp in moved:
        cp.wait()
    for p, (last, ends) in enumerate(((tot0[z], end0), (tot1[x], end1), (tot2[ylo, yhi], end2))):
        total = last.astype(F32)
        for n in range(3):
            total = total + ends[n].astype(F32)
        fin[p] = total.astype(BF)
    cp = pltpu.make_async_copy(fin, out.at[ylo, x, z], fsem.at[0])
    cp.start()
    cp.wait()
    spread(out, gss, grs)
    scatter(ys, y_out, ys_s, ys_r, False)
    scatter(gs, g_out, gs_s, gs_r, False)


def reduce_all(g0, g1, ys, gs):
    dma = pltpu.SemaphoreType.DMA

    def buf(*dims):
        return pltpu.VMEM(dims + (48, D), BF)

    return pl.pallas_call(
        reduce_kernel,
        out_shape=(
            jax.ShapeDtypeStruct((2, 4, 4, 3, 48, D), BF),
            jax.ShapeDtypeStruct((2, 2, TOK, D), BF),
            jax.ShapeDtypeStruct((2, 2, TOK, D), BF),
        ),
        in_specs=[ANY] * 4,
        out_specs=(ANY,) * 3,
        scratch_shapes=[
            buf(2, 2, 4),
            buf(4, 4),
            buf(2, 2, 4),
            buf(3, 2, 2, 4),
            buf(3, 4, 4),
            buf(3, 2, 2, 4),
            buf(2, 2, 4),
            buf(4, 4),
            buf(2, 2, 4),
            buf(3, 4),
            buf(3, 4),
            buf(3, 2, 2),
            buf(4),
            buf(4),
            buf(2, 2),
            buf(3),
            buf(3),
            buf(3),
            buf(3),
            dma((5,)),
            dma((3, 3, 2)),
            dma((3, 3, 2)),
            dma((3, 3)),
            dma((3, 3)),
            dma((3, 3)),
            dma((3, 3)),
            dma((27,)),
            dma((27,)),
            dma((4,)),
            dma((4,)),
            dma((4,)),
            dma((4,)),
            dma((1,)),
        ],
        compiler_params=pltpu.CompilerParams(
            collective_id=6, has_side_effects=True, vmem_limit_bytes=50 * 2**20
        ),
        name="reduce_all",
    )(g0, g1, ys, gs)


def rotary(count):
    frequency = np.exp(-np.log(10000.0) * np.arange(32) / 32)
    angles = np.arange(count)[:, None] * frequency[None, :]
    cos, sin = np.cos(angles), np.sin(angles)
    return (
        np.concatenate([cos] * 4, axis=1).astype(np.float32),
        np.concatenate([-sin, sin, -sin, sin], axis=1).astype(np.float32),
    )


def time_features(step_values, feature_count):
    half_count = feature_count // 2
    frequency = jnp.exp(-np.log(10000.0) * jnp.arange(half_count, dtype=F32) / half_count)
    angles = step_values.astype(F32)[:, None] * frequency[None, :]
    return jnp.concatenate([jnp.cos(angles), jnp.sin(angles)], axis=1)


def on_device(hidden_in, segments, timestep, w_qkv, w_out, w_up, w_down, w_mod, b_mod, cotangent):
    x, ylo, z, yhi, c = here()
    tall = jnp.swapaxes(w_qkv, 1, 2).reshape(2, 9, 64, D)
    tall = jnp.concatenate([tall[:, g] for g in PACK], axis=1)
    wloc = jnp.concatenate([tall, w_out, w_up, w_down], axis=1).reshape(2, 4, 4, 3, 48, D)
    x0, cots, w_all = prepare(
        hidden_in.reshape(2, 2, TOK, D), cotangent.reshape(2, 2, TOK, D), wloc
    )
    w_all = w_all.reshape(4, 2, ROWS, D)

    features = time_features(timestep, w_mod.shape[1])
    mine = lax.dynamic_slice_in_dim(features, yhi, 1, 0)
    modulation = jnp.einsum(
        "rf,lfm->lrm", mine, w_mod.astype(F32), precision=highest
    ) + b_mod.astype(F32)[:, None, :]
    modulation = modulation.reshape(2, 6, D)
    mods = (modulation[0], modulation[1])
    seg = lax.dynamic_slice_in_dim(segments, yhi, 1, 0)
    segc, segr = seg.reshape(SEQ, 1), seg
    cosine, sine = (jnp.asarray(v) for v in rotary(SEQ))
    place = (2 * z + c) * TOK
    cos_here = lax.dynamic_slice_in_dim(cosine, place, TOK, 0)
    sin_here = lax.dynamic_slice_in_dim(sine, place, TOK, 0)

    none = jnp.zeros_like(x0)
    ins, kept, ys = [], [], []
    for s in range(4):
        a = x0 if s == 0 else ys[-1]
        b = x0 if s == 2 else none
        y, *saved = forward(s % 2, a, b, mods[s % 2], segc, segr, cos_here, sin_here, w_all)
        ins.append((a, b))
        kept.append(saved)
        ys.append(y)

    def stage(layer, dy0, dy1):
        e0, e1 = layer, layer + 2
        pairs = [item for pair in zip(kept[e0], kept[e1]) for item in pair]
        return backward(
            layer, *ins[e0], *ins[e1], dy0, dy1, mods[layer], segc, segr, cosine, sine, *pairs, w_all
        )

    din1, dmod1, *parts1 = stage(1, cots[1].astype(F32), cots[3].astype(F32))
    din0, dmod0, *parts0 = stage(
        0, cots[0].astype(F32) + din1[0], cots[2].astype(F32) + din1[1]
    )
    units = (2, 4, 4, 3, 48, D)
    g1 = weight_grads(*parts1).reshape(units)
    g0 = weight_grads(*parts0).reshape(units)

    d_mod = jnp.stack([dmod0[:6].reshape(-1), dmod1[:6].reshape(-1)])
    d_rows = jnp.where((jnp.arange(2) == yhi)[:, None, None], d_mod[None], 0.0)
    d_rows = lax.psum(d_rows, ("section", "tensor"))
    sent = jnp.concatenate([d_rows.reshape(2, -1), features], axis=1)
    sent = lax.all_gather(sent, "dp", axis=0, tiled=True)
    d_all, features_all = sent[:, : 2 * 6 * D].reshape(-1, 2, 6 * D), sent[:, 2 * 6 * D :]
    grad_mod = jnp.einsum("rf,rlm->lfm", features_all, d_all, precision=highest)
    grad_bias = jnp.sum(d_all, axis=0)

    y_all = jnp.stack(ys)
    d_ins = jnp.stack([din0[0], din1[0], din0[1], din1[1]]).astype(BF)
    out, y_out, g_out = reduce_all(g0, g1, y_all, d_ins)
    out = out.reshape(2, ROWS, D)
    groups = out[:, :576].reshape(2, 9, 64, D)
    grad_qkv = jnp.concatenate([groups[:, g] for g in UNPACK], axis=1).swapaxes(1, 2)
    return (
        y_out.reshape(1, 2, 2 * TOK, D),
        g_out.reshape(1, 2, 2 * TOK, D).astype(F32),
        grad_qkv.astype(F32),
        out[:, 576:768].astype(F32),
        out[:, 768:1536].astype(F32),
        out[:, 1536:2304].astype(F32),
        grad_mod,
        grad_bias,
    )


def solution(mesh):
    placed = (
        P("dp", "tensor", None),
        P("dp", None),
        P("dp"),
        P(None, None, "tensor"),
        P(None, "tensor", None),
        P(None, None, "tensor"),
        P(None, "tensor", None),
        P(),
        P(),
        P("section", "dp", "tensor", None),
    )
    return jax.shard_map(
        on_device,
        mesh=mesh,
        in_specs=placed,
        out_specs=(
            P("section", "dp", "tensor", None),
            P("section", "dp", "tensor", None),
            P(None, None, "tensor"),
            P(None, "tensor", None),
            P(None, None, "tensor"),
            P(None, "tensor", None),
            P(),
            P(),
        ),
        check_vma=False,
    )
```

```python
import functools

import jax
import jax.numpy as jnp
import numpy as np
from jax import lax
from jax.experimental import pallas as pl
from jax.experimental.pallas import tpu as pltpu
from jax.sharding import PartitionSpec as P

MESH = pl.DeviceIdType.MESH
BF = jnp.bfloat16
F32 = jnp.float32
highest = lax.Precision.HIGHEST
EPS = 1e-06
D = 768
TOK = 128
SEQ = 1024
ANY = pl.BlockSpec(memory_space=pl.ANY)
VM = pl.BlockSpec(memory_space=pltpu.VMEM)
HALF = 384
ATTN = (4, 4, 3, 16, D)
MLP = (4, 4, 3, 32, D)
UNIT = (4, 4, 3, 48, D)


def here():
    dp = lax.axis_index("dp")
    t = lax.axis_index("tensor")
    return dp // 2, dp % 2, lax.axis_index("section"), t // 2, t % 2


def dev(x, ylo, z, yhi, c):
    return (2 * x + ylo, z, 2 * yhi + c)


def push(src, dst, send_sem, recv_sem, where):
    return pltpu.make_async_remote_copy(
        src_ref=src,
        dst_ref=dst,
        send_sem=send_sem,
        recv_sem=recv_sem,
        device_id=where,
        device_id_type=MESH,
    )


def greet(devices):
    barrier = pltpu.get_barrier_semaphore()
    for where in devices:
        pl.semaphore_signal(barrier, inc=1, device_id=where, device_id_type=MESH)
    return lambda: pl.semaphore_wait(barrier, len(devices))


def nn(a, b):
    return lax.dot_general(a, b, (((1,), (0,)), ((), ())), preferred_element_type=F32)


def nt(a, b):
    return lax.dot_general(a, b, (((1,), (1,)), ((), ())), preferred_element_type=F32)


def tn(a, b):
    return lax.dot_general(a, b, (((0,), (0,)), ((), ())), preferred_element_type=F32)


def normalize(values):
    centred = values - jnp.mean(values, axis=-1, keepdims=True)
    inverse = lax.rsqrt(jnp.mean(centred * centred, axis=-1, keepdims=True) + EPS)
    return centred * inverse, inverse


def norm_back(gradient, normed, inverse):
    return inverse * (
        gradient
        - jnp.mean(gradient, axis=-1, keepdims=True)
        - normed * jnp.mean(gradient * normed, axis=-1, keepdims=True)
    )


def lanes(shape):
    return lax.broadcasted_iota(jnp.int32, shape, len(shape) - 1)


def swap(x):
    return pltpu.roll(x, 64, 1)


def turn(x, cosine, sine):
    low = (lanes(x.shape) % 64) < 32
    other = jnp.where(low, pltpu.roll(x, 96, 1), pltpu.roll(x, 32, 1))
    return x * cosine + other * sine


def half(ylo):
    return pl.ds(pl.multiple_of(HALF * ylo, 128), HALF)


class Spread:
    orders = ("zyx", "xzy", "yxz")

    def __init__(self, buf, ss, rs):
        self.buf, self.ss, self.rs = buf, ss, rs
        self.running = None

    def at(self, dims, part, by):
        x, ylo, z, yhi, c = here()
        everything = slice(None)
        i = everything if "x" in dims else by.get("x", x)
        j = everything if "z" in dims else by.get("z", z)
        k = everything if "y" in dims else half(by.get("y", ylo))
        return self.buf.at[i, j, part, :, k]

    def peer(self, dim, o):
        x, ylo, z, yhi, c = here()
        if dim == "y":
            return dev(x, 1 - ylo, z, yhi, c), 1 - ylo
        if dim == "x":
            return dev((x + o) % 4, ylo, z, yhi, c), (x - o + 4) % 4
        return dev(x, ylo, (z + o) % 4, yhi, c), (z - o + 4) % 4

    def start(self, phase):
        sent, got = [], []
        for part in range(3):
            dim, done = self.orders[part][phase], self.orders[part][:phase]
            for o in (1,) if dim == "y" else (2, 1, 3):
                where, origin = self.peer(dim, o)
                n = (phase * 3 + part) * 3 + o - 1
                here_now = self.at(done, part, {})
                cp = push(here_now, here_now, self.ss.at[n], self.rs.at[n], where)
                cp.start()
                sent.append(cp)
                back = self.at(done, part, {dim: origin})
                got.append((push(back, back, self.ss.at[n], self.rs.at[n], where), back))
        self.running = sent, got

    def finish(self, each=None):
        sent, got = self.running
        for cp, back in got:
            cp.wait_recv()
            if each is not None:
                each(back)
        for cp in sent:
            cp.wait_send()

    def held(self):
        return [self.at(self.orders[p][:2], p, {}) for p in range(3)]


class Gather:
    def __init__(self, wv, pieces, ss, rs, ps, pr, ls):
        x, ylo, z, yhi, c = here()
        self.wv, self.pieces = wv, pieces
        self.ps, self.pr, self.ls = ps, pr, ls
        self.t = 2 * yhi + c
        self.other = 2 * (1 - yhi) + c
        self.partner = dev(x, ylo, z, yhi, 1 - c)
        self.cross = dev(x, 1 - ylo, z, 1 - yhi, c)
        self.spread = Spread(wv.at[self.other], ss, rs)
        self.handed = []

    def side(self, n):
        ref, first = self.pieces[n]
        spot = self.wv.at[self.t, pl.ds(first, ref.shape[0])]
        return (
            pltpu.make_async_copy(ref, spot, self.ls.at[n]),
            push(ref, spot, self.ps.at[n], self.pr.at[n], self.partner),
        )

    def s0(self):
        x, ylo, z, yhi, c = here()
        for ref, first in self.pieces:

            @pl.when((x >= first) & (x < first + ref.shape[0]))
            def _(ref=ref, first=first):
                push(
                    ref.at[x - first, z, :, :, half(1 - ylo)],
                    self.wv.at[self.t, x, z, :, :, half(1 - ylo)],
                    self.ps.at[2],
                    self.pr.at[2],
                    self.cross,
                ).start()

        for n in range(len(self.pieces)):
            for cp in self.side(n):
                cp.start()

    def s1(self):
        x, ylo, z, yhi, c = here()
        landed = self.wv.at[self.other, x, z, :, :, half(ylo)]
        cp = push(landed, landed, self.ps.at[2], self.pr.at[2], self.cross)
        cp.wait_recv()
        cp.wait_send()
        self.spread.start(0)

    def s2(self):
        self.spread.finish()
        self.spread.start(1)

    def hand(self, ref):
        n = 3 + len(self.handed)
        cp = push(ref, ref, self.ps.at[n], self.pr.at[n], self.partner)
        cp.start()
        self.handed.append(cp)

    def s3(self):
        self.spread.finish()
        self.spread.start(2)
        for ref in self.spread.held():
            self.hand(ref)

    def s4(self):
        self.spread.finish(self.hand)

    def s5(self):
        for n in range(len(self.pieces)):
            local, cp = self.side(n)
            local.wait()
            cp.wait_send()
            cp.wait_recv()
        for cp in self.handed:
            cp.wait_send()
            cp.wait_recv()


def gather_scratch():
    dma = pltpu.SemaphoreType.DMA
    return [dma((27,)), dma((27,)), dma((13,)), dma((13,)), dma((2,))]


def chips_around():
    x, ylo, z, yhi, c = here()
    return [dev((x + o) % 4, ylo, z, yhi, c) for o in (1, 2, 3)] + [
        dev(x, 1 - ylo, z, yhi, c),
        dev(x, 1 - ylo, z, 1 - yhi, c),
    ]


def dp_group():
    x, ylo, z, yhi, c = here()
    t = 2 * yhi + c
    return [(2 * x + ylo, (z + a) % 4, (t + b) % 4) for a in range(4) for b in range(4) if a or b]


def row_places():
    x, ylo, z, yhi, c = here()
    return [(2 * a + b, dev(x, ylo, a, yhi, b)) for a in range(4) for b in range(2)], 2 * z + c


def row_mates():
    x, ylo, z, yhi, c = here()
    me = 2 * z + c
    return [dev(x, ylo, ((me + o) % 8) // 2, yhi, (me + o) % 2) for o in range(1, 8)]


def deal(j, where, me, src, dst, s, r):
    @pl.when(me != j)
    def _():
        push(src, dst, s(j), r(me), where).start()

    @pl.when(me == j)
    def _():
        pltpu.make_async_copy(src, dst, s(j)).start()


def dealt(j, where, me, src, dst, s, r):
    @pl.when(me != j)
    def _():
        cp = push(src, dst, s(j), r(j), where)
        cp.wait_send()
        cp.wait_recv()

    @pl.when(me == j)
    def _():
        pltpu.make_async_copy(src, dst, s(j)).wait()


def place_of(sem):
    return lambda j: sem.at[j]


def attn_rows(wa, t, low, high):
    first, last = low // 192, -(-high // 192)
    whole = wa[t, first:last].reshape(192 * (last - first), D)
    return whole[low - 192 * first : high - 192 * first]


def up_rows(wt):
    return wt[0:2].reshape(D, D)


def down_rows(wt):
    return wt[2:4].reshape(D, D)


class Inputs:
    def __init__(self, hid, cot, x0, cots, hs, hr, cs, cr, ls):
        self.refs = hid, cot, x0, cots
        self.sems = hs, hr, cs, cr, ls

    def move(self, begin):
        hid, cot, x0, cots = self.refs
        hs, hr, cs, cr, ls = self.sems
        x, ylo, z, yhi, c = here()
        t = 2 * yhi + c
        dp = 2 * x + ylo
        for b in range(4):

            @pl.when((t == z) & (t != b))
            def _(b=b):
                cp = push(hid.at[b // 2, b % 2], x0, hs.at[b], hr.at[0], (dp, z, b))
                if begin:
                    cp.start()
                else:
                    cp.wait_send()

            @pl.when(jnp.logical_not((t == z) & (t == b)))
            def _(b=b):
                cp = push(cot.at[b // 2, b % 2], cots.at[z], cs.at[b], cr.at[z], (dp, t, b))
                if begin:
                    cp.start()
                else:
                    cp.wait_send()

            @pl.when((t == z) & (t == b))
            def _(b=b):
                first = pltpu.make_async_copy(hid.at[b // 2, b % 2], x0, ls.at[0])
                second = pltpu.make_async_copy(cot.at[b // 2, b % 2], cots.at[z], ls.at[1])
                if begin:
                    first.start()
                    second.start()
                else:
                    second.wait()

            if not begin:

                @pl.when(jnp.logical_not((t == z) & (z == b)))
                def _(b=b):
                    push(cots.at[b], cots.at[b], cs.at[b], cr.at[b], (dp, z, (t + 1) % 4)).wait_recv()

    def tokens(self):
        hid, cot, x0, cots = self.refs
        hs, hr, cs, cr, ls = self.sems
        x, ylo, z, yhi, c = here()
        t = 2 * yhi + c

        @pl.when(t != z)
        def _():
            push(x0, x0, hs.at[0], hr.at[0], (2 * x + ylo, z, (t + 1) % 4)).wait_recv()

        @pl.when(t == z)
        def _():
            pltpu.make_async_copy(hid.at[0, 0], x0, ls.at[0]).wait()


def forward_kernel(app, *refs):
    refs = list(refs)

    def take(count):
        got = refs[:count]
        del refs[:count]
        return got

    if app == 0:
        hid, cot = take(2)
    else:
        (a_ref,) = take(1)
        b_ref = take(1)[0] if app == 2 else None
    mod, segc, segr, cosine, sine = take(5)
    if app == 0:
        attn_loc, up_loc, down_loc = take(3)
    elif app == 1:
        wa_in, up_loc, down_loc = take(3)
    else:
        wa_in, wm_in = take(2)
    y_ref, qkv, lse, att, ba, mid, pre, bb = take(8)
    if app == 0:
        x0, cots, wa_out, wm_out, wa1_out = take(5)
    elif app == 1:
        (wm_out,) = take(1)
    sbuf, obuf, rbuf, wa, wm, wsem, ss, rs, ss2, rs2 = take(10)
    x, ylo, z, yhi, c = here()
    places, me = row_places()
    saved = []

    def save(src, dst):
        cp = pltpu.make_async_copy(src, dst, wsem.at[8 + len(saved)])
        cp.start()
        saved.append(cp)

    fetches = []
    if app == 0:
        (wa1,) = take(1)
        g_attn = Gather(wa, [(attn_loc.at[0], 0)], *take(5))
        g_mlp = Gather(wm, [(up_loc.at[0], 0), (down_loc.at[0], 2)], *take(5))
        g_next = Gather(wa1, [(attn_loc.at[1], 0)], *take(5))
        inputs = Inputs(hid, cot, x0, cots, *take(5))
        greet(dp_group() + chips_around())()
        inputs.move(True)
        g_attn.s0()
        g_mlp.s0()
        g_attn.s1()
        g_attn.s2()
        g_mlp.s1()
        g_attn.s3()
        inputs.tokens()
        a_ref, b_ref = x0, None
        entered = lambda: None
    else:
        if app == 1:
            g_mlp = Gather(wm, [(up_loc.at[1], 0), (down_loc.at[1], 2)], *take(5))
            entered = greet(row_mates() + chips_around())
        else:
            entered = greet(row_mates())
        fetches.append(pltpu.make_async_copy(wa_in, wa, wsem.at[0]))
        if app > 1:
            for t in range(4):
                fetches.append(pltpu.make_async_copy(wm_in.at[t], wm.at[t], wsem.at[1 + t]))
        for cp in fetches:
            cp.start()

    v = a_ref[...].astype(F32)
    if b_ref is not None:
        v = v + b_ref[...].astype(F32)
    hat, _ = normalize(v)
    normed = (hat * (1.0 + mod[1:2, :]) + mod[0:1, :]).astype(BF)
    cos_here, sin_here = cosine[...], sine[...]
    low = lanes((TOK, 128)) < 64
    if app == 0:
        g_attn.s4()
        g_mlp.s2()
        g_attn.s5()
        save(wa, wa_out)
    else:
        entered()
        if app == 1:
            g_mlp.s0()
        fetches[0].wait()
    for t in range(4):
        got = nt(normed, attn_rows(wa, t, 0, 640))
        t0, t1, t2, t3, t4 = (got[:, 128 * i : 128 * (i + 1)] for i in range(5))
        s0, s1, s2, s3, s4 = (swap(u) for u in (t0, t1, t2, t3, t4))
        for head, (q, k, w) in enumerate(
            (
                (jnp.where(low, t0, s3), jnp.where(low, s0, t3), jnp.where(low, t1, s4)),
                (jnp.where(low, s1, s3), jnp.where(low, t2, t3), jnp.where(low, s2, s4)),
            )
        ):
            j = 2 * t + head
            sbuf[j, :, 0:128] = (turn(q, cos_here, sin_here).astype(BF).astype(F32) * 0.125).astype(BF)
            sbuf[j, :, 128:256] = turn(k, cos_here, sin_here).astype(BF)
            sbuf[j, :, 256:384] = w.astype(BF)
            deal(j, places[j][1], me, sbuf.at[j], qkv.at[me], place_of(ss), place_of(rs))
    if app == 0:
        g_mlp.s3()
        g_next.s0()
    if app == 1:
        g_mlp.s1()
    for j, where in places:
        dealt(j, where, me, sbuf.at[j], qkv.at[j], place_of(ss), place_of(rs))
    if app == 1:
        g_mlp.s2()

    keys = qkv[:, :, 128:256].reshape(SEQ, 128)
    values = qkv[:, :, 256:384].reshape(SEQ, 128)
    seg_keys = segr[...]

    def softmax(q, seg_q):
        scores = jnp.where(seg_q == seg_keys, nt(q, keys), -1e30)
        largest = jnp.max(scores, axis=-1, keepdims=True)
        raised = jnp.exp(scores - largest)
        total = jnp.sum(raised, axis=-1, keepdims=True)
        mixed = nn(raised.astype(BF), values) * (1.0 / total)
        return mixed, largest + jnp.log(total)

    def flat(column):
        wide = jnp.broadcast_to(column, (column.shape[0], 128))
        return jnp.transpose(wide)[0:8, :]

    for a in range(4):
        if app == 0 and a == 1:
            g_next.s1()
        if app == 1 and a == 2:
            g_mlp.s3()
        q = qkv[2 * a : 2 * a + 2, :, 0:128].reshape(256, 128)
        q = jnp.where(lanes((256, 128)) < 64, q, 0).astype(BF)
        mixed, total = softmax(q, segc[256 * a : 256 * (a + 1), :])
        q2 = jnp.where(low, 0, qkv[2 * a + c, :, 0:128]).astype(BF)
        mixed2, total2 = softmax(q2, segc[pl.ds(256 * a + TOK * c, TOK), :])
        lse[a, :, 0:256] = flat(total)
        lse[a, :, 256:384] = flat(total2)
        for b in range(2):
            j = 2 * a + b
            part = mixed[TOK * b : TOK * (b + 1)]
            obuf[j] = jnp.where(low | (c != b), part, mixed2).astype(BF)
            deal(j, places[j][1], me, obuf.at[j], rbuf.at[me], place_of(ss2), place_of(rs2))
    if app < 2:
        g_mlp.s4()
    if app == 0:
        g_next.s2()
    for j, where in places:
        dealt(j, where, me, obuf.at[j], rbuf.at[j], place_of(ss2), place_of(rs2))

    branch_a = jnp.zeros((TOK, D), F32)
    for t in range(4):
        first, second = rbuf[2 * t], rbuf[2 * t + 1]
        own = jnp.where(low, first.astype(F32), swap(second.astype(F32))).astype(BF)
        extra = jnp.where(low, 0, rbuf[2 * t + c]).astype(BF)
        att[:, 128 * t : 128 * (t + 1)] = own
        att[:, 512 + 128 * t : 512 + 128 * (t + 1)] = extra
        branch_a = branch_a + nn(own, attn_rows(wa, t, 576, 704)) + nn(extra, attn_rows(wa, t, 640, 768))
    ba[...] = branch_a
    middle = v + mod[2:3, :] * branch_a
    mid[...] = middle
    hat_b, _ = normalize(middle)
    normed_b = (hat_b * (1.0 + mod[4:5, :]) + mod[3:4, :]).astype(BF)
    if app < 2:
        g_mlp.s5()
        save(wm, wm_out)
    if app == 0:
        g_next.s3()
    for cp in fetches[1:]:
        cp.wait()
    total_b = jnp.zeros((TOK, D), F32)
    for t in range(4):
        before = nn(normed_b, up_rows(wm.at[t]))
        pre[:, D * t : D * (t + 1)] = before.astype(pre.dtype)
        total_b = total_b + nn(jax.nn.gelu(before, approximate=True).astype(BF), down_rows(wm.at[t]))
    bb[...] = total_b
    y_ref[...] = (middle + mod[5:6, :] * total_b).astype(BF)
    if app == 0:
        g_next.s4()
        g_next.s5()
        save(wa1, wa1_out)
        inputs.move(False)
    for cp in saved:
        cp.wait()


def forward(app, *operands):
    dma = pltpu.SemaphoreType.DMA

    def shape(*dims, dtype=BF):
        return jax.ShapeDtypeStruct(dims, dtype)

    outs = [
        shape(TOK, D),
        shape(8, TOK, 384),
        shape(4, 8, 384, dtype=F32),
        shape(TOK, 1024),
        shape(TOK, D, dtype=F32),
        shape(TOK, D, dtype=F32),
        shape(TOK, 4 * D, dtype=F32),
        shape(TOK, D, dtype=F32),
    ]
    out_specs = [VM] * 8
    scratch = [
        pltpu.VMEM((8, TOK, 384), BF),
        pltpu.VMEM((8, TOK, 128), BF),
        pltpu.VMEM((8, TOK, 128), BF),
        pltpu.VMEM((4,) + ATTN, BF),
        pltpu.VMEM((4,) + MLP, BF),
        dma((11,)),
    ] + [dma((8,))] * 4
    if app == 0:
        in_specs = [ANY] * 2 + [VM] * 5 + [ANY] * 3
        outs += [shape(TOK, D), shape(4, TOK, D), shape(4, *ATTN), shape(4, *MLP), shape(4, *ATTN)]
        out_specs += [VM] + [ANY] * 4
        scratch.append(pltpu.VMEM((4,) + ATTN, BF))
        for _ in range(3):
            scratch += gather_scratch()
        scratch += [dma((4,)), dma((1,)), dma((4,)), dma((4,)), dma((2,))]
    elif app == 1:
        in_specs = [VM] * 6 + [ANY] * 3
        outs.append(shape(4, *MLP))
        out_specs.append(ANY)
        scratch += gather_scratch()
    else:
        in_specs = [VM] * (7 if app == 2 else 6) + [ANY] * 2
    return pl.pallas_call(
        functools.partial(forward_kernel, app),
        out_shape=tuple(outs),
        in_specs=in_specs,
        out_specs=tuple(out_specs),
        scratch_shapes=scratch,
        compiler_params=pltpu.CompilerParams(
            collective_id=1 + app, has_side_effects=True, vmem_limit_bytes=52 * 2**20
        ),
        name=f"forward_{app}",
    )(*operands)


class Reduce:
    def __init__(self, grads, refs):
        self.grads = grads
        (
            self.own0, self.own1, self.own2, self.in0, self.in1, self.in2,
            self.mid0, self.mid1, self.mid2, self.tot0, self.tot1, self.tot2,
            self.end0, self.end1, self.end2,
            self.ls, self.ss, self.rs, self.ss2, self.rs2, self.ss3, self.rs3,
        ) = refs

    @staticmethod
    def scratch():
        dma = pltpu.SemaphoreType.DMA

        def buf(*dims):
            return pltpu.VMEM(dims, BF)

        return [
            buf(2, 4, 48, D), buf(4, 4, 48, HALF), buf(2, 4, 48, D),
            buf(3, 2, 4, 48, D), buf(3, 4, 4, 48, HALF), buf(3, 2, 4, 48, D),
            buf(3, 4, 48, HALF), buf(3, 4, 48, HALF), buf(3, 2, 48, D),
            buf(4, 48, HALF), buf(4, 48, HALF), buf(2, 48, D),
            buf(3, 48, HALF), buf(3, 48, HALF), buf(3, 48, HALF),
            dma((3,)), dma((9,)), dma((9,)), dma((9,)), dma((9,)), dma((9,)), dma((9,)),
        ]

    @staticmethod
    def greeted():
        x, ylo, z, yhi, c = here()
        y = 2 * yhi + ylo
        found = [dev((x + o) % 4, ylo, z, yhi, c) for o in (1, 2, 3)]
        found += [dev(x, (y + o) % 2, z, ((y + o) % 4) // 2, c) for o in (1, 2, 3)]
        return found

    def xpeer(self, o):
        x, ylo, z, yhi, c = here()
        return dev((x + o) % 4, ylo, z, yhi, c), (x + o) % 4

    def zpeer(self, o):
        x, ylo, z, yhi, c = here()
        return dev(x, ylo, (z + o) % 4, yhi, c), (z + o) % 4

    def ypeer(self, o):
        x, ylo, z, yhi, c = here()
        to = (2 * yhi + ylo + o) % 4
        return dev(x, to % 2, z, to // 2, c), to

    def load(self):
        x, ylo, z, yhi, c = here()
        g = self.grads
        pairs = (
            (g.at[:, x, :, 0], self.own0),
            (g.at[yhi, :, :, 1, :, half(ylo)], self.own1),
            (g.at[:, :, z, 2], self.own2),
        )
        return [pltpu.make_async_copy(a, b, self.ls.at[n]) for n, (a, b) in enumerate(pairs)]

    def first(self):
        g, found = self.grads, []
        for o in (2, 1, 3):
            n = o - 1
            where, to = self.xpeer(o)
            found.append(push(g.at[:, to, :, 0], self.in0.at[n], self.ss.at[n], self.rs.at[n], where))
            where, to = self.ypeer(o)
            found.append(
                push(g.at[to // 2, :, :, 1, :, half(to % 2)], self.in1.at[n], self.ss.at[3 + n], self.rs.at[3 + n], where)
            )
            where, to = self.zpeer(o)
            found.append(push(g.at[:, :, to, 2], self.in2.at[n], self.ss.at[6 + n], self.rs.at[6 + n], where))
        return found

    def second(self):
        found = []
        for o in (2, 1, 3):
            n = o - 1
            where, to = self.ypeer(o)
            found.append(
                push(self.own0.at[to // 2, :, :, half(to % 2)], self.mid0.at[n], self.ss2.at[n], self.rs2.at[n], where)
            )
            where, to = self.zpeer(o)
            found.append(push(self.own1.at[:, to], self.mid1.at[n], self.ss2.at[3 + n], self.rs2.at[3 + n], where))
            where, to = self.xpeer(o)
            found.append(push(self.own2.at[:, to], self.mid2.at[n], self.ss2.at[6 + n], self.rs2.at[6 + n], where))
        return found

    def third(self):
        found = []
        for o in (2, 1, 3):
            n = o - 1
            where, to = self.zpeer(o)
            found.append(push(self.tot0.at[to], self.end0.at[n], self.ss3.at[n], self.rs3.at[n], where))
            where, to = self.xpeer(o)
            found.append(push(self.tot1.at[to], self.end1.at[n], self.ss3.at[3 + n], self.rs3.at[3 + n], where))
            where, to = self.ypeer(o)
            found.append(
                push(self.tot2.at[to // 2, :, half(to % 2)], self.end2.at[n], self.ss3.at[6 + n], self.rs3.at[6 + n], where)
            )
        return found

    def begin(self):
        for cp in self.load() + self.first():
            cp.start()

    def sum_first(self):
        for cp in self.load() + self.first():
            cp.wait()

        def body(i, carry):
            j, k = i // 4, i % 4
            for own, more in ((self.own0, self.in0), (self.own2, self.in2)):
                total = own[j, k].astype(F32)
                for n in range(3):
                    total = total + more[n, j, k].astype(F32)
                own[j, k] = total.astype(BF)
            for row in (j, j + 2):
                total = self.own1[row, k].astype(F32)
                for n in range(3):
                    total = total + self.in1[n, row, k].astype(F32)
                self.own1[row, k] = total.astype(BF)
            return carry

        lax.fori_loop(0, 8, body, 0)
        for cp in self.second():
            cp.start()

    def sum_second(self):
        x, ylo, z, yhi, c = here()
        for cp in self.second():
            cp.wait()
        for i in range(4):
            first = self.own0[yhi, i, :, half(ylo)].astype(F32)
            other = self.own1[i, z].astype(F32)
            for n in range(3):
                first = first + self.mid0[n, i].astype(F32)
                other = other + self.mid1[n, i].astype(F32)
            self.tot0[i] = first.astype(BF)
            self.tot1[i] = other.astype(BF)
        for i in range(2):
            total = self.own2[i, x].astype(F32)
            for n in range(3):
                total = total + self.mid2[n, i].astype(F32)
            self.tot2[i] = total.astype(BF)
        for cp in self.third():
            cp.start()

    def sum_third(self, fin):
        x, ylo, z, yhi, c = here()
        for cp in self.third():
            cp.wait()
        lasts = (self.tot0[z], self.tot1[x], self.tot2[yhi, :, half(ylo)])
        for p, (last, ends) in enumerate(zip(lasts, (self.end0, self.end1, self.end2))):
            total = last.astype(F32)
            for n in range(3):
                total = total + ends[n].astype(F32)
            fin[p] = total.astype(BF)


def gelu_parts(u):
    k = 0.7978845608028654
    square = u * u
    th = jnp.tanh(k * u * (1.0 + 0.044715 * square))
    half_up = 0.5 * (1.0 + th)
    slope = half_up + 0.5 * u * (1.0 - th * th) * (k * (1.0 + 0.134145 * square))
    return u * half_up, slope


def backward_kernel(layer, *refs):
    refs = list(refs)

    def take(count):
        got = refs[:count]
        del refs[:count]
        return got

    a_refs = take(2)
    b_refs = [None, take(1)[0]] if layer == 0 else [None, None]
    (cots,) = take(1)
    more_dy = take(1)[0] if layer == 0 else None
    mod, segc, segr, cosine, sine = take(5)
    qkvs, lses, atts, bas, mids, pres, bbs = (take(2) for _ in range(7))
    wa_in, wm_in = take(2)
    before = take(1)[0] if layer == 0 else None
    din, dinb, dmod, grads = take(4)
    fin = take(1)[0] if layer == 0 else None
    own_na, own_nb, own_dba, own_dbb, own_act, own_dpre, own_dpj = take(7)
    got_na, got_nb, got_dba, got_dbb, got_at, got_act, got_dpre, got_dpj = take(8)
    sbuf, rbuf, sbig, rbig, dmid, dnb, k_own, k_sh, v_own, v_sh = take(10)
    wa, wm, stage_up, stage_down, stage_attn = take(5)
    wsem, gsem, ss, rs, ss2, rs2, xs, xr = take(8)
    rows_of = [slice(TOK * e, TOK * (e + 1)) for e in range(2)]
    x, ylo, z, yhi, c = here()
    places, me = row_places()
    partner = dev(x, ylo, z, yhi, 1 - c)
    reduce = Reduce(before, take(22)) if layer == 0 else None
    entered = greet(row_mates() + (Reduce.greeted() if layer == 0 else []))

    def wm_fetch(t):
        return pltpu.make_async_copy(wm_in.at[t], wm.at[t % 2], wsem.at[1 + t])

    wm_fetch(0).start()
    wm_fetch(1).start()
    wa_fetch = pltpu.make_async_copy(wa_in, wa, wsem.at[0])
    wa_fetch.start()
    scale_a, gate_a = mod[1:2, :], mod[2:3, :]
    scale_b, gate_b = mod[4:5, :], mod[5:6, :]
    low = lanes((TOK, 128)) < 64
    exchanged = {}

    def hand(name, src, dst):
        n = len(exchanged)
        cp = push(src, dst, xs.at[n], xr.at[n], partner)
        cp.start()
        exchanged[name] = cp

    def have(*names):
        for name in names:
            exchanged[name].wait_send()
            exchanged[name].wait_recv()

    def gradient(e):
        dy = cots[layer + 2 * e].astype(F32)
        return dy if more_dy is None else dy + more_dy[e]

    def entry(e):
        v = a_refs[e][...].astype(F32)
        return v if b_refs[e] is None else v + b_refs[e][...].astype(F32)

    dgate_b = jnp.zeros((1, D), F32)
    for e in range(2):
        dy = gradient(e)
        dgate_b = dgate_b + jnp.sum(dy * bbs[e][...], axis=0, keepdims=True)
        own_dbb[rows_of[e], :] = (gate_b * dy).astype(BF)
        hat_b, _ = normalize(mids[e][...])
        own_nb[rows_of[e], :] = (hat_b * (1.0 + scale_b) + mod[3:4, :]).astype(BF)
        hat_a, _ = normalize(entry(e))
        own_na[rows_of[e], :] = (hat_a * (1.0 + scale_a) + mod[0:1, :]).astype(BF)
    entered()
    hand("dbb", own_dbb, got_dbb)
    hand("nb", own_nb, got_nb)
    hand("na", own_na, got_na)
    for e in range(2):
        hand(f"at{e}", atts[e], got_at.at[e])
    if reduce is not None:
        reduce.begin()

    for t in range(4):
        wm_fetch(t).wait()
        d_act = nt(own_dbb[...], down_rows(wm.at[t % 2]))
        for e in range(2):
            act, slope = gelu_parts(pres[e][:, D * t : D * (t + 1)])
            own_act[t, rows_of[e], :] = act.astype(BF)
            own_dpre[t, rows_of[e], :] = (d_act[rows_of[e]] * slope).astype(BF)
        more = nt(own_dpre[t], up_rows(wm.at[t % 2]))
        dnb[...] = more if t == 0 else dnb[...] + more
        if t < 2:
            wm_fetch(t + 2).start()
    for h in range(2):
        hand(f"act{h}", own_act.at[2 * h + 1 - c], got_act.at[h])
        hand(f"dpre{h}", own_dpre.at[2 * h + 1 - c], got_dpre.at[h])

    dgate_a = jnp.zeros((1, D), F32)
    dscale_b = jnp.zeros((1, D), F32)
    dshift_b = jnp.zeros((1, D), F32)
    for e in range(2):
        hat_b, inv_b = normalize(mids[e][...])
        g = dnb[rows_of[e], :]
        dscale_b = dscale_b + jnp.sum(g * hat_b, axis=0, keepdims=True)
        dshift_b = dshift_b + jnp.sum(g, axis=0, keepdims=True)
        d_middle = gradient(e) + norm_back(g * (1.0 + scale_b), hat_b, inv_b)
        dmid[rows_of[e], :] = d_middle
        dgate_a = dgate_a + jnp.sum(d_middle * bas[e][...], axis=0, keepdims=True)
        own_dba[rows_of[e], :] = (gate_a * d_middle).astype(BF)
    hand("dba", own_dba, got_dba)
    wa_fetch.wait()
    for t in range(4):
        first = nt(own_dba[...], attn_rows(wa, t, 576, 704))
        second = nt(own_dba[...], attn_rows(wa, t, 640, 768))
        for e in range(2):
            sbuf[2 * t, e] = jnp.where(low, first[rows_of[e]], second[rows_of[e]]).astype(BF)
            sbuf[2 * t + 1, e] = second[rows_of[e]].astype(BF)
        for b in range(2):
            j = 2 * t + b
            deal(j, places[j][1], me, sbuf.at[j], rbuf.at[me], place_of(ss), place_of(rs))

    have("dbb", "nb", "act0", "dpre0", "act1", "dpre1")

    def staged(n, stage, dst):
        return pltpu.make_async_copy(stage, dst, gsem.at[n])

    for h in range(2):
        t = 2 * h + c
        up_copy = staged(0, stage_up, grads.at[h, 0:2, :, :, 16:48])
        down_copy = staged(1, stage_down, grads.at[h, 2:4, :, :, 16:48])
        if h:
            up_copy.wait()
        total = tn(own_nb[...], own_dpre[t]) + tn(got_nb[...], got_dpre[h])
        stage_up[...] = total.astype(BF).reshape(2, 4, 3, 32, D)
        up_copy.start()
        if h:
            down_copy.wait()
        total = tn(own_act[t], own_dbb[...]) + tn(got_act[h], got_dbb[...])
        stage_down[...] = total.astype(BF).reshape(2, 4, 3, 32, D)
        down_copy.start()
    for j, where in places:
        dealt(j, where, me, sbuf.at[j], rbuf.at[j], place_of(ss), place_of(rs))

    seg_keys = segc[...]
    wide = lanes((256, 128)) < 64
    for e in range(2):
        qkv, lse = qkvs[e], lses[e]
        for ref in (k_own, k_sh, v_own, v_sh):
            ref[...] = jnp.zeros_like(ref)

        def one(q, go, seg_q, total, k_sum, v_sum, qkv=qkv):
            keys = qkv[:, :, 128:256].reshape(SEQ, 128)
            values = qkv[:, :, 256:384].reshape(SEQ, 128)
            scores = jnp.where(seg_keys == seg_q, nt(keys, q), -1e30)
            p = jnp.exp(scores - total)
            d_p = nt(values, go)
            centre = jnp.sum(d_p * p, axis=0, keepdims=True)
            d_s = (p * (d_p - centre)).astype(BF)
            v_sum[...] += nn(p.astype(BF), go)
            k_sum[...] += nn(d_s, q)
            return tn(d_s, keys) * 0.125

        for a in range(4):
            q = qkv[2 * a : 2 * a + 2, :, 0:128].reshape(256, 128)
            go = rbuf[2 * a : 2 * a + 2, e].reshape(256, 128)
            dq = one(
                jnp.where(wide, q, 0).astype(BF),
                jnp.where(wide, go, 0).astype(BF),
                segr[0:1, 256 * a : 256 * (a + 1)],
                lse[a, 0:1, 0:256],
                k_own,
                v_own,
            )
            q2 = jnp.where(low, 0, qkv[2 * a + c, :, 0:128]).astype(BF)
            go2 = jnp.where(low, 0, rbuf[2 * a + c, e]).astype(BF)
            seg2 = jnp.where(
                c == 0,
                segr[0:1, 256 * a : 256 * a + 128],
                segr[0:1, 256 * a + 128 : 256 * a + 256],
            )
            dq2 = one(q2, go2, seg2, lse[a, 0:1, 256:384], k_sh, v_sh)
            for b in range(2):
                rows = slice(256 * a + TOK * b, 256 * a + TOK * (b + 1))
                whole = jnp.where(low, dq[TOK * b : TOK * (b + 1)], jnp.where(c == b, dq2, 0.0))
                sbig[2 * a + b, e, :, 0:128] = turn(whole, cosine[rows, :], -sine[rows, :]).astype(BF)
        for j, where in places:
            rows = slice(TOK * j, TOK * (j + 1))
            whole = jnp.where(low, k_own[rows, :], k_sh[rows, :])
            sbig[j, e, :, 128:256] = turn(whole, cosine[rows, :], -sine[rows, :]).astype(BF)
            sbig[j, e, :, 256:384] = jnp.where(low, v_own[rows, :], v_sh[rows, :]).astype(BF)
            deal(
                j, where, me, sbig.at[j, e], rbig.at[me, e],
                lambda i, e=e: ss2.at[e, i], lambda i, e=e: rs2.at[e, i],
            )
        if reduce is not None:
            (reduce.sum_first, reduce.sum_second)[e]()
    for e in range(2):
        for j, where in places:
            dealt(
                j, where, me, sbig.at[j, e], rbig.at[j, e],
                lambda i, e=e: ss2.at[e, i], lambda i, e=e: rs2.at[e, i],
            )
        for t in range(4):
            q0, k0, v0 = (rbig[2 * t, e, :, 128 * i : 128 * (i + 1)].astype(F32) for i in range(3))
            q1, k1, v1 = (rbig[2 * t + 1, e, :, 128 * i : 128 * (i + 1)].astype(F32) for i in range(3))
            tiles = (
                jnp.where(low, q0, swap(k0)),
                jnp.where(low, v0, swap(q1)),
                jnp.where(low, k1, swap(v1)),
                jnp.where(low, swap(q0 + q1), k0 + k1),
                jnp.where(low, swap(v0 + v1), 0.0),
            )
            for i, tile in enumerate(tiles):
                own_dpj[t, rows_of[e], 128 * i : 128 * (i + 1)] = tile.astype(BF)
    for h in range(2):
        hand(f"dpj{h}", own_dpj.at[2 * h + 1 - c], got_dpj.at[h])
    dna = jnp.zeros((2 * TOK, D), F32)
    for t in range(4):
        dna = dna + nn(own_dpj[t], attn_rows(wa, t, 0, 640))
    dscale_a = jnp.zeros((1, D), F32)
    dshift_a = jnp.zeros((1, D), F32)
    for e in range(2):
        hat_a, inv_a = normalize(entry(e))
        g = dna[rows_of[e]]
        dscale_a = dscale_a + jnp.sum(g * hat_a, axis=0, keepdims=True)
        dshift_a = dshift_a + jnp.sum(g, axis=0, keepdims=True)
        total = dmid[rows_of[e], :] + norm_back(g * (1.0 + scale_a), hat_a, inv_a)
        din[e] = total
        dinb[e] = total.astype(BF)
    for i, part in enumerate((dshift_a, dscale_a, dgate_a, dshift_b, dscale_b, dgate_b)):
        dmod[i : i + 1, :] = part
    dmod[6:8, :] = jnp.zeros((2, D), F32)

    have("na", "at0", "at1", "dba", "dpj0", "dpj1")
    for h in range(2):
        t = 2 * h + c
        copy = staged(2, stage_attn, grads.at[h, :, :, :, 0:16])
        if h:
            copy.wait()
        total = tn(own_dpj[t], own_na[...]) + tn(got_dpj[h], got_na[...])
        stage_attn[0:3] = total[0:576].astype(BF).reshape(3, 4, 3, 16, D)
        parts = []
        for first in (0, 512):
            cols = pl.ds(pl.multiple_of(first + 128 * t, 128), 128)
            total = jnp.zeros((128, D), F32)
            for e in range(2):
                total = total + tn(atts[e][:, cols], own_dba[rows_of[e], :])
                total = total + tn(got_at[e, :, cols], got_dba[rows_of[e], :])
            parts.append(total)
        total = jnp.concatenate([parts[0], parts[1][64:128]], axis=0)
        stage_attn[3] = total.astype(BF).reshape(4, 3, 16, D)
        copy.start()
    if reduce is not None:
        reduce.sum_third(fin)
    staged(0, stage_up, grads.at[1, 0:2, :, :, 16:48]).wait()
    staged(1, stage_down, grads.at[1, 2:4, :, :, 16:48]).wait()
    staged(2, stage_attn, grads.at[1, :, :, :, 0:16]).wait()


def backward(layer, *operands):
    dma = pltpu.SemaphoreType.DMA
    both = 2 * TOK

    def buf(*dims, dtype=BF):
        return pltpu.VMEM(dims, dtype)

    outs = [
        jax.ShapeDtypeStruct((2, TOK, D), F32),
        jax.ShapeDtypeStruct((2, TOK, D), BF),
        jax.ShapeDtypeStruct((8, D), F32),
        jax.ShapeDtypeStruct((2,) + UNIT, BF),
    ]
    out_specs = [VM, VM, VM, ANY]
    if layer == 0:
        outs.append(jax.ShapeDtypeStruct((3, 48, HALF), BF))
        out_specs.append(VM)
    scratch = [buf(both, D)] * 4 + [buf(4, both, D)] * 2 + [buf(4, both, 640)]
    scratch += [buf(both, D)] * 4 + [buf(2, TOK, 1024)] + [buf(2, both, D)] * 2 + [buf(2, both, 640)]
    scratch += [buf(8, 2, TOK, 128)] * 2 + [buf(8, 2, TOK, 384)] * 2
    scratch += [buf(both, D, dtype=F32)] * 2 + [buf(SEQ, 128, dtype=F32)] * 4
    scratch += [buf(4, *ATTN), buf(2, *MLP), buf(2, 4, 3, 32, D), buf(2, 4, 3, 32, D), buf(*ATTN)]
    scratch += [dma((5,)), dma((3,)), dma((8,)), dma((8,)), dma((2, 8)), dma((2, 8)), dma((12,)), dma((12,))]
    if layer == 0:
        scratch += Reduce.scratch()
    vmem_in = len(operands) - (3 if layer == 0 else 2)
    return pl.pallas_call(
        functools.partial(backward_kernel, layer),
        out_shape=tuple(outs),
        in_specs=[VM] * vmem_in + [ANY] * (len(operands) - vmem_in),
        out_specs=tuple(out_specs),
        scratch_shapes=scratch,
        compiler_params=pltpu.CompilerParams(
            collective_id=5 + layer, has_side_effects=True, vmem_limit_bytes=62 * 2**20
        ),
        name=f"backward_{layer}",
    )(*operands)


def finish_kernel(
    g0, fin1, dm0, dm1, feat, y0, y1, y2, y3, db0, db1,
    out0, out1, y_out, g_out, rows_out,
    fin0, dm_in, dsum, *rest,
):
    rest = list(rest)
    reduce = Reduce(g0, rest[:22])
    ss_a, rs_a, ss_b, rs_b, ys_s, ys_r, gs_s, gs_r, ms, mr, ms2, mr2, fsem = rest[22:]
    x, ylo, z, yhi, c = here()
    t = 2 * yhi + c
    dp = 2 * x + ylo
    places, me = row_places()
    row = 2 * dp + yhi
    others = []
    for o in range(1, 16):
        r = (row + o) % 16
        others.append(dev(r // 4, (r // 2) % 2, z, r % 2, c))
    far = []
    for o in range(1, 8):
        g = (dp + o) % 8
        far += [(g, z, 2 * b + c) for b in range(2)]
    greet(dp_group() + far)()
    reduce.begin()

    first = pltpu.make_async_copy(fin1, out1.at[x, z, :, :, half(ylo)], fsem.at[0])
    first.start()
    for j, where in places:

        @pl.when(me != j)
        def _(j=j, where=where):
            push(dm0, dm_in.at[me, 0], ms.at[0, j], mr.at[0, me], where).start()
            push(dm1, dm_in.at[me, 1], ms.at[1, j], mr.at[1, me], where).start()

    y_src = (y0, y1, y2, y3)
    g_src = (db0.at[0], db1.at[0], db0.at[1], db1.at[1])

    def scatter(src, dst, s_sem, r_sem, begin):
        for s in range(4):
            mine = (z == s) & (t == z)

            @pl.when(jnp.logical_not(mine))
            def _(s=s):
                cp = push(src[s], dst.at[yhi, c], s_sem.at[s], r_sem.at[t], (dp, s, z))
                if begin:
                    cp.start()
                else:
                    cp.wait_send()

            @pl.when(mine)
            def _(s=s):
                cp = pltpu.make_async_copy(src[s], dst.at[yhi, c], s_sem.at[s])
                if begin:
                    cp.start()
                else:
                    cp.wait()

        if not begin:
            for b in range(4):

                @pl.when(jnp.logical_not((t == z) & (t == b)))
                def _(b=b):
                    spot = dst.at[b // 2, b % 2]
                    push(spot, spot, s_sem.at[b], r_sem.at[b], (dp, z, (t + 1) % 4)).wait_recv()

    scatter(y_src, y_out, ys_s, ys_r, True)
    scatter(g_src, g_out, gs_s, gs_r, True)
    ag1, ag0 = Spread(out1, ss_a, rs_a), Spread(out0, ss_b, rs_b)
    first.wait()
    ag1.start(0)

    for j, where in places:

        @pl.when(me != j)
        def _(j=j, where=where):
            for l, ref in enumerate((dm0, dm1)):
                cp = push(ref, dm_in.at[j, l], ms.at[l, j], mr.at[l, j], where)
                cp.wait_send()
                cp.wait_recv()

        @pl.when(me == j)
        def _(j=j):
            dm_in[j, 0] = dm0[...]
            dm_in[j, 1] = dm1[...]

    total = dm_in[0]
    for j in range(1, 8):
        total = total + dm_in[j]
    dsum[...] = total
    dsum[0, 6:7, 0:128] = feat[...]
    moved = [
        push(dsum, rows_out.at[row], ms2.at[o], mr2.at[o], where) for o, where in enumerate(others)
    ]
    for cp in moved:
        cp.start()
    keep = pltpu.make_async_copy(dsum, rows_out.at[row], fsem.at[1])
    keep.start()
    ag1.finish()
    ag1.start(1)

    reduce.sum_first()
    ag1.finish()
    reduce.sum_second()
    ag1.start(2)
    reduce.sum_third(fin0)
    last = pltpu.make_async_copy(fin0, out0.at[x, z, :, :, half(ylo)], fsem.at[2])
    last.start()
    last.wait()
    for phase in range(3):
        ag0.start(phase)
        ag0.finish()
    ag1.finish()
    keep.wait()
    for cp in moved:
        cp.wait()
    scatter(y_src, y_out, ys_s, ys_r, False)
    scatter(g_src, g_out, gs_s, gs_r, False)


def finish(*operands):
    dma = pltpu.SemaphoreType.DMA
    return pl.pallas_call(
        finish_kernel,
        out_shape=(
            jax.ShapeDtypeStruct(UNIT, BF),
            jax.ShapeDtypeStruct(UNIT, BF),
            jax.ShapeDtypeStruct((2, 2, TOK, D), BF),
            jax.ShapeDtypeStruct((2, 2, TOK, D), BF),
            jax.ShapeDtypeStruct((16, 2, 8, D), F32),
        ),
        in_specs=[ANY] + [VM] * 4 + [ANY] * 6,
        out_specs=(ANY,) * 5,
        scratch_shapes=[
            pltpu.VMEM((3, 48, HALF), BF),
            pltpu.VMEM((8, 2, 8, D), F32),
            pltpu.VMEM((2, 8, D), F32),
        ]
        + Reduce.scratch()
        + [dma((27,)), dma((27,)), dma((27,)), dma((27,))]
        + [dma((4,)), dma((4,)), dma((4,)), dma((4,))]
        + [dma((2, 8)), dma((2, 8)), dma((15,)), dma((15,)), dma((3,))],
        compiler_params=pltpu.CompilerParams(
            collective_id=7, has_side_effects=True, vmem_limit_bytes=40 * 2**20
        ),
        name="finish",
    )(*operands)


def modulation_kernel(rows, grad_mod, grad_bias):
    features = rows[:, 0, 6, 0:128]
    for l in range(2):
        for i in range(6):
            cols = slice(D * i, D * (i + 1))
            d = rows[:, l, i, :]
            grad_mod[l, :, cols] = lax.dot_general(
                features, d, (((0,), (0,)), ((), ())), precision=highest, preferred_element_type=F32
            )
            grad_bias[l : l + 1, cols] = jnp.sum(d, axis=0, keepdims=True)


def modulation_grads(rows):
    return pl.pallas_call(
        modulation_kernel,
        out_shape=(
            jax.ShapeDtypeStruct((2, 128, 6 * D), F32),
            jax.ShapeDtypeStruct((2, 6 * D), F32),
        ),
        in_specs=[VM],
        out_specs=(VM, VM),
        compiler_params=pltpu.CompilerParams(vmem_limit_bytes=30 * 2**20),
        name="modulation_grads",
    )(rows)


def rotary(count):
    frequency = np.exp(-np.log(10000.0) * np.arange(32) / 32)
    angles = np.arange(count)[:, None] * frequency[None, :]
    cos, sin = np.cos(angles), np.sin(angles)
    return (
        np.concatenate([cos] * 4, axis=1).astype(np.float32),
        np.concatenate([-sin, sin, -sin, sin], axis=1).astype(np.float32),
    )


def time_features(step_values, feature_count):
    half_count = feature_count // 2
    frequency = jnp.exp(-np.log(10000.0) * jnp.arange(half_count, dtype=F32) / half_count)
    angles = step_values.astype(F32)[:, None] * frequency[None, :]
    return jnp.concatenate([jnp.cos(angles), jnp.sin(angles)], axis=1)


def on_device(hidden_in, segments, timestep, w_qkv, w_out, w_up, w_down, w_mod, b_mod, cotangent):
    x, ylo, z, yhi, c = here()
    attn_loc = jnp.concatenate([jnp.swapaxes(w_qkv, 1, 2), w_out], axis=1).reshape((2,) + ATTN)
    up_loc = w_up.reshape(2, 2, 4, 3, 32, D)
    down_loc = w_down.reshape(2, 2, 4, 3, 32, D)

    mine = lax.dynamic_slice_in_dim(timestep, yhi, 1, 0)
    features = time_features(mine, w_mod.shape[1])
    modulation = jnp.einsum(
        "rf,lfm->lrm", features, w_mod.astype(F32), precision=highest
    ) + b_mod.astype(F32)[:, None, :]
    modulation = modulation.reshape(2, 6, D)
    mods = (modulation[0], modulation[1])
    seg = lax.dynamic_slice_in_dim(segments, yhi, 1, 0)
    segc, segr = seg.reshape(SEQ, 1), seg
    cosine, sine = (jnp.asarray(v) for v in rotary(SEQ))
    place = (2 * z + c) * TOK
    cos_here = lax.dynamic_slice_in_dim(cosine, place, TOK, 0)
    sin_here = lax.dynamic_slice_in_dim(sine, place, TOK, 0)

    shared = (segc, segr, cos_here, sin_here)
    y0, *rest = forward(
        0,
        hidden_in.reshape(2, 2, TOK, D),
        cotangent.reshape(2, 2, TOK, D),
        mods[0],
        *shared,
        attn_loc,
        up_loc,
        down_loc,
    )
    kept0, (x0, cots, wa0, wm0, wa1) = rest[:7], rest[7:]
    y1, *rest = forward(1, y0, mods[1], *shared, wa1, up_loc, down_loc)
    kept1, (wm1,) = rest[:7], rest[7:]
    y2, *kept2 = forward(2, x0, y1, mods[0], *shared, wa0, wm0)
    y3, *kept3 = forward(3, y2, mods[1], *shared, wa1, wm1)

    def pairs(one, two):
        return [item for pair in zip(one, two) for item in pair]

    tables = (segc, segr, cosine, sine)
    din1, dinb1, dm1, g1 = backward(1, y0, y2, cots, mods[1], *tables, *pairs(kept1, kept3), wa1, wm1)
    din0, dinb0, dm0, g0, fin1 = backward(
        0, x0, x0, y1, cots, din1, mods[0], *tables, *pairs(kept0, kept2), wa0, wm0, g1
    )
    out0, out1, y_out, g_out, rows = finish(g0, fin1, dm0, dm1, features, y0, y1, y2, y3, dinb0, dinb1)
    grad_mod, grad_bias = modulation_grads(rows)

    out = jnp.stack([out0, out1])
    attn = out[:, :, :, :, 0:16].reshape(2, D, D)
    mlp = out[:, :, :, :, 16:48].reshape(2, 2 * D, D)
    return (
        y_out.reshape(1, 2, 2 * TOK, D),
        g_out.reshape(1, 2, 2 * TOK, D).astype(F32),
        attn[:, 0:576].swapaxes(1, 2).astype(F32),
        attn[:, 576:768].astype(F32),
        mlp[:, 0:768].astype(F32),
        mlp[:, 768:1536].astype(F32),
        grad_mod,
        grad_bias,
    )


def solution(mesh):
    placed = (
        P("dp", "tensor", None),
        P("dp", None),
        P("dp"),
        P(None, None, "tensor"),
        P(None, "tensor", None),
        P(None, None, "tensor"),
        P(None, "tensor", None),
        P(),
        P(),
        P("section", "dp", "tensor", None),
    )
    return jax.shard_map(
        on_device,
        mesh=mesh,
        in_specs=placed,
        out_specs=(
            P("section", "dp", "tensor", None),
            P("section", "dp", "tensor", None),
            P(None, None, "tensor"),
            P(None, "tensor", None),
            P(None, None, "tensor"),
            P(None, "tensor", None),
            P(),
            P(),
        ),
        check_vma=False,
    )
```

```python
import functools

import jax
import jax.numpy as jnp
import numpy as np
from jax import lax
from jax.experimental import pallas as pl
from jax.experimental.pallas import tpu as pltpu
from jax.sharding import PartitionSpec as P

MESH = pl.DeviceIdType.MESH
BF = jnp.bfloat16
F32 = jnp.float32
highest = lax.Precision.HIGHEST
EPS = 1e-06
D = 768
TOK = 128
SEQ = 1024
ANY = pl.BlockSpec(memory_space=pl.ANY)
VM = pl.BlockSpec(memory_space=pltpu.VMEM)
HALF = 384
ATTN = (4, 4, 3, 16, D)
MLP = (4, 4, 2, 48, D)


def here():
    dp = lax.axis_index("dp")
    t = lax.axis_index("tensor")
    return dp // 2, dp % 2, lax.axis_index("section"), t // 2, t % 2


def dev(x, ylo, z, yhi, c):
    return (2 * x + ylo, z, 2 * yhi + c)


def push(src, dst, send_sem, recv_sem, where):
    return pltpu.make_async_remote_copy(
        src_ref=src,
        dst_ref=dst,
        send_sem=send_sem,
        recv_sem=recv_sem,
        device_id=where,
        device_id_type=MESH,
    )


def greet(devices):
    barrier = pltpu.get_barrier_semaphore()
    for where in devices:
        pl.semaphore_signal(barrier, inc=1, device_id=where, device_id_type=MESH)
    return lambda: pl.semaphore_wait(barrier, len(devices))


def nn(a, b):
    return lax.dot_general(a, b, (((1,), (0,)), ((), ())), preferred_element_type=F32)


def nt(a, b):
    return lax.dot_general(a, b, (((1,), (1,)), ((), ())), preferred_element_type=F32)


def tn(a, b):
    return lax.dot_general(a, b, (((0,), (0,)), ((), ())), preferred_element_type=F32)


def normalize(values):
    centred = values - jnp.mean(values, axis=-1, keepdims=True)
    inverse = lax.rsqrt(jnp.mean(centred * centred, axis=-1, keepdims=True) + EPS)
    return centred * inverse, inverse


def norm_back(gradient, normed, inverse):
    return inverse * (
        gradient
        - jnp.mean(gradient, axis=-1, keepdims=True)
        - normed * jnp.mean(gradient * normed, axis=-1, keepdims=True)
    )


def lanes(shape):
    return lax.broadcasted_iota(jnp.int32, shape, len(shape) - 1)


def swap(x):
    return pltpu.roll(x, 64, 1)


def turn(x, cosine, sine):
    low = (lanes(x.shape) % 64) < 32
    other = jnp.where(low, pltpu.roll(x, 96, 1), pltpu.roll(x, 32, 1))
    return x * cosine + other * sine


def half(ylo):
    return pl.ds(pl.multiple_of(HALF * ylo, 128), HALF)


class Spread:
    def __init__(self, buf, orders, ss, rs):
        self.buf, self.orders, self.ss, self.rs = buf, orders, ss, rs
        self.running = None

    def at(self, dims, part, by):
        x, ylo, z, yhi, c = here()
        everything = slice(None)
        i = everything if "x" in dims else by.get("x", x)
        j = everything if "z" in dims else by.get("z", z)
        k = everything if "y" in dims else half(by.get("y", ylo))
        return self.buf.at[i, j, part, :, k]

    def peer(self, dim, o):
        x, ylo, z, yhi, c = here()
        if dim == "y":
            return dev(x, 1 - ylo, z, yhi, c), 1 - ylo
        if dim == "x":
            return dev((x + o) % 4, ylo, z, yhi, c), (x - o + 4) % 4
        return dev(x, ylo, (z + o) % 4, yhi, c), (z - o + 4) % 4

    def start(self, phase):
        sent, got = [], []
        for part in range(len(self.orders)):
            dim, done = self.orders[part][phase], self.orders[part][:phase]
            for o in (1,) if dim == "y" else (2, 1, 3):
                where, origin = self.peer(dim, o)
                n = (phase * 3 + part) * 3 + o - 1
                here_now = self.at(done, part, {})
                cp = push(here_now, here_now, self.ss.at[n], self.rs.at[n], where)
                cp.start()
                sent.append(cp)
                back = self.at(done, part, {dim: origin})
                got.append((push(back, back, self.ss.at[n], self.rs.at[n], where), back))
        self.running = sent, got

    def finish(self, each=None):
        sent, got = self.running
        for cp, back in got:
            cp.wait_recv()
            if each is not None:
                each(back)
        for cp in sent:
            cp.wait_send()

    def held(self):
        return [self.at(self.orders[p][:2], p, {}) for p in range(len(self.orders))]


class Gather:
    def __init__(self, wv, pieces, orders, ss, rs, ps, pr, ls):
        x, ylo, z, yhi, c = here()
        self.wv, self.pieces = wv, pieces
        self.ps, self.pr, self.ls = ps, pr, ls
        self.t = 2 * yhi + c
        self.other = 2 * (1 - yhi) + c
        self.partner = dev(x, ylo, z, yhi, 1 - c)
        self.cross = dev(x, 1 - ylo, z, 1 - yhi, c)
        self.spread = Spread(wv.at[self.other], orders, ss, rs)
        self.handed = []

    def side(self, n):
        ref, first = self.pieces[n]
        spot = self.wv.at[self.t, pl.ds(first, ref.shape[0])]
        return (
            pltpu.make_async_copy(ref, spot, self.ls.at[n]),
            push(ref, spot, self.ps.at[n], self.pr.at[n], self.partner),
        )

    def s0(self):
        x, ylo, z, yhi, c = here()
        for ref, first in self.pieces:

            @pl.when((x >= first) & (x < first + ref.shape[0]))
            def _(ref=ref, first=first):
                push(
                    ref.at[x - first, z, :, :, half(1 - ylo)],
                    self.wv.at[self.t, x, z, :, :, half(1 - ylo)],
                    self.ps.at[2],
                    self.pr.at[2],
                    self.cross,
                ).start()

        for n in range(len(self.pieces)):
            for cp in self.side(n):
                cp.start()

    def s1(self):
        x, ylo, z, yhi, c = here()
        landed = self.wv.at[self.other, x, z, :, :, half(ylo)]
        cp = push(landed, landed, self.ps.at[2], self.pr.at[2], self.cross)
        cp.wait_recv()
        cp.wait_send()
        self.spread.start(0)

    def s2(self):
        self.spread.finish()
        self.spread.start(1)

    def hand(self, ref):
        n = 3 + len(self.handed)
        cp = push(ref, ref, self.ps.at[n], self.pr.at[n], self.partner)
        cp.start()
        self.handed.append(cp)

    def s3(self):
        self.spread.finish()
        self.spread.start(2)
        for ref in self.spread.held():
            self.hand(ref)

    def s4(self):
        self.spread.finish(self.hand)

    def s5(self):
        for n in range(len(self.pieces)):
            local, cp = self.side(n)
            local.wait()
            cp.wait_send()
            cp.wait_recv()
        for cp in self.handed:
            cp.wait_send()
            cp.wait_recv()


def gather_scratch():
    dma = pltpu.SemaphoreType.DMA
    return [dma((27,)), dma((27,)), dma((13,)), dma((13,)), dma((2,))]


def chips_around():
    x, ylo, z, yhi, c = here()
    return [dev((x + o) % 4, ylo, z, yhi, c) for o in (1, 2, 3)] + [
        dev(x, 1 - ylo, z, yhi, c),
        dev(x, 1 - ylo, z, 1 - yhi, c),
    ]


def dp_group():
    x, ylo, z, yhi, c = here()
    t = 2 * yhi + c
    return [(2 * x + ylo, (z + a) % 4, (t + b) % 4) for a in range(4) for b in range(4) if a or b]


def row_places():
    x, ylo, z, yhi, c = here()
    return [(2 * a + b, dev(x, ylo, a, yhi, b)) for a in range(4) for b in range(2)], 2 * z + c


def row_mates():
    x, ylo, z, yhi, c = here()
    me = 2 * z + c
    return [dev(x, ylo, ((me + o) % 8) // 2, yhi, (me + o) % 2) for o in range(1, 8)]


def deal(j, where, me, src, dst, s, r):
    @pl.when(me != j)
    def _():
        push(src, dst, s(j), r(me), where).start()

    @pl.when(me == j)
    def _():
        dst[...] = src[...]


def dealt(j, where, me, src, dst, s, r):
    @pl.when(me != j)
    def _():
        cp = push(src, dst, s(j), r(j), where)
        cp.wait_send()
        cp.wait_recv()


def place_of(sem):
    return lambda j: sem.at[j]


def attn_rows(wa, t, low, high):
    first, last = low // 192, -(-high // 192)
    whole = wa[t, first:last].reshape(192 * (last - first), D)
    return whole[low - 192 * first : high - 192 * first]


def up_rows(wt):
    return wt[0:2].reshape(D, D)


def down_rows(wt):
    return wt[2:4].reshape(D, D)


class Tokens:
    def __init__(self, hid, x0, hs, hr, ls):
        self.refs = hid, x0, hs, hr, ls

    def start(self):
        hid, x0, hs, hr, ls = self.refs
        x, ylo, z, yhi, c = here()
        t = 2 * yhi + c
        for b in range(4):

            @pl.when((t == z) & (t != b))
            def _(b=b):
                push(hid.at[b // 2, b % 2], x0, hs.at[b], hr.at[0], (2 * x + ylo, z, b)).start()

            @pl.when((t == z) & (t == b))
            def _(b=b):
                pltpu.make_async_copy(hid.at[b // 2, b % 2], x0, ls.at[0]).start()

    def arrive(self):
        hid, x0, hs, hr, ls = self.refs
        x, ylo, z, yhi, c = here()
        t = 2 * yhi + c

        @pl.when(t != z)
        def _():
            push(x0, x0, hs.at[0], hr.at[0], (2 * x + ylo, z, (t + 1) % 4)).wait_recv()

        @pl.when(t == z)
        def _():
            pltpu.make_async_copy(hid.at[0, 0], x0, ls.at[0]).wait()

    def sent(self):
        hid, x0, hs, hr, ls = self.refs
        x, ylo, z, yhi, c = here()
        t = 2 * yhi + c
        for b in range(4):

            @pl.when((t == z) & (t != b))
            def _(b=b):
                push(hid.at[b // 2, b % 2], x0, hs.at[b], hr.at[0], (2 * x + ylo, z, b)).wait_send()


class Cotangents:
    def __init__(self, cot, cots, over, cs, cr, ls):
        self.refs = cot, cots, over, cs, cr, ls

    def load(self, begin):
        cot, cots, over, cs, cr, ls = self.refs
        x, ylo, z, yhi, c = here()

        @pl.when(2 * yhi + c == z)
        def _():
            cp = pltpu.make_async_copy(cot.at[yhi, c], over, ls.at[0])
            if begin:
                cp.start()
            else:
                cp.wait()

    def move(self, step, begin):
        cot, cots, over, cs, cr, ls = self.refs
        x, ylo, z, yhi, c = here()
        t = 2 * yhi + c
        dp = 2 * x + ylo
        b = (step + z) % 4

        @pl.when((t != z) | (t != b))
        def _():
            cp = push(cot.at[b // 2, b % 2], cots.at[z], cs.at[step], cr.at[z], (dp, t, b))
            if begin:
                cp.start()
            else:
                cp.wait_send()

        @pl.when((t == z) & (t == b))
        def _():
            cp = pltpu.make_async_copy(over, cots.at[z], ls.at[1])
            if begin:
                cp.start()
            else:
                cp.wait()

        if not begin:

            @pl.when((t != z) | (z != step))
            def _():
                spot = cots.at[step]
                push(spot, spot, cs.at[step], cr.at[step], (dp, z, (t + 1) % 4)).wait_recv()


class Scatter:
    def __init__(self, dst, s_sem, r_sem):
        self.dst, self.s_sem, self.r_sem = dst, s_sem, r_sem

    def send(self, s, src, begin):
        x, ylo, z, yhi, c = here()
        t = 2 * yhi + c
        mine = (z == s) & (t == z)

        @pl.when(jnp.logical_not(mine))
        def _():
            where = (2 * x + ylo, s, z)
            cp = push(src, self.dst.at[yhi, c], self.s_sem.at[s], self.r_sem.at[t], where)
            if begin:
                cp.start()
            else:
                cp.wait_send()

        @pl.when(mine)
        def _():
            cp = pltpu.make_async_copy(src, self.dst.at[yhi, c], self.s_sem.at[s])
            if begin:
                cp.start()
            else:
                cp.wait()

    def received(self, s):
        x, ylo, z, yhi, c = here()
        t = 2 * yhi + c
        for b in range(4):

            @pl.when((z == s) & ((t != b) | (t != z)))
            def _(b=b):
                spot = self.dst.at[b // 2, b % 2]
                where = (2 * x + ylo, z, (t + 1) % 4)
                push(spot, spot, self.s_sem.at[b], self.r_sem.at[b], where).wait_recv()


STATE = ("y", "qkv", "lse", "att", "ba", "mid", "pre", "bb")


def state_shapes():
    return (
        ((TOK, D), BF),
        ((8, TOK, 384), BF),
        ((4, 8, 384), F32),
        ((TOK, 1024), BF),
        ((TOK, D), F32),
        ((TOK, D), F32),
        ((TOK, 4 * D), F32),
        ((TOK, D), F32),
    )


def forward_kernel(*refs):
    refs = list(refs)

    def take(count):
        got = refs[:count]
        del refs[:count]
        return got

    hid, cot, mods, segc, segr, cosine, sine, attn_loc, up_loc, down_loc = take(10)
    outs = dict(zip(STATE, take(8)))
    x0, cots, *weights_out = take(6)
    held = dict(zip(STATE, take(8)))
    sbuf, obuf, rbuf, wa0, wa1, wm0, wm1 = take(7)
    wsem, ksem, ss, rs, ss2, rs2 = take(6)
    x, ylo, z, yhi, c = here()
    places, me = row_places()
    saved = []

    def save(src, dst):
        cp = pltpu.make_async_copy(src, dst, wsem.at[len(saved)])
        cp.start()
        saved.append(cp)

    beside = ("zyx", "zxy")
    a0 = Gather(wa0, [(attn_loc.at[0], 0)], ("zyx", "xzy", "yxz"), *take(5))
    m0 = Gather(wm0, [(up_loc.at[0], 0), (down_loc.at[0], 2)], beside, *take(5))
    a1 = Gather(wa1, [(attn_loc.at[1], 0)], ("zyx", "zxy", "zyx"), *take(5))
    m1 = Gather(wm1, [(up_loc.at[1], 0), (down_loc.at[1], 2)], beside, *take(5))
    tokens = Tokens(hid, x0, *take(3))
    cotangents = Cotangents(cot, cots, *take(4))
    greet(dp_group() + chips_around())()
    a0.s0()
    tokens.start()
    cotangents.load(True)
    a0.s1()
    m0.s0()
    a0.s2()
    m0.s1()
    a0.s3()
    tokens.arrive()

    cos_here, sin_here = cosine[...], sine[...]
    low = lanes((TOK, 128)) < 64
    seg_keys = segr[...]

    def flat(column):
        wide = jnp.broadcast_to(column, (column.shape[0], 128))
        return jnp.transpose(wide)[0:8, :]

    def keeping(app):
        slot = app % 2
        return [
            pltpu.make_async_copy(held[name].at[slot], outs[name].at[app], ksem.at[slot, n])
            for n, name in enumerate(STATE)
        ]

    for app in range(4):
        slot = app % 2
        wa, wm = ((wa0, wm0), (wa1, wm1))[slot]
        mod = mods.at[slot]
        qkv, lse, att, ba, mid, pre, bb = (held[name].at[slot] for name in STATE[1:])
        if app == 0:
            v = x0[...].astype(F32)
        else:
            v = held["y"][1 - slot].astype(F32)
            if app == 2:
                v = v + x0[...].astype(F32)
        hat, _ = normalize(v)
        normed = (hat * (1.0 + mod[1:2, :]) + mod[0:1, :]).astype(BF)
        if app == 0:
            a0.s4()
            m0.s2()
            a0.s5()
            save(wa0, weights_out[0])
        if app == 1:
            a1.s5()
            save(wa1, weights_out[2])
        for t in range(4):
            got = nt(normed, attn_rows(wa, t, 0, 640))
            t0, t1, t2, t3, t4 = (got[:, 128 * i : 128 * (i + 1)] for i in range(5))
            s0, s1, s2, s3, s4 = (swap(u) for u in (t0, t1, t2, t3, t4))
            for head, (q, k, w) in enumerate(
                (
                    (jnp.where(low, t0, s3), jnp.where(low, s0, t3), jnp.where(low, t1, s4)),
                    (jnp.where(low, s1, s3), jnp.where(low, t2, t3), jnp.where(low, s2, s4)),
                )
            ):
                j = 2 * t + head
                sbuf[j, :, 0:128] = (turn(q, cos_here, sin_here).astype(BF).astype(F32) * 0.125).astype(BF)
                sbuf[j, :, 128:256] = turn(k, cos_here, sin_here).astype(BF)
                sbuf[j, :, 256:384] = w.astype(BF)
                deal(j, places[j][1], me, sbuf.at[j], qkv.at[me], place_of(ss.at[app]), place_of(rs.at[app]))
        if app == 0:
            m0.s3()
            a1.s0()
            m1.s0()
        if app == 1:
            m1.s3()
        for j, where in places:
            dealt(j, where, me, sbuf.at[j], qkv.at[j], place_of(ss.at[app]), place_of(rs.at[app]))
        if app:
            for cp in keeping(app - 1):
                cp.wait()

        keys = qkv[:, :, 128:256].reshape(SEQ, 128)
        values = qkv[:, :, 256:384].reshape(SEQ, 128)

        def softmax(q, seg_q, keys=keys, values=values):
            scores = jnp.where(seg_q == seg_keys, nt(q, keys), -1e30)
            largest = jnp.max(scores, axis=-1, keepdims=True)
            raised = jnp.exp(scores - largest)
            total = jnp.sum(raised, axis=-1, keepdims=True)
            mixed = nn(raised.astype(BF), values) * (1.0 / total)
            return mixed, largest + jnp.log(total)

        for a in range(4):
            if app == 0 and a == 0:
                a1.s1()
            if app == 0 and a == 2:
                a1.s2()
            q = qkv[2 * a : 2 * a + 2, :, 0:128].reshape(256, 128)
            q = jnp.where(lanes((256, 128)) < 64, q, 0).astype(BF)
            mixed, total = softmax(q, segc[256 * a : 256 * (a + 1), :])
            q2 = jnp.where(low, 0, qkv[2 * a + c, :, 0:128]).astype(BF)
            mixed2, total2 = softmax(q2, segc[pl.ds(256 * a + TOK * c, TOK), :])
            lse[a, :, 0:256] = flat(total)
            lse[a, :, 256:384] = flat(total2)
            for b in range(2):
                j = 2 * a + b
                part = mixed[TOK * b : TOK * (b + 1)]
                obuf[j] = jnp.where(low | (c != b), part, mixed2).astype(BF)
                deal(j, places[j][1], me, obuf.at[j], rbuf.at[me], place_of(ss2.at[app]), place_of(rs2.at[app]))
        if app == 0:
            a1.s3()
            m0.s4()
        if app == 1:
            m1.s4()
        for j, where in places:
            dealt(j, where, me, obuf.at[j], rbuf.at[j], place_of(ss2.at[app]), place_of(rs2.at[app]))

        if app == 0:
            cotangents.load(False)
        cotangents.move(app, True)
        branch_a = jnp.zeros((TOK, D), F32)
        for t in range(4):
            first, second = rbuf[2 * t], rbuf[2 * t + 1]
            own = jnp.where(low, first.astype(F32), swap(second.astype(F32))).astype(BF)
            extra = jnp.where(low, 0, rbuf[2 * t + c]).astype(BF)
            att[:, 128 * t : 128 * (t + 1)] = own
            att[:, 512 + 128 * t : 512 + 128 * (t + 1)] = extra
            branch_a = branch_a + nn(own, attn_rows(wa, t, 576, 704)) + nn(extra, attn_rows(wa, t, 640, 768))
        ba[...] = branch_a
        middle = v + mod[2:3, :] * branch_a
        mid[...] = middle
        hat_b, _ = normalize(middle)
        normed_b = (hat_b * (1.0 + mod[4:5, :]) + mod[3:4, :]).astype(BF)
        if app == 0:
            m0.s5()
            save(wm0, weights_out[1])
            m1.s1()
        if app == 1:
            m1.s5()
            save(wm1, weights_out[3])
        total_b = jnp.zeros((TOK, D), F32)
        for t in range(4):
            before = nn(normed_b, up_rows(wm.at[t]))
            pre[:, D * t : D * (t + 1)] = before
            total_b = total_b + nn(jax.nn.gelu(before, approximate=True).astype(BF), down_rows(wm.at[t]))
        bb[...] = total_b
        held["y"][slot] = (middle + mod[5:6, :] * total_b).astype(BF)
        for cp in keeping(app):
            cp.start()
        if app == 0:
            m1.s2()
            a1.s4()
    for b in range(4):
        cotangents.move(b, False)
    tokens.sent()
    for cp in keeping(3) + saved:
        cp.wait()


def forward(*operands):
    dma = pltpu.SemaphoreType.DMA
    outs = [jax.ShapeDtypeStruct((4,) + dims, dtype) for dims, dtype in state_shapes()]
    outs += [jax.ShapeDtypeStruct(dims, BF) for dims in ((TOK, D), (4, TOK, D))]
    outs += [jax.ShapeDtypeStruct((4,) + group, BF) for group in (ATTN, MLP, ATTN, MLP)]
    scratch = [pltpu.VMEM((2,) + dims, dtype) for dims, dtype in state_shapes()]
    scratch += [
        pltpu.VMEM((8, TOK, 384), BF),
        pltpu.VMEM((8, TOK, 128), BF),
        pltpu.VMEM((8, TOK, 128), BF),
    ]
    scratch += [pltpu.VMEM((4,) + group, BF) for group in (ATTN, ATTN, MLP, MLP)]
    scratch += [dma((4,)), dma((2, 8))] + [dma((4, 8))] * 4
    for _ in range(4):
        scratch += gather_scratch()
    scratch += [dma((4,)), dma((1,)), dma((1,))]
    scratch += [pltpu.VMEM((TOK, D), BF), dma((4,)), dma((4,)), dma((2,))]
    return pl.pallas_call(
        forward_kernel,
        out_shape=tuple(outs),
        in_specs=[ANY] * 2 + [VM] * 5 + [ANY] * 3,
        out_specs=tuple([ANY] * 8 + [VM] + [ANY] * 5),
        scratch_shapes=scratch,
        compiler_params=pltpu.CompilerParams(
            collective_id=1, has_side_effects=True, vmem_limit_bytes=62 * 2**20
        ),
        name="forward",
    )(*operands)


def across(dim, o):
    x, ylo, z, yhi, c = here()
    if dim == "x":
        to = (x + o) % 4
        return dev(to, ylo, z, yhi, c), to
    if dim == "z":
        to = (z + o) % 4
        return dev(x, ylo, to, yhi, c), to
    to = (2 * yhi + ylo + o) % 4
    return dev(x, to % 2, z, to // 2, c), to


def own_place(dim):
    x, ylo, z, yhi, c = here()
    return {"x": x, "z": z, "y": 2 * yhi + ylo}[dim]


def reduce_greeted():
    return [across(dim, o)[0] for dim in "xy" for o in (1, 2, 3)]


def left(order, steps):
    return [label for label in "Yxz" if label.lower() not in order[:steps]]


def block(order, steps, rows):
    sizes = {"Y": 2, "x": 4, "z": 4}
    lane_count = HALF if "y" in order[:steps] else D
    return tuple(sizes[label] for label in left(order, steps)) + (rows, lane_count)


def pick(labels, dim, to):
    index = [slice(None)] * len(labels)
    if dim == "y":
        index[labels.index("Y")] = to // 2
        return tuple(index), half(to % 2)
    index[labels.index(dim)] = to
    return tuple(index), slice(None)


def each_unit(dims, body):
    count = 1
    for size in dims:
        count *= size

    def step(i, carry):
        index, rest = [], i
        for size in reversed(dims):
            index.append(rest % size)
            rest = rest // size
        body(tuple(reversed(index)))
        return carry

    lax.fori_loop(0, count, step, 0)


class ReduceFirst:
    def __init__(self, grads, orders, own, arrived, ls, ss, rs):
        self.grads, self.orders, self.own, self.arrived = grads, orders, own, arrived
        self.ls, self.ss, self.rs = ls, ss, rs

    def source(self, p, to):
        index, cols = pick(["Y", "x", "z"], self.orders[p][0], to)
        return self.grads.at[index + (p, slice(None), cols)]

    def copies(self):
        found = []
        if self.ls is not None:
            for p, order in enumerate(self.orders):
                found.append(pltpu.make_async_copy(self.source(p, own_place(order[0])), self.own[p], self.ls.at[p]))
        for o in (2, 1, 3):
            for p, order in enumerate(self.orders):
                where, to = across(order[0], o)
                n = 3 * p + o - 1
                found.append(push(self.source(p, to), self.arrived[p].at[o - 1], self.ss.at[n], self.rs.at[n], where))
        return found

    def begin(self):
        for cp in self.copies():
            cp.start()

    def sum(self):
        for cp in self.copies():
            cp.wait()
        for p in range(len(self.orders)):
            own, arrived = self.own[p], self.arrived[p]
            mine = own if self.ls is not None else self.source(p, own_place(self.orders[p][0]))

            def body(index, own=own, arrived=arrived, mine=mine):
                total = mine[index].astype(F32)
                for n in range(3):
                    total = total + arrived[(n,) + index].astype(F32)
                own[index] = total.astype(BF)

            each_unit(own.shape[:-2], body)

    @staticmethod
    def shapes(orders, rows):
        return [block(order, 1, rows) for order in orders]

    @staticmethod
    def scratch(orders, rows):
        dma = pltpu.SemaphoreType.DMA
        arrived = [pltpu.VMEM((3,) + dims, BF) for dims in ReduceFirst.shapes(orders, rows)]
        return arrived + [dma((3,)), dma((9,)), dma((9,))]


class ReduceRest:
    def __init__(self, orders, own, refs):
        refs = list(refs)
        count = len(orders)
        self.orders, self.own = orders, own
        self.mid, self.tot, self.end = refs[:count], refs[count : 2 * count], refs[2 * count : 3 * count]
        self.ss2, self.rs2, self.ss3, self.rs3 = refs[3 * count :]

    @staticmethod
    def scratch(orders, rows):
        dma = pltpu.SemaphoreType.DMA
        shapes = [pltpu.VMEM((3,) + block(order, 2, rows), BF) for order in orders]
        shapes += [pltpu.VMEM(block(order, 2, rows), BF) for order in orders]
        shapes += [pltpu.VMEM((3,) + block(order, 3, rows), BF) for order in orders]
        return shapes + [dma((9,))] * 4

    @staticmethod
    def count(orders):
        return 3 * len(orders) + 4

    def copies(self, step):
        found = []
        sources, targets = (self.own, self.mid) if step == 1 else (self.tot, self.end)
        send, recv = (self.ss2, self.rs2) if step == 1 else (self.ss3, self.rs3)
        for o in (2, 1, 3):
            for p, order in enumerate(self.orders):
                where, to = across(order[step], o)
                index, cols = pick(left(order, step), order[step], to)
                n = 3 * p + o - 1
                found.append(
                    push(sources[p].at[index + (slice(None), cols)], targets[p].at[o - 1], send.at[n], recv.at[n], where)
                )
        return found

    def begin(self):
        for cp in self.copies(1):
            cp.start()

    def sum_second(self):
        for cp in self.copies(1):
            cp.wait()
        for p, order in enumerate(self.orders):
            own, mid, tot = self.own[p], self.mid[p], self.tot[p]
            labels = left(order, 1)
            index, cols = pick(labels, order[1], own_place(order[1]))
            free = [n for n, value in enumerate(index) if isinstance(value, slice)]
            for i in range(tot.shape[0]):
                spot = list(index)
                spot[free[0]] = i
                total = own[tuple(spot) + (slice(None), cols)].astype(F32)
                for n in range(3):
                    total = total + mid[n, i].astype(F32)
                tot[i] = total.astype(BF)
        for cp in self.copies(2):
            cp.start()

    def sum_third(self, fin):
        for cp in self.copies(2):
            cp.wait()
        for p, order in enumerate(self.orders):
            index, cols = pick(left(order, 2), order[2], own_place(order[2]))
            total = self.tot[p][index + (slice(None), cols)].astype(F32)
            for n in range(3):
                total = total + self.end[p][n].astype(F32)
            fin[p] = total.astype(BF)


MLP_SUM = ("xyz", "yxz")
ATTN_SUM = ("xyz", "yzx", "zxy")
MLP_ROWS, ATTN_ROWS = 48, 16


def gelu_parts(u):
    k = 0.7978845608028654
    square = u * u
    th = jnp.tanh(k * u * (1.0 + 0.044715 * square))
    half_up = 0.5 * (1.0 + th)
    slope = half_up + 0.5 * u * (1.0 - th * th) * (k * (1.0 + 0.134145 * square))
    return u * half_up, slope


def backward_kernel(layer, *refs):
    refs = list(refs)

    def take(count):
        got = refs[:count]
        del refs[:count]
        return got

    mods, segc, segr = take(3)
    more_dy, prior, *last_shares = take(4) if layer == 0 else [None, None]
    cosine_in, sine_in, x0_in, cots_in = take(4)
    outer = dict(zip(STATE, take(8)))
    wa_in, wm_in = take(2)
    before = take(1)[0] if layer == 0 else None
    din, dinb, dmod, grads, *shares = take(6)
    (spread_out,) = take(1)
    if layer == 0:
        fin_attn, fin_mlp = take(2)
    held = dict(zip(STATE, take(8)))
    cosine, sine, x0, cots, lsem = take(5)
    mod = mods.at[layer]
    own_na, own_nb, own_dba, own_dbb, own_act, own_dpre, own_dpj = take(7)
    got_na, got_nb, got_dba, got_dbb, got_at, got_act, got_dpre, got_dpj = take(8)
    sbuf, rbuf, sbig, rbig, dmid, dnb, k_own, k_sh, v_own, v_sh = take(10)
    wa, wm, mlp_grads, stage_attn = take(4)
    wsem, gsem, ss, rs, ss2, rs2, xs, xr = take(8)
    mlp_first = ReduceFirst(mlp_grads, MLP_SUM, shares, take(2), None, *take(3)[1:])
    rows_of = [slice(TOK * e, TOK * (e + 1)) for e in range(2)]
    x, ylo, z, yhi, c = here()
    places, me = row_places()
    partner = dev(x, ylo, z, yhi, 1 - c)
    scattered = Scatter(spread_out, *take(2))
    if layer == 1:
        (ys,) = take(1)
    if layer == 0:
        mlp_rest = ReduceRest(MLP_SUM, last_shares, take(ReduceRest.count(MLP_SUM)))
        attn_first = ReduceFirst(before, ATTN_SUM, take(3), take(3), *take(3))
        attn_rest = ReduceRest(ATTN_SUM, attn_first.own, take(ReduceRest.count(ATTN_SUM)))
    entered = greet(dp_group() + reduce_greeted())
    loads = {}

    def load(name, src, dst):
        cp = pltpu.make_async_copy(src, dst, lsem.at[len(loads)])
        cp.start()
        loads[name] = cp

    def loaded(*names):
        for name in names:
            loads[name].wait()

    def load_state(name):
        for e in range(2):
            load((name, e), outer[name].at[layer + 2 * e], held[name].at[e])

    def state(name):
        loaded((name, 0), (name, 1))

    for e in range(2):
        load(("cots", e), cots_in.at[layer + 2 * e], cots.at[e])
    load_state("mid")
    load_state("bb")
    if layer == 0:
        load("x0", x0_in, x0)
        load(("y", 1), outer["y"].at[1], held["y"].at[1])
    else:
        load("y", outer["y"], ys)
    load_state("att")

    def wm_fetch(t):
        return pltpu.make_async_copy(wm_in.at[t], wm.at[t % 2], wsem.at[1 + t])

    wm_fetch(0).start()
    load_state("pre")
    wm_fetch(1).start()
    wa_fetch = pltpu.make_async_copy(wa_in, wa, wsem.at[0])
    wa_fetch.start()
    for name in ("ba", "qkv", "lse"):
        load_state(name)
    load("cosine", cosine_in, cosine)
    load("sine", sine_in, sine)
    qkvs, lses, atts, bas, mids, pres, bbs = ([held[name].at[e] for e in range(2)] for name in STATE[1:])
    scale_a, gate_a = mod[1:2, :], mod[2:3, :]
    scale_b, gate_b = mod[4:5, :], mod[5:6, :]
    low = lanes((TOK, 128)) < 64
    exchanged = {}

    def hand(name, src, dst):
        n = len(exchanged)
        cp = push(src, dst, xs.at[n], xr.at[n], partner)
        cp.start()
        exchanged[name] = cp

    def have(*names):
        for name in names:
            exchanged[name].wait_send()
            exchanged[name].wait_recv()

    def gradient(e):
        dy = cots[e].astype(F32)
        return dy if more_dy is None else dy + more_dy[e]

    def entry(e):
        if layer == 1:
            return ys[2 * e].astype(F32)
        v = x0[...].astype(F32)
        return v + held["y"][1].astype(F32) if e else v

    loaded(("cots", 0), ("cots", 1))
    state("mid")
    state("bb")
    loaded(*(["x0", ("y", 1)] if layer == 0 else ["y"]))
    dgate_b = jnp.zeros((1, D), F32)
    for e in range(2):
        dy = gradient(e)
        dgate_b = dgate_b + jnp.sum(dy * bbs[e][...], axis=0, keepdims=True)
        own_dbb[rows_of[e], :] = (gate_b * dy).astype(BF)
        hat_b, _ = normalize(mids[e][...])
        own_nb[rows_of[e], :] = (hat_b * (1.0 + scale_b) + mod[3:4, :]).astype(BF)
        hat_a, _ = normalize(entry(e))
        own_na[rows_of[e], :] = (hat_a * (1.0 + scale_a) + mod[0:1, :]).astype(BF)
    entered()
    hand("dbb", own_dbb, got_dbb)
    hand("nb", own_nb, got_nb)
    hand("na", own_na, got_na)
    state("att")
    for e in range(2):
        hand(f"at{e}", atts[e], got_at.at[e])
    given = {s: ys.at[s] for s in range(4)} if layer == 1 else {1: prior.at[0], 3: prior.at[1]}
    for s, ref in given.items():
        scattered.send(s, ref, True)
    if layer == 0:
        mlp_rest.begin()
        attn_first.begin()
    state("pre")

    for t in range(4):
        wm_fetch(t).wait()
        d_act = nt(own_dbb[...], down_rows(wm.at[t % 2]))
        for e in range(2):
            act, slope = gelu_parts(pres[e][:, D * t : D * (t + 1)])
            own_act[t, rows_of[e], :] = act.astype(BF)
            own_dpre[t, rows_of[e], :] = (d_act[rows_of[e]] * slope).astype(BF)
        more = nt(own_dpre[t], up_rows(wm.at[t % 2]))
        dnb[...] = more if t == 0 else dnb[...] + more
        if t < 2:
            wm_fetch(t + 2).start()
    for h in range(2):
        hand(f"act{h}", own_act.at[2 * h + 1 - c], got_act.at[h])
        hand(f"dpre{h}", own_dpre.at[2 * h + 1 - c], got_dpre.at[h])

    state("ba")
    dgate_a = jnp.zeros((1, D), F32)
    dscale_b = jnp.zeros((1, D), F32)
    dshift_b = jnp.zeros((1, D), F32)
    for e in range(2):
        hat_b, inv_b = normalize(mids[e][...])
        g = dnb[rows_of[e], :]
        dscale_b = dscale_b + jnp.sum(g * hat_b, axis=0, keepdims=True)
        dshift_b = dshift_b + jnp.sum(g, axis=0, keepdims=True)
        d_middle = gradient(e) + norm_back(g * (1.0 + scale_b), hat_b, inv_b)
        dmid[rows_of[e], :] = d_middle
        dgate_a = dgate_a + jnp.sum(d_middle * bas[e][...], axis=0, keepdims=True)
        own_dba[rows_of[e], :] = (gate_a * d_middle).astype(BF)
    hand("dba", own_dba, got_dba)
    wa_fetch.wait()
    for t in range(4):
        first = nt(own_dba[...], attn_rows(wa, t, 576, 704))
        second = nt(own_dba[...], attn_rows(wa, t, 640, 768))
        for e in range(2):
            sbuf[2 * t, e] = jnp.where(low, first[rows_of[e]], second[rows_of[e]]).astype(BF)
            sbuf[2 * t + 1, e] = second[rows_of[e]].astype(BF)
        for b in range(2):
            j = 2 * t + b
            deal(j, places[j][1], me, sbuf.at[j], rbuf.at[me], place_of(ss), place_of(rs))

    if layer == 0:
        mlp_rest.sum_second()
        attn_first.sum()
        attn_rest.begin()
    have("dbb", "nb", "act0", "dpre0", "act1", "dpre1")

    for h in range(2):
        t = 2 * h + c
        total = tn(own_nb[...], own_dpre[t]) + tn(got_nb[...], got_dpre[h])
        mlp_grads[h, 0:2] = total.astype(BF).reshape(2, 4, 2, 48, D)
        total = tn(own_act[t], own_dbb[...]) + tn(got_act[h], got_dbb[...])
        mlp_grads[h, 2:4] = total.astype(BF).reshape(2, 4, 2, 48, D)
    mlp_first.begin()
    for j, where in places:
        dealt(j, where, me, sbuf.at[j], rbuf.at[j], place_of(ss), place_of(rs))

    state("qkv")
    state("lse")
    loaded("cosine", "sine")
    seg_keys = segc[...]
    wide = lanes((256, 128)) < 64
    for e in range(2):
        qkv, lse = qkvs[e], lses[e]
        for ref in (k_own, k_sh, v_own, v_sh):
            ref[...] = jnp.zeros_like(ref)

        def one(q, go, seg_q, total, k_sum, v_sum, qkv=qkv):
            keys = qkv[:, :, 128:256].reshape(SEQ, 128)
            values = qkv[:, :, 256:384].reshape(SEQ, 128)
            scores = jnp.where(seg_keys == seg_q, nt(keys, q), -1e30)
            p = jnp.exp(scores - total)
            d_p = nt(values, go)
            centre = jnp.sum(d_p * p, axis=0, keepdims=True)
            d_s = (p * (d_p - centre)).astype(BF)
            v_sum[...] += nn(p.astype(BF), go)
            k_sum[...] += nn(d_s, q)
            return tn(d_s, keys) * 0.125

        for a in range(4):
            q = qkv[2 * a : 2 * a + 2, :, 0:128].reshape(256, 128)
            go = rbuf[2 * a : 2 * a + 2, e].reshape(256, 128)
            dq = one(
                jnp.where(wide, q, 0).astype(BF),
                jnp.where(wide, go, 0).astype(BF),
                segr[0:1, 256 * a : 256 * (a + 1)],
                lse[a, 0:1, 0:256],
                k_own,
                v_own,
            )
            q2 = jnp.where(low, 0, qkv[2 * a + c, :, 0:128]).astype(BF)
            go2 = jnp.where(low, 0, rbuf[2 * a + c, e]).astype(BF)
            seg2 = jnp.where(
                c == 0,
                segr[0:1, 256 * a : 256 * a + 128],
                segr[0:1, 256 * a + 128 : 256 * a + 256],
            )
            dq2 = one(q2, go2, seg2, lse[a, 0:1, 256:384], k_sh, v_sh)
            for b in range(2):
                rows = slice(256 * a + TOK * b, 256 * a + TOK * (b + 1))
                whole = jnp.where(low, dq[TOK * b : TOK * (b + 1)], jnp.where(c == b, dq2, 0.0))
                sbig[2 * a + b, e, :, 0:128] = turn(whole, cosine[rows, :], -sine[rows, :]).astype(BF)
        for j, where in places:
            rows = slice(TOK * j, TOK * (j + 1))
            whole = jnp.where(low, k_own[rows, :], k_sh[rows, :])
            sbig[j, e, :, 128:256] = turn(whole, cosine[rows, :], -sine[rows, :]).astype(BF)
            sbig[j, e, :, 256:384] = jnp.where(low, v_own[rows, :], v_sh[rows, :]).astype(BF)
            deal(
                j, where, me, sbig.at[j, e], rbig.at[me, e],
                lambda i, e=e: ss2.at[e, i], lambda i, e=e: rs2.at[e, i],
            )
        if layer == 0 and e == 0:
            mlp_rest.sum_third(fin_mlp)
            attn_rest.sum_second()
    for e in range(2):
        for j, where in places:
            dealt(
                j, where, me, sbig.at[j, e], rbig.at[j, e],
                lambda i, e=e: ss2.at[e, i], lambda i, e=e: rs2.at[e, i],
            )
        for t in range(4):
            q0, k0, v0 = (rbig[2 * t, e, :, 128 * i : 128 * (i + 1)].astype(F32) for i in range(3))
            q1, k1, v1 = (rbig[2 * t + 1, e, :, 128 * i : 128 * (i + 1)].astype(F32) for i in range(3))
            tiles = (
                jnp.where(low, q0, swap(k0)),
                jnp.where(low, v0, swap(q1)),
                jnp.where(low, k1, swap(v1)),
                jnp.where(low, swap(q0 + q1), k0 + k1),
                jnp.where(low, swap(v0 + v1), 0.0),
            )
            for i, tile in enumerate(tiles):
                own_dpj[t, rows_of[e], 128 * i : 128 * (i + 1)] = tile.astype(BF)
    for h in range(2):
        hand(f"dpj{h}", own_dpj.at[2 * h + 1 - c], got_dpj.at[h])
    dna = jnp.zeros((2 * TOK, D), F32)
    for t in range(4):
        dna = dna + nn(own_dpj[t], attn_rows(wa, t, 0, 640))
    dscale_a = jnp.zeros((1, D), F32)
    dshift_a = jnp.zeros((1, D), F32)
    for e in range(2):
        hat_a, inv_a = normalize(entry(e))
        g = dna[rows_of[e]]
        dscale_a = dscale_a + jnp.sum(g * hat_a, axis=0, keepdims=True)
        dshift_a = dshift_a + jnp.sum(g, axis=0, keepdims=True)
        total = dmid[rows_of[e], :] + norm_back(g * (1.0 + scale_a), hat_a, inv_a)
        din[e] = total
        dinb[e] = total.astype(BF)
    for i, part in enumerate((dshift_a, dscale_a, dgate_a, dshift_b, dscale_b, dgate_b)):
        dmod[i : i + 1, :] = part
    dmod[6:8, :] = jnp.zeros((2, D), F32)

    have("na", "at0", "at1", "dba", "dpj0", "dpj1")
    for h in range(2):
        t = 2 * h + c
        copy = pltpu.make_async_copy(stage_attn, grads.at[h], gsem.at[0])
        if h:
            copy.wait()
        total = tn(own_dpj[t], own_na[...]) + tn(got_dpj[h], got_na[...])
        stage_attn[0:3] = total[0:576].astype(BF).reshape(3, 4, 3, 16, D)
        parts = []
        for first in (0, 512):
            cols = pl.ds(pl.multiple_of(first + 128 * t, 128), 128)
            total = jnp.zeros((128, D), F32)
            for e in range(2):
                total = total + tn(atts[e][:, cols], own_dba[rows_of[e], :])
                total = total + tn(got_at[e, :, cols], got_dba[rows_of[e], :])
            parts.append(total)
        total = jnp.concatenate([parts[0], parts[1][64:128]], axis=0)
        stage_attn[3] = total.astype(BF).reshape(4, 3, 16, D)
        copy.start()
    if layer == 0:
        attn_rest.sum_third(fin_attn)
    mlp_first.sum()
    for s, ref in given.items():
        scattered.send(s, ref, False)
        scattered.received(s)
    pltpu.make_async_copy(stage_attn, grads.at[1], gsem.at[0]).wait()


def backward(layer, *operands):
    dma = pltpu.SemaphoreType.DMA
    both = 2 * TOK

    def buf(*dims, dtype=BF):
        return pltpu.VMEM(dims, dtype)

    outs = [
        jax.ShapeDtypeStruct((2, TOK, D), F32),
        jax.ShapeDtypeStruct((2, TOK, D), BF),
        jax.ShapeDtypeStruct((8, D), F32),
        jax.ShapeDtypeStruct((2,) + ATTN, BF),
    ]
    outs += [jax.ShapeDtypeStruct(dims, BF) for dims in ReduceFirst.shapes(MLP_SUM, MLP_ROWS)]
    outs.append(jax.ShapeDtypeStruct((2, 2, TOK, D), BF))
    out_specs = [VM, VM, VM, ANY, VM, VM, ANY]
    if layer == 0:
        outs += [jax.ShapeDtypeStruct(dims, BF) for dims in ((3, 16, HALF), (2, 48, HALF))]
        out_specs += [VM, VM]
    scratch = [buf(2, *dims, dtype=dtype) for dims, dtype in state_shapes()]
    scratch += [buf(SEQ, 128, dtype=F32)] * 2 + [buf(TOK, D), buf(2, TOK, D), dma((24,))]
    scratch += [buf(both, D)] * 4 + [buf(4, both, D)] * 2 + [buf(4, both, 640)]
    scratch += [buf(both, D)] * 4 + [buf(2, TOK, 1024)] + [buf(2, both, D)] * 2 + [buf(2, both, 640)]
    scratch += [buf(8, 2, TOK, 128)] * 2 + [buf(8, 2, TOK, 384)] * 2
    scratch += [buf(both, D, dtype=F32)] * 2 + [buf(SEQ, 128, dtype=F32)] * 4
    scratch += [buf(4, *ATTN), buf(2, *MLP), buf(2, *MLP), buf(*ATTN)]
    scratch += [dma((5,)), dma((1,)), dma((8,)), dma((8,)), dma((2, 8)), dma((2, 8)), dma((12,)), dma((12,))]
    scratch += ReduceFirst.scratch(MLP_SUM, MLP_ROWS)
    scratch += [dma((4,)), dma((4,))]
    if layer == 1:
        scratch.append(buf(4, TOK, D))
    if layer == 0:
        scratch += ReduceRest.scratch(MLP_SUM, MLP_ROWS)
        scratch += [pltpu.VMEM(dims, BF) for dims in ReduceFirst.shapes(ATTN_SUM, ATTN_ROWS)]
        scratch += ReduceFirst.scratch(ATTN_SUM, ATTN_ROWS)
        scratch += ReduceRest.scratch(ATTN_SUM, ATTN_ROWS)
    vmem_in = 7 if layer == 0 else 3
    return pl.pallas_call(
        functools.partial(backward_kernel, layer),
        out_shape=tuple(outs),
        in_specs=[VM] * vmem_in + [ANY] * (len(operands) - vmem_in),
        out_specs=tuple(out_specs),
        scratch_shapes=scratch,
        compiler_params=pltpu.CompilerParams(
            collective_id=2 + layer, has_side_effects=True, vmem_limit_bytes=62 * 2**20
        ),
        name=f"backward_{layer}",
    )(*operands)


def finish_kernel(*refs):
    refs = list(refs)

    def take(count):
        got = refs[:count]
        del refs[:count]
        return got

    shares = take(2)
    fin_a1, fin_m1, dm0, dm1, feat, db0 = take(6)
    (attn_grads,) = take(1)
    out_a0, out_m0, out_a1, out_m1, g_out, rows_out = take(6)
    fin_a0, fin_m0, dm_in, dsum = take(4)
    mlp_rest = ReduceRest(MLP_SUM, shares, take(ReduceRest.count(MLP_SUM)))
    attn_first = ReduceFirst(attn_grads, ATTN_SUM, take(3), take(3), *take(3))
    attn_rest = ReduceRest(ATTN_SUM, attn_first.own, take(ReduceRest.count(ATTN_SUM)))
    ag_a0 = Spread(out_a0, ("xzy", "xyz", "xzy"), *take(2))
    ag_m0 = Spread(out_m0, ("zyx", "xzy"), *take(2))
    ag_a1 = Spread(out_a1, ("xyz", "xzy", "xyz"), *take(2))
    ag_m1 = Spread(out_m1, ("zyx", "yxz"), *take(2))
    scattered = Scatter(g_out, *take(2))
    ms, mr, ms2, mr2, fsem = take(5)
    x, ylo, z, yhi, c = here()
    dp = 2 * x + ylo
    places, me = row_places()
    row = 2 * dp + yhi
    others = []
    for o in range(1, 16):
        r = (row + o) % 16
        others.append(dev(r // 4, (r // 2) % 2, z, r % 2, c))
    far = []
    for o in range(1, 8):
        g = (dp + o) % 8
        far += [(g, z, 2 * b + c) for b in range(2)]
    greet(dp_group() + far)()

    def place_in(n, fin, out):
        return pltpu.make_async_copy(fin, out.at[x, z, :, :, half(ylo)], fsem.at[n])

    settled = [place_in(0, fin_m1, out_m1), place_in(1, fin_a1, out_a1)]
    for cp in settled:
        cp.start()
    mlp_rest.begin()
    attn_first.begin()
    for cp in settled:
        cp.wait()
    ag_m1.start(0)
    ag_a1.start(0)
    for j, where in places:

        @pl.when(me != j)
        def _(j=j, where=where):
            push(dm0, dm_in.at[me, 0], ms.at[0, j], mr.at[0, me], where).start()
            push(dm1, dm_in.at[me, 1], ms.at[1, j], mr.at[1, me], where).start()

    for e in range(2):
        scattered.send(2 * e, db0.at[e], True)
    mlp_rest.sum_second()
    ag_m1.finish()
    ag_m1.start(1)
    ag_a1.finish()
    ag_a1.start(1)

    for j, where in places:

        @pl.when(me != j)
        def _(j=j, where=where):
            for l, ref in enumerate((dm0, dm1)):
                cp = push(ref, dm_in.at[j, l], ms.at[l, j], mr.at[l, j], where)
                cp.wait_send()
                cp.wait_recv()

        @pl.when(me == j)
        def _(j=j):
            dm_in[j, 0] = dm0[...]
            dm_in[j, 1] = dm1[...]

    total = dm_in[0]
    for j in range(1, 8):
        total = total + dm_in[j]
    lane = lax.broadcasted_iota(jnp.int32, (2, 8, D), 1)
    wide = jnp.concatenate([feat[...]] * 6, axis=1)
    high = wide.astype(BF).astype(F32)
    total = jnp.where(lane == 6, high, jnp.where(lane == 7, wide - high, total))
    dsum[...] = total.astype(BF)
    mlp_rest.sum_third(fin_m0)
    done = place_in(0, fin_m0, out_m0)
    done.start()
    attn_first.sum()
    attn_rest.begin()
    done.wait()
    ag_m0.start(0)
    ag_m1.finish()
    ag_m1.start(2)
    ag_a1.finish()
    ag_a1.start(2)
    attn_rest.sum_second()
    ag_m0.finish()
    ag_m0.start(1)
    moved = [push(dsum, rows_out.at[row], ms2.at[o], mr2.at[o], where) for o, where in enumerate(others)]
    for cp in moved:
        cp.start()
    keep = pltpu.make_async_copy(dsum, rows_out.at[row], fsem.at[2])
    keep.start()
    attn_rest.sum_third(fin_a0)
    done = place_in(1, fin_a0, out_a0)
    done.start()
    done.wait()
    ag_a0.start(0)
    ag_m0.finish()
    ag_m0.start(2)
    ag_a0.finish()
    ag_a0.start(1)
    ag_a0.finish()
    ag_a0.start(2)
    for ag in (ag_m1, ag_a1, ag_m0, ag_a0):
        ag.finish()
    keep.wait()
    for cp in moved:
        cp.wait()
    for s in (0, 2):
        scattered.send(s, db0.at[s // 2], False)
        scattered.received(s)


def finish(*operands):
    dma = pltpu.SemaphoreType.DMA
    shapes = [ATTN, MLP, ATTN, MLP, (2, 2, TOK, D)]
    scratch = [
        pltpu.VMEM((3, 16, HALF), BF),
        pltpu.VMEM((2, 48, HALF), BF),
        pltpu.VMEM((8, 2, 8, D), F32),
        pltpu.VMEM((2, 8, D), BF),
    ]
    scratch += ReduceRest.scratch(MLP_SUM, MLP_ROWS)
    scratch += [pltpu.VMEM(dims, BF) for dims in ReduceFirst.shapes(ATTN_SUM, ATTN_ROWS)]
    scratch += ReduceFirst.scratch(ATTN_SUM, ATTN_ROWS)
    scratch += ReduceRest.scratch(ATTN_SUM, ATTN_ROWS)
    scratch += [dma((27,))] * 8 + [dma((4,)), dma((4,))]
    scratch += [dma((2, 8)), dma((2, 8)), dma((15,)), dma((15,)), dma((3,))]
    return pl.pallas_call(
        finish_kernel,
        out_shape=tuple(
            [jax.ShapeDtypeStruct(dims, BF) for dims in shapes] + [jax.ShapeDtypeStruct((16, 2, 8, D), BF)]
        ),
        in_specs=[VM] * 8 + [ANY],
        out_specs=(ANY,) * 6,
        scratch_shapes=scratch,
        compiler_params=pltpu.CompilerParams(
            collective_id=4, has_side_effects=True, vmem_limit_bytes=62 * 2**20
        ),
        name="finish",
    )(*operands)


def modulation_kernel(rows, grad_mod, grad_bias):
    features = rows[:, 0, 6, 0:128].astype(F32) + rows[:, 0, 7, 0:128].astype(F32)
    for l in range(2):
        for i in range(6):
            cols = slice(D * i, D * (i + 1))
            d = rows[:, l, i, :].astype(F32)
            grad_mod[l, :, cols] = lax.dot_general(
                features, d, (((0,), (0,)), ((), ())), precision=highest, preferred_element_type=F32
            )
            grad_bias[l : l + 1, cols] = jnp.sum(d, axis=0, keepdims=True)


def modulation_grads(rows):
    return pl.pallas_call(
        modulation_kernel,
        out_shape=(
            jax.ShapeDtypeStruct((2, 128, 6 * D), F32),
            jax.ShapeDtypeStruct((2, 6 * D), F32),
        ),
        in_specs=[VM],
        out_specs=(VM, VM),
        compiler_params=pltpu.CompilerParams(vmem_limit_bytes=30 * 2**20),
        name="modulation_grads",
    )(rows)


def rotary(count):
    frequency = np.exp(-np.log(10000.0) * np.arange(32) / 32)
    angles = np.arange(count)[:, None] * frequency[None, :]
    cos, sin = np.cos(angles), np.sin(angles)
    return (
        np.concatenate([cos] * 4, axis=1).astype(np.float32),
        np.concatenate([-sin, sin, -sin, sin], axis=1).astype(np.float32),
    )


def time_features(step_values, feature_count):
    half_count = feature_count // 2
    frequency = jnp.exp(-np.log(10000.0) * jnp.arange(half_count, dtype=F32) / half_count)
    angles = step_values.astype(F32)[:, None] * frequency[None, :]
    return jnp.concatenate([jnp.cos(angles), jnp.sin(angles)], axis=1)


def on_device(hidden_in, segments, timestep, w_qkv, w_out, w_up, w_down, w_mod, b_mod, cotangent):
    x, ylo, z, yhi, c = here()
    attn_loc = jnp.concatenate([jnp.swapaxes(w_qkv, 1, 2), w_out], axis=1).reshape((2,) + ATTN)
    up_loc = w_up.reshape(2, 2, 4, 2, 48, D)
    down_loc = w_down.reshape(2, 2, 4, 2, 48, D)

    mine = lax.dynamic_slice_in_dim(timestep, yhi, 1, 0)
    features = time_features(mine, w_mod.shape[1])
    modulation = jnp.einsum(
        "rf,lfm->lrm", features, w_mod.astype(F32), precision=highest
    ) + b_mod.astype(F32)[:, None, :]
    modulation = modulation.reshape(2, 6, D)
    seg = lax.dynamic_slice_in_dim(segments, yhi, 1, 0)
    segc, segr = seg.reshape(SEQ, 1), seg
    cosine, sine = (jnp.asarray(v) for v in rotary(SEQ))
    place = (2 * z + c) * TOK
    cos_here = lax.dynamic_slice_in_dim(cosine, place, TOK, 0)
    sin_here = lax.dynamic_slice_in_dim(sine, place, TOK, 0)

    *state, x0, cots, wa0, wm0, wa1, wm1 = forward(
        hidden_in.reshape(2, 2, TOK, D),
        cotangent.reshape(2, 2, TOK, D),
        modulation,
        segc,
        segr,
        cos_here,
        sin_here,
        attn_loc,
        up_loc,
        down_loc,
    )
    known = (cosine, sine, x0, cots, *state)
    din1, dinb1, dm1, ga1, *shares1, y_out = backward(1, modulation, segc, segr, *known, wa1, wm1)
    _, dinb0, dm0, ga0, *shares0, g_out1, fin_a1, fin_m1 = backward(
        0, modulation, segc, segr, din1, dinb1, *shares1, *known, wa0, wm0, ga1
    )
    out_a0, out_m0, out_a1, out_m1, g_out0, rows = finish(
        *shares0, fin_a1, fin_m1, dm0, dm1, features, dinb0, ga0
    )
    g_out = jnp.where(z % 2 == 1, g_out1, g_out0)
    grad_mod, grad_bias = modulation_grads(rows)

    attn = jnp.stack([out_a0, out_a1]).reshape(2, D, D)
    mlp = jnp.stack([out_m0, out_m1]).reshape(2, 2 * D, D)
    return (
        y_out.reshape(1, 2, 2 * TOK, D),
        g_out.reshape(1, 2, 2 * TOK, D).astype(F32),
        attn[:, 0:576].swapaxes(1, 2).astype(F32),
        attn[:, 576:768].astype(F32),
        mlp[:, 0:768].astype(F32),
        mlp[:, 768:1536].astype(F32),
        grad_mod,
        grad_bias,
    )


def solution(mesh):
    placed = (
        P("dp", "tensor", None),
        P("dp", None),
        P("dp"),
        P(None, None, "tensor"),
        P(None, "tensor", None),
        P(None, None, "tensor"),
        P(None, "tensor", None),
        P(),
        P(),
        P("section", "dp", "tensor", None),
    )
    return jax.shard_map(
        on_device,
        mesh=mesh,
        in_specs=placed,
        out_specs=(
            P("section", "dp", "tensor", None),
            P("section", "dp", "tensor", None),
            P(None, None, "tensor"),
            P(None, "tensor", None),
            P(None, None, "tensor"),
            P(None, "tensor", None),
            P(),
            P(),
        ),
        check_vma=False,
    )
```

```python
import functools

import jax
import jax.numpy as jnp
import numpy as np
from jax import lax
from jax.experimental import pallas as pl
from jax.experimental.pallas import tpu as pltpu
from jax.sharding import PartitionSpec as P

MESH = pl.DeviceIdType.MESH
BF = jnp.bfloat16
F32 = jnp.float32
highest = lax.Precision.HIGHEST
EPS = 1e-06
D = 768
TOK = 128
SEQ = 1024
ANY = pl.BlockSpec(memory_space=pl.ANY)
VM = pl.BlockSpec(memory_space=pltpu.VMEM)
HALF = 384
ATTN = (4, 4, 3, 16, D)
MLP = (4, 4, 2, 48, D)


def here():
    dp = lax.axis_index("dp")
    t = lax.axis_index("tensor")
    return dp // 2, dp % 2, lax.axis_index("section"), t // 2, t % 2


def dev(x, ylo, z, yhi, c):
    return (2 * x + ylo, z, 2 * yhi + c)


def push(src, dst, send_sem, recv_sem, where):
    return pltpu.make_async_remote_copy(
        src_ref=src,
        dst_ref=dst,
        send_sem=send_sem,
        recv_sem=recv_sem,
        device_id=where,
        device_id_type=MESH,
    )


def greet(devices):
    barrier = pltpu.get_barrier_semaphore()
    for where in devices:
        pl.semaphore_signal(barrier, inc=1, device_id=where, device_id_type=MESH)
    return lambda: pl.semaphore_wait(barrier, len(devices))


def nn(a, b):
    return lax.dot_general(a, b, (((1,), (0,)), ((), ())), preferred_element_type=F32)


def nt(a, b):
    return lax.dot_general(a, b, (((1,), (1,)), ((), ())), preferred_element_type=F32)


def tn(a, b):
    return lax.dot_general(a, b, (((0,), (0,)), ((), ())), preferred_element_type=F32)


def normalize(values):
    centred = values - jnp.mean(values, axis=-1, keepdims=True)
    inverse = lax.rsqrt(jnp.mean(centred * centred, axis=-1, keepdims=True) + EPS)
    return centred * inverse, inverse


def norm_back(gradient, normed, inverse):
    return inverse * (
        gradient
        - jnp.mean(gradient, axis=-1, keepdims=True)
        - normed * jnp.mean(gradient * normed, axis=-1, keepdims=True)
    )


def lanes(shape):
    return lax.broadcasted_iota(jnp.int32, shape, len(shape) - 1)


def swap(x):
    return pltpu.roll(x, 64, 1)


def turn(x, cosine, sine):
    low = (lanes(x.shape) % 64) < 32
    other = jnp.where(low, pltpu.roll(x, 96, 1), pltpu.roll(x, 32, 1))
    return x * cosine + other * sine


def half(ylo):
    return pl.ds(pl.multiple_of(HALF * ylo, 128), HALF)


class Spread:
    def __init__(self, buf, orders, ss, rs, ring=False):
        self.buf, self.orders, self.ss, self.rs, self.ring = buf, orders, ss, rs, ring
        self.sent, self.rest, self.relays = [], [], []

    def at(self, dims, part, by, cols=None):
        x, ylo, z, yhi, c = here()
        everything = slice(None)
        i = everything if "x" in dims else by.get("x", x)
        j = everything if "z" in dims else by.get("z", z)
        k = cols if cols is not None else everything if "y" in dims else half(by.get("y", ylo))
        return self.buf.at[i, j, part, :, k]

    def peer(self, dim, o):
        x, ylo, z, yhi, c = here()
        if dim == "y":
            return dev(x, 1 - ylo, z, yhi, c), 1 - ylo
        if dim == "x":
            return dev((x + o) % 4, ylo, z, yhi, c), (x - o + 4) % 4
        return dev(x, ylo, (z + o) % 4, yhi, c), (z - o + 4) % 4

    def start(self, phase):
        self.sent, self.rest, self.relays = [], [], []
        for part in range(len(self.orders)):
            dim, done = self.orders[part][phase], self.orders[part][:phase]
            ring = self.ring and phase == 2 and dim != "y"
            for o in (1, 3) if ring else (1,) if dim == "y" else (2, 1, 3):
                where, origin = self.peer(dim, o)
                n = (phase * 3 + part) * 3 + o - 1
                here_now = self.at(done, part, {})
                cp = push(here_now, here_now, self.ss.at[n], self.rs.at[n], where)
                cp.start()
                self.sent.append(cp)
                back = self.at(done, part, {dim: origin})
                got = push(back, back, self.ss.at[n], self.rs.at[n], where), back
                if ring:
                    self.relays.append((part, dim, done, o, got))
                else:
                    self.rest.append(got)

    def relay(self, each=None):
        x, ylo, z, yhi, c = here()
        for part, dim, done, o, (cp, back) in self.relays:
            cp.wait_recv()
            if each is not None:
                each(back)
            where, origin = self.peer(dim, o)
            cols = pl.ds(0 if o == 1 else HALF, HALF)
            n = (2 * 3 + part) * 3 + 1 if o == 1 else 27 + part
            ref = self.at(done, part, {dim: origin}, cols)
            cp = push(ref, ref, self.ss.at[n], self.rs.at[n], where)
            cp.start()
            self.sent.append(cp)
            far = self.at(done, part, {dim: ((x if dim == "x" else z) + 2) % 4}, cols)
            self.rest.append((push(far, far, self.ss.at[n], self.rs.at[n], where), far))
        self.relays = []

    def finish(self, each=None):
        self.relay(each)
        for cp, back in self.rest:
            cp.wait_recv()
            if each is not None:
                each(back)
        for cp in self.sent:
            cp.wait_send()

    def held(self):
        return [self.at(self.orders[p][:2], p, {}) for p in range(len(self.orders))]


class Gather:
    def __init__(self, wv, pieces, orders, ss, rs, ps, pr, ls):
        x, ylo, z, yhi, c = here()
        self.wv, self.pieces = wv, pieces
        self.ps, self.pr, self.ls = ps, pr, ls
        self.t = 2 * yhi + c
        self.other = 2 * (1 - yhi) + c
        self.partner = dev(x, ylo, z, yhi, 1 - c)
        self.cross = dev(x, 1 - ylo, z, 1 - yhi, c)
        self.spread = Spread(wv.at[self.other], orders, ss, rs)
        self.handed = []

    def side(self, n):
        ref, first = self.pieces[n]
        spot = self.wv.at[self.t, pl.ds(first, ref.shape[0])]
        return (
            pltpu.make_async_copy(ref, spot, self.ls.at[n]),
            push(ref, spot, self.ps.at[n], self.pr.at[n], self.partner),
        )

    def s0(self):
        x, ylo, z, yhi, c = here()
        for ref, first in self.pieces:

            @pl.when((x >= first) & (x < first + ref.shape[0]))
            def _(ref=ref, first=first):
                push(
                    ref.at[x - first, z, :, :, half(1 - ylo)],
                    self.wv.at[self.t, x, z, :, :, half(1 - ylo)],
                    self.ps.at[2],
                    self.pr.at[2],
                    self.cross,
                ).start()

    def beside(self):
        for n in range(len(self.pieces)):
            for cp in self.side(n):
                cp.start()

    def s1(self):
        x, ylo, z, yhi, c = here()
        landed = self.wv.at[self.other, x, z, :, :, half(ylo)]
        cp = push(landed, landed, self.ps.at[2], self.pr.at[2], self.cross)
        cp.wait_recv()
        cp.wait_send()
        self.spread.start(0)

    def s2(self):
        self.spread.finish()
        self.spread.start(1)

    def hand(self, ref):
        n = 3 + len(self.handed)
        cp = push(ref, ref, self.ps.at[n], self.pr.at[n], self.partner)
        cp.start()
        self.handed.append(cp)

    def s3(self):
        self.spread.finish()
        self.spread.start(2)
        for ref in self.spread.held():
            self.hand(ref)

    def s4(self):
        self.spread.finish(self.hand)

    def own(self):
        for n in range(len(self.pieces)):
            local, cp = self.side(n)
            local.wait()
            cp.wait_send()
            cp.wait_recv()

    def s5(self):
        for cp in self.handed:
            cp.wait_send()
            cp.wait_recv()


def gather_scratch():
    dma = pltpu.SemaphoreType.DMA
    return [dma((30,)), dma((30,)), dma((16,)), dma((16,)), dma((2,))]


def chips_around():
    x, ylo, z, yhi, c = here()
    return [dev((x + o) % 4, ylo, z, yhi, c) for o in (1, 2, 3)] + [
        dev(x, 1 - ylo, z, yhi, c),
        dev(x, 1 - ylo, z, 1 - yhi, c),
    ]


def dp_group():
    x, ylo, z, yhi, c = here()
    t = 2 * yhi + c
    return [(2 * x + ylo, (z + a) % 4, (t + b) % 4) for a in range(4) for b in range(4) if a or b]


def row_places():
    x, ylo, z, yhi, c = here()
    return [(2 * a + b, dev(x, ylo, a, yhi, b)) for a in range(4) for b in range(2)], 2 * z + c


def row_mates():
    x, ylo, z, yhi, c = here()
    me = 2 * z + c
    return [dev(x, ylo, ((me + o) % 8) // 2, yhi, (me + o) % 2) for o in range(1, 8)]


def deal(j, where, me, src, dst, s, r):
    @pl.when(me != j)
    def _():
        push(src, dst, s(j), r(me), where).start()

    @pl.when(me == j)
    def _():
        dst[...] = src[...]


def dealt(j, where, me, src, dst, s, r):
    @pl.when(me != j)
    def _():
        cp = push(src, dst, s(j), r(j), where)
        cp.wait_send()
        cp.wait_recv()


def place_of(sem):
    return lambda j: sem.at[j]


def attn_rows(wa, t, low, high):
    first, last = low // 192, -(-high // 192)
    whole = wa[t, first:last].reshape(192 * (last - first), D)
    return whole[low - 192 * first : high - 192 * first]


def up_rows(wt):
    return wt[0:2].reshape(D, D)


def down_rows(wt):
    return wt[2:4].reshape(D, D)


class Tokens:
    def __init__(self, hid, x0, hs, hr, ls):
        self.refs = hid, x0, hs, hr, ls

    def start(self):
        hid, x0, hs, hr, ls = self.refs
        x, ylo, z, yhi, c = here()
        t = 2 * yhi + c
        for b in range(4):

            @pl.when((t == z) & (t != b))
            def _(b=b):
                push(hid.at[b // 2, b % 2], x0, hs.at[b], hr.at[0], (2 * x + ylo, z, b)).start()

            @pl.when((t == z) & (t == b))
            def _(b=b):
                pltpu.make_async_copy(hid.at[b // 2, b % 2], x0, ls.at[0]).start()

    def arrive(self):
        hid, x0, hs, hr, ls = self.refs
        x, ylo, z, yhi, c = here()
        t = 2 * yhi + c

        @pl.when(t != z)
        def _():
            push(x0, x0, hs.at[0], hr.at[0], (2 * x + ylo, z, (t + 1) % 4)).wait_recv()

        @pl.when(t == z)
        def _():
            pltpu.make_async_copy(hid.at[0, 0], x0, ls.at[0]).wait()

    def sent(self):
        hid, x0, hs, hr, ls = self.refs
        x, ylo, z, yhi, c = here()
        t = 2 * yhi + c
        for b in range(4):

            @pl.when((t == z) & (t != b))
            def _(b=b):
                push(hid.at[b // 2, b % 2], x0, hs.at[b], hr.at[0], (2 * x + ylo, z, b)).wait_send()


class Cotangents:
    def __init__(self, cot, cots, over, cs, cr, ls):
        self.refs = cot, cots, over, cs, cr, ls

    def load(self, begin):
        cot, cots, over, cs, cr, ls = self.refs
        x, ylo, z, yhi, c = here()

        @pl.when(2 * yhi + c == z)
        def _():
            cp = pltpu.make_async_copy(cot.at[yhi, c], over, ls.at[0])
            if begin:
                cp.start()
            else:
                cp.wait()

    def move(self, step, begin):
        cot, cots, over, cs, cr, ls = self.refs
        x, ylo, z, yhi, c = here()
        t = 2 * yhi + c
        dp = 2 * x + ylo
        b = (step + z) % 4

        @pl.when((t != z) | (t != b))
        def _():
            cp = push(cot.at[b // 2, b % 2], cots.at[z], cs.at[step], cr.at[z], (dp, t, b))
            if begin:
                cp.start()
            else:
                cp.wait_send()

        @pl.when((t == z) & (t == b))
        def _():
            cp = pltpu.make_async_copy(over, cots.at[z], ls.at[1])
            if begin:
                cp.start()
            else:
                cp.wait()

        if not begin:

            @pl.when((t != z) | (z != step))
            def _():
                spot = cots.at[step]
                push(spot, spot, cs.at[step], cr.at[step], (dp, z, (t + 1) % 4)).wait_recv()


class Scatter:
    def __init__(self, dst, s_sem, r_sem):
        self.dst, self.s_sem, self.r_sem = dst, s_sem, r_sem

    def send(self, s, src, begin):
        x, ylo, z, yhi, c = here()
        t = 2 * yhi + c
        mine = (z == s) & (t == z)

        @pl.when(jnp.logical_not(mine))
        def _():
            where = (2 * x + ylo, s, z)
            cp = push(src, self.dst.at[yhi, c], self.s_sem.at[s], self.r_sem.at[t], where)
            if begin:
                cp.start()
            else:
                cp.wait_send()

        @pl.when(mine)
        def _():
            cp = pltpu.make_async_copy(src, self.dst.at[yhi, c], self.s_sem.at[s])
            if begin:
                cp.start()
            else:
                cp.wait()

    def received(self, s):
        x, ylo, z, yhi, c = here()
        t = 2 * yhi + c
        for b in range(4):

            @pl.when((z == s) & ((t != b) | (t != z)))
            def _(b=b):
                spot = self.dst.at[b // 2, b % 2]
                where = (2 * x + ylo, z, (t + 1) % 4)
                push(spot, spot, self.s_sem.at[b], self.r_sem.at[b], where).wait_recv()


STATE = ("y", "qkv", "lse", "att", "ba", "mid", "pre", "bb", "o")


def state_shapes():
    return (
        ((TOK, D), BF),
        ((8, TOK, 384), BF),
        ((4, 8, 384), F32),
        ((TOK, 1024), BF),
        ((TOK, D), F32),
        ((TOK, D), F32),
        ((TOK, 4 * D), F32),
        ((TOK, D), F32),
        ((8, TOK, 128), BF),
    )


def forward_kernel(*refs):
    refs = list(refs)

    def take(count):
        got = refs[:count]
        del refs[:count]
        return got

    hid, cot, mods, segc, segr, cosine, sine, attn_loc, up_loc, down_loc = take(10)
    outs = dict(zip(STATE, take(9)))
    x0, cots, *weights_out = take(6)
    held = dict(zip(STATE, take(9)))
    sbuf, rbuf, cos_ref, sin_ref, wa0, wa1, wm0, wm1 = take(8)
    wsem, ksem, ss, rs, ss2, rs2 = take(6)
    x, ylo, z, yhi, c = here()
    places, me = row_places()
    saved = []

    def save(src, dst):
        cp = pltpu.make_async_copy(src, dst, wsem.at[len(saved)])
        cp.start()
        saved.append(cp)

    beside = ("zyx", "zxy")
    a0 = Gather(wa0, [(attn_loc.at[0], 0)], ("zyx", "xzy", "yxz"), *take(5))
    m0 = Gather(wm0, [(up_loc.at[0], 0), (down_loc.at[0], 2)], beside, *take(5))
    a1 = Gather(wa1, [(attn_loc.at[1], 0)], ("zyx", "zxy", "zyx"), *take(5))
    m1 = Gather(wm1, [(up_loc.at[1], 0), (down_loc.at[1], 2)], beside, *take(5))
    tokens = Tokens(hid, x0, *take(3))
    cotangents = Cotangents(cot, cots, *take(4))
    mine = pl.ds(pl.multiple_of(TOK * me, TOK), TOK)
    tables = [
        pltpu.make_async_copy(cosine.at[mine], cos_ref, wsem.at[4]),
        pltpu.make_async_copy(sine.at[mine], sin_ref, wsem.at[5]),
    ]
    for cp in tables:
        cp.start()
    greet(dp_group() + chips_around())()
    for gather in (a0, m0, a1, m1):
        gather.s0()
    a0.beside()
    tokens.start()
    cotangents.load(True)
    a0.s1()
    a0.s2()
    m0.s1()
    a0.s3()
    m0.beside()
    tokens.arrive()

    for cp in tables:
        cp.wait()
    cos_here, sin_here = cos_ref[...], sin_ref[...]
    low = lanes((TOK, 128)) < 64
    seg_keys = segr[...]

    def flat(column):
        wide = jnp.broadcast_to(column, (column.shape[0], 128))
        return jnp.transpose(wide)[0:8, :]

    def keeping(app):
        slot = app % 2
        return [
            pltpu.make_async_copy(held[name].at[app if name == "y" else slot], outs[name].at[app], ksem.at[slot, n])
            for n, name in enumerate(STATE)
        ]

    for app in range(4):
        slot = app % 2
        wa, wm = ((wa0, wm0), (wa1, wm1))[slot]
        mod = mods.at[slot]
        qkv, lse, att, ba, mid, pre, bb, obuf = (held[name].at[slot] for name in STATE[1:])
        if app == 0:
            v = x0[...].astype(F32)
        else:
            v = held["y"][app - 1].astype(F32)
            if app == 2:
                v = v + x0[...].astype(F32)
        hat, _ = normalize(v)
        normed = (hat * (1.0 + mod[1:2, :]) + mod[0:1, :]).astype(BF)
        if app == 0:
            a0.own()
        if app == 1:
            a1.s4()
            m1.s2()
            a1.own()
            a1.s5()
            save(wa1, weights_out[2])
        for i in range(4):
            if app == 0 and i == 2:
                a0.s4()
                m0.s2()
                a0.s5()
                save(wa0, weights_out[0])
            t = (2 * yhi + i) % 4
            got = nt(normed, attn_rows(wa, t, 0, 640))
            t0, t1, t2, t3, t4 = (got[:, 128 * n : 128 * (n + 1)] for n in range(5))
            s0, s1, s2, s3, s4 = (swap(u) for u in (t0, t1, t2, t3, t4))
            for head, (q, k, w) in enumerate(
                (
                    (jnp.where(low, t0, s3), jnp.where(low, s0, t3), jnp.where(low, t1, s4)),
                    (jnp.where(low, s1, s3), jnp.where(low, t2, t3), jnp.where(low, s2, s4)),
                )
            ):
                j = 2 * t + head
                sbuf[j, :, 0:128] = (turn(q, cos_here, sin_here).astype(BF).astype(F32) * 0.125).astype(BF)
                sbuf[j, :, 128:256] = turn(k, cos_here, sin_here).astype(BF)
                sbuf[j, :, 256:384] = w.astype(BF)
                where = dev(x, ylo, t, yhi, head)
                deal(j, where, me, sbuf.at[j], qkv.at[me], place_of(ss.at[app]), place_of(rs.at[app]))
        if app == 0:
            a1.beside()
            m0.s3()
            a1.s1()
        if app == 1:
            m1.s3()
        for j, where in places:
            dealt(j, where, me, sbuf.at[j], qkv.at[j], place_of(ss.at[app]), place_of(rs.at[app]))
        if app:
            for cp in keeping(app - 1):
                cp.wait()

        if app == 0:
            a1.s2()
            m1.beside()

        keys = qkv[:, :, 128:256].reshape(SEQ, 128)
        values = qkv[:, :, 256:384].reshape(SEQ, 128)

        def softmax(q, seg_q, keys=keys, values=values):
            scores = jnp.where(seg_q == seg_keys, nt(q, keys), -1e30)
            largest = jnp.max(scores, axis=-1, keepdims=True)
            raised = jnp.exp(scores - largest)
            total = jnp.sum(raised, axis=-1, keepdims=True)
            mixed = nn(raised.astype(BF), values) * (1.0 / total)
            return mixed, largest + jnp.log(total)

        for a in range(4):
            q = qkv[2 * a : 2 * a + 2, :, 0:128].reshape(256, 128)
            q = jnp.where(lanes((256, 128)) < 64, q, 0).astype(BF)
            mixed, total = softmax(q, segc[256 * a : 256 * (a + 1), :])
            q2 = jnp.where(low, 0, qkv[2 * a + c, :, 0:128]).astype(BF)
            mixed2, total2 = softmax(q2, segc[pl.ds(256 * a + TOK * c, TOK), :])
            lse[a, :, 0:256] = flat(total)
            lse[a, :, 256:384] = flat(total2)
            for b in range(2):
                j = 2 * a + b
                part = mixed[TOK * b : TOK * (b + 1)]
                obuf[j] = jnp.where(low | (c != b), part, mixed2).astype(BF)
                deal(j, places[j][1], me, obuf.at[j], rbuf.at[me], place_of(ss2.at[app]), place_of(rs2.at[app]))
        if app == 0:
            a1.s3()
        for j, where in places:
            dealt(j, where, me, obuf.at[j], rbuf.at[j], place_of(ss2.at[app]), place_of(rs2.at[app]))

        if app == 0:
            cotangents.load(False)
        cotangents.move(app, True)
        branch_a = jnp.zeros((TOK, D), F32)
        for t in range(4):
            first, second = rbuf[2 * t], rbuf[2 * t + 1]
            own = jnp.where(low, first.astype(F32), swap(second.astype(F32))).astype(BF)
            extra = jnp.where(low, 0, rbuf[2 * t + c]).astype(BF)
            att[:, 128 * t : 128 * (t + 1)] = own
            att[:, 512 + 128 * t : 512 + 128 * (t + 1)] = extra
            branch_a = branch_a + nn(own, attn_rows(wa, t, 576, 704)) + nn(extra, attn_rows(wa, t, 640, 768))
        ba[...] = branch_a
        middle = v + mod[2:3, :] * branch_a
        mid[...] = middle
        hat_b, _ = normalize(middle)
        normed_b = (hat_b * (1.0 + mod[4:5, :]) + mod[3:4, :]).astype(BF)
        if app == 0:
            m0.s4()
            m0.own()
            m0.s5()
            save(wm0, weights_out[1])
            m1.s1()
        if app == 1:
            m1.s4()
            m1.own()
            m1.s5()
            save(wm1, weights_out[3])
        total_b = jnp.zeros((TOK, D), F32)
        for t in range(4):
            before = nn(normed_b, up_rows(wm.at[t]))
            pre[:, D * t : D * (t + 1)] = before
            total_b = total_b + nn(jax.nn.gelu(before, approximate=True).astype(BF), down_rows(wm.at[t]))
        bb[...] = total_b
        held["y"][app] = (middle + mod[5:6, :] * total_b).astype(BF)
        for cp in keeping(app):
            cp.start()
    for b in range(4):
        cotangents.move(b, False)
    tokens.sent()
    for cp in keeping(3) + saved:
        cp.wait()


def forward(*operands):
    dma = pltpu.SemaphoreType.DMA
    outs = [jax.ShapeDtypeStruct((4,) + dims, dtype) for dims, dtype in state_shapes()]
    outs += [jax.ShapeDtypeStruct(dims, BF) for dims in ((TOK, D), (4, TOK, D))]
    outs += [jax.ShapeDtypeStruct((4,) + group, BF) for group in (ATTN, MLP, ATTN, MLP)]
    scratch = [pltpu.VMEM((2,) + dims, dtype) for dims, dtype in state_shapes()]
    scratch[0] = pltpu.VMEM((4, TOK, D), BF)
    scratch += [
        pltpu.VMEM((8, TOK, 384), BF),
        pltpu.VMEM((8, TOK, 128), BF),
        pltpu.VMEM((TOK, 128), F32),
        pltpu.VMEM((TOK, 128), F32),
    ]
    scratch += [pltpu.VMEM((4,) + group, BF) for group in (ATTN, ATTN, MLP, MLP)]
    scratch += [dma((6,)), dma((2, 9))] + [dma((4, 8))] * 4
    for _ in range(4):
        scratch += gather_scratch()
    scratch += [dma((4,)), dma((1,)), dma((1,))]
    scratch += [pltpu.VMEM((TOK, D), BF), dma((4,)), dma((4,)), dma((2,))]
    return pl.pallas_call(
        forward_kernel,
        out_shape=tuple(outs),
        in_specs=[ANY] * 2 + [VM] * 3 + [ANY] * 5,
        out_specs=tuple([ANY] * 9 + [VM] + [ANY] * 5),
        scratch_shapes=scratch,
        compiler_params=pltpu.CompilerParams(
            collective_id=1, has_side_effects=True, vmem_limit_bytes=62 * 2**20
        ),
        name="forward",
    )(*operands)


def across(dim, o):
    x, ylo, z, yhi, c = here()
    if dim == "x":
        to = (x + o) % 4
        return dev(to, ylo, z, yhi, c), to
    if dim == "z":
        to = (z + o) % 4
        return dev(x, ylo, to, yhi, c), to
    to = (2 * yhi + ylo + o) % 4
    return dev(x, to % 2, z, to // 2, c), to


def own_place(dim):
    x, ylo, z, yhi, c = here()
    return {"x": x, "z": z, "y": 2 * yhi + ylo}[dim]


def reduce_greeted():
    return [across(dim, o)[0] for dim in "xy" for o in (1, 2, 3)]


def left(order, steps):
    return [label for label in "Yxz" if label.lower() not in order[:steps]]


def block(order, steps, rows):
    sizes = {"Y": 2, "x": 4, "z": 4}
    lane_count = HALF if "y" in order[:steps] else D
    return tuple(sizes[label] for label in left(order, steps)) + (rows, lane_count)


def pick(labels, dim, to):
    index = [slice(None)] * len(labels)
    if dim == "y":
        index[labels.index("Y")] = to // 2
        return tuple(index), half(to % 2)
    index[labels.index(dim)] = to
    return tuple(index), slice(None)


def each_unit(dims, body):
    count = 1
    for size in dims:
        count *= size

    def step(i, carry):
        index, rest = [], i
        for size in reversed(dims):
            index.append(rest % size)
            rest = rest // size
        body(tuple(reversed(index)))
        return carry

    lax.fori_loop(0, count, step, 0)


class ReduceFirst:
    def __init__(self, grads, orders, own, arrived, ls, ss, rs):
        self.grads, self.orders, self.own, self.arrived = grads, orders, own, arrived
        self.ls, self.ss, self.rs = ls, ss, rs

    def source(self, p, to):
        index, cols = pick(["Y", "x", "z"], self.orders[p][0], to)
        return self.grads.at[index + (p, slice(None), cols)]

    def copies(self):
        found = []
        if self.ls is not None:
            for p, order in enumerate(self.orders):
                found.append(pltpu.make_async_copy(self.source(p, own_place(order[0])), self.own[p], self.ls.at[p]))
        for o in (2, 1, 3):
            for p, order in enumerate(self.orders):
                where, to = across(order[0], o)
                n = 3 * p + o - 1
                found.append(push(self.source(p, to), self.arrived[p].at[o - 1], self.ss.at[n], self.rs.at[n], where))
        return found

    def begin(self):
        for cp in self.copies():
            cp.start()

    def sum(self):
        for cp in self.copies():
            cp.wait()
        for p in range(len(self.orders)):
            own, arrived = self.own[p], self.arrived[p]
            mine = own if self.ls is not None else self.source(p, own_place(self.orders[p][0]))

            def body(index, own=own, arrived=arrived, mine=mine):
                total = mine[index].astype(F32)
                for n in range(3):
                    total = total + arrived[(n,) + index].astype(F32)
                own[index] = total.astype(BF)

            each_unit(own.shape[:-2], body)

    @staticmethod
    def shapes(orders, rows):
        return [block(order, 1, rows) for order in orders]

    @staticmethod
    def scratch(orders, rows):
        dma = pltpu.SemaphoreType.DMA
        arrived = [pltpu.VMEM((3,) + dims, BF) for dims in ReduceFirst.shapes(orders, rows)]
        return arrived + [dma((3,)), dma((9,)), dma((9,))]


class ReduceRest:
    def __init__(self, orders, own, refs):
        refs = list(refs)
        count = len(orders)
        self.orders, self.own = orders, own
        self.mid, self.tot, self.end = refs[:count], refs[count : 2 * count], refs[2 * count : 3 * count]
        self.ss2, self.rs2, self.ss3, self.rs3 = refs[3 * count :]

    @staticmethod
    def scratch(orders, rows):
        dma = pltpu.SemaphoreType.DMA
        shapes = [pltpu.VMEM((3,) + block(order, 2, rows), BF) for order in orders]
        shapes += [pltpu.VMEM(block(order, 2, rows), BF) for order in orders]
        shapes += [pltpu.VMEM((3,) + block(order, 3, rows), BF) for order in orders]
        return shapes + [dma((9,))] * 4

    @staticmethod
    def count(orders):
        return 3 * len(orders) + 4

    def copies(self, step):
        found = []
        sources, targets = (self.own, self.mid) if step == 1 else (self.tot, self.end)
        send, recv = (self.ss2, self.rs2) if step == 1 else (self.ss3, self.rs3)
        for o in (2, 1, 3):
            for p, order in enumerate(self.orders):
                where, to = across(order[step], o)
                index, cols = pick(left(order, step), order[step], to)
                n = 3 * p + o - 1
                found.append(
                    push(sources[p].at[index + (slice(None), cols)], targets[p].at[o - 1], send.at[n], recv.at[n], where)
                )
        return found

    def begin(self):
        for cp in self.copies(1):
            cp.start()

    def sum_second(self):
        for cp in self.copies(1):
            cp.wait()
        for p, order in enumerate(self.orders):
            own, mid, tot = self.own[p], self.mid[p], self.tot[p]
            labels = left(order, 1)
            index, cols = pick(labels, order[1], own_place(order[1]))
            free = [n for n, value in enumerate(index) if isinstance(value, slice)]
            for i in range(tot.shape[0]):
                spot = list(index)
                spot[free[0]] = i
                total = own[tuple(spot) + (slice(None), cols)].astype(F32)
                for n in range(3):
                    total = total + mid[n, i].astype(F32)
                tot[i] = total.astype(BF)
        for cp in self.copies(2):
            cp.start()

    def sum_third(self, fin):
        for cp in self.copies(2):
            cp.wait()
        for p, order in enumerate(self.orders):
            index, cols = pick(left(order, 2), order[2], own_place(order[2]))
            total = self.tot[p][index + (slice(None), cols)].astype(F32)
            for n in range(3):
                total = total + self.end[p][n].astype(F32)
            fin[p] = total.astype(BF)


MLP_SUM = ("xyz", "yxz")
ATTN_SUM = ("xyz", "yzx", "zxy")
MLP_ROWS, ATTN_ROWS = 48, 16


def gelu_parts(u):
    k = 0.7978845608028654
    square = u * u
    th = jnp.tanh(k * u * (1.0 + 0.044715 * square))
    half_up = 0.5 * (1.0 + th)
    slope = half_up + 0.5 * u * (1.0 - th * th) * (k * (1.0 + 0.134145 * square))
    return u * half_up, slope


def backward_kernel(layer, *refs):
    refs = list(refs)

    def take(count):
        got = refs[:count]
        del refs[:count]
        return got

    mods, segc, segr = take(3)
    more_dy, *last_shares = take(3) if layer == 0 else [None]
    cosine_in, sine_in, x0_in, cots_in = take(4)
    outer = dict(zip(STATE, take(9)))
    wa_in, wm_in = take(2)
    before = take(1)[0] if layer == 0 else None
    din, dinb, dmod, grads, *shares = take(6)
    if layer == 0:
        fin_attn, fin_mlp = take(2)
    else:
        (y_out,) = take(1)
    held = dict(zip(STATE, take(9)))
    cosine, sine, x0, cots, lsem = take(5)
    mod = mods.at[layer]
    own_na, own_nb, own_dba, own_dbb, own_act, own_dpre, own_dpj = take(7)
    got_na, got_nb, got_dba, got_dbb, got_at, got_act, got_dpre, got_dpj = take(8)
    sbuf, rbuf, sbig, rbig, dmid, dnb, q_own, g_own, q_sh, g_sh, dq_own, dq_sh = take(12)
    wa, wm, mlp_grads, stage_attn = take(4)
    wsem, gsem, ss, rs, ss2, rs2, ss3, rs3, xs, xr = take(10)
    mlp_first = ReduceFirst(mlp_grads, MLP_SUM, shares, take(2), None, *take(3)[1:])
    rows_of = [slice(TOK * e, TOK * (e + 1)) for e in range(2)]
    x, ylo, z, yhi, c = here()
    places, me = row_places()
    partner = dev(x, ylo, z, yhi, 1 - c)
    if layer == 1:
        (ys,) = take(1)
        scattered = Scatter(y_out, *take(2))
    if layer == 0:
        mlp_rest = ReduceRest(MLP_SUM, last_shares, take(ReduceRest.count(MLP_SUM)))
        attn_first = ReduceFirst(before, ATTN_SUM, take(3), take(3), *take(3))
        attn_rest = ReduceRest(ATTN_SUM, attn_first.own, take(ReduceRest.count(ATTN_SUM)))
    entered = greet(dp_group() + reduce_greeted())
    loads = {}

    def load(name, src, dst):
        cp = pltpu.make_async_copy(src, dst, lsem.at[len(loads)])
        cp.start()
        loads[name] = cp

    def loaded(*names):
        for name in names:
            loads[name].wait()

    def load_state(name):
        for e in range(2):
            load((name, e), outer[name].at[layer + 2 * e], held[name].at[e])

    def state(name):
        loaded((name, 0), (name, 1))

    for e in range(2):
        load(("cots", e), cots_in.at[layer + 2 * e], cots.at[e])
    load_state("mid")
    load_state("bb")
    if layer == 0:
        load("x0", x0_in, x0)
        load(("y", 1), outer["y"].at[1], held["y"].at[1])
    else:
        load("y", outer["y"], ys)
    load_state("att")

    def wm_fetch(t):
        return pltpu.make_async_copy(wm_in.at[t], wm.at[t % 2], wsem.at[1 + t])

    wm_fetch(0).start()
    load_state("pre")
    wm_fetch(1).start()
    wa_fetch = pltpu.make_async_copy(wa_in, wa, wsem.at[0])
    wa_fetch.start()
    for name in ("ba", "qkv", "lse", "o"):
        load_state(name)
    load("cosine", cosine_in, cosine)
    load("sine", sine_in, sine)
    qkvs, lses, atts, bas, mids, pres, bbs, outputs = ([held[name].at[e] for e in range(2)] for name in STATE[1:])
    scale_a, gate_a = mod[1:2, :], mod[2:3, :]
    scale_b, gate_b = mod[4:5, :], mod[5:6, :]
    low = lanes((TOK, 128)) < 64
    exchanged = {}

    def hand(name, src, dst):
        n = len(exchanged)
        cp = push(src, dst, xs.at[n], xr.at[n], partner)
        cp.start()
        exchanged[name] = cp

    def have(*names):
        for name in names:
            exchanged[name].wait_send()
            exchanged[name].wait_recv()

    def gradient(e):
        dy = cots[e].astype(F32)
        return dy if more_dy is None else dy + more_dy[e]

    def entry(e):
        if layer == 1:
            return ys[2 * e].astype(F32)
        v = x0[...].astype(F32)
        return v + held["y"][1].astype(F32) if e else v

    loaded(("cots", 0), ("cots", 1))
    state("mid")
    state("bb")
    loaded(*(["x0", ("y", 1)] if layer == 0 else ["y"]))
    dgate_b = jnp.zeros((1, D), F32)
    for e in range(2):
        dy = gradient(e)
        dgate_b = dgate_b + jnp.sum(dy * bbs[e][...], axis=0, keepdims=True)
        own_dbb[rows_of[e], :] = (gate_b * dy).astype(BF)
        hat_b, _ = normalize(mids[e][...])
        own_nb[rows_of[e], :] = (hat_b * (1.0 + scale_b) + mod[3:4, :]).astype(BF)
        hat_a, _ = normalize(entry(e))
        own_na[rows_of[e], :] = (hat_a * (1.0 + scale_a) + mod[0:1, :]).astype(BF)
    entered()
    if layer == 1:
        for s in range(4):
            scattered.send(s, ys.at[s], True)
    hand("dbb", own_dbb, got_dbb)
    hand("nb", own_nb, got_nb)
    if layer == 0:
        mlp_rest.begin()
        attn_first.begin()
    state("pre")

    for t in range(4):
        wm_fetch(t).wait()
        d_act = nt(own_dbb[...], down_rows(wm.at[t % 2]))
        for e in range(2):
            act, slope = gelu_parts(pres[e][:, D * t : D * (t + 1)])
            own_act[t, rows_of[e], :] = act.astype(BF)
            own_dpre[t, rows_of[e], :] = (d_act[rows_of[e]] * slope).astype(BF)
        more = nt(own_dpre[t], up_rows(wm.at[t % 2]))
        dnb[...] = more if t == 0 else dnb[...] + more
        if t < 2:
            wm_fetch(t + 2).start()
    for h in range(2):
        hand(f"act{h}", own_act.at[2 * h + 1 - c], got_act.at[h])
        hand(f"dpre{h}", own_dpre.at[2 * h + 1 - c], got_dpre.at[h])

    hand("na", own_na, got_na)
    state("att")
    for e in range(2):
        hand(f"at{e}", atts[e], got_at.at[e])
    state("ba")
    dgate_a = jnp.zeros((1, D), F32)
    dscale_b = jnp.zeros((1, D), F32)
    dshift_b = jnp.zeros((1, D), F32)
    for e in range(2):
        hat_b, inv_b = normalize(mids[e][...])
        g = dnb[rows_of[e], :]
        dscale_b = dscale_b + jnp.sum(g * hat_b, axis=0, keepdims=True)
        dshift_b = dshift_b + jnp.sum(g, axis=0, keepdims=True)
        d_middle = gradient(e) + norm_back(g * (1.0 + scale_b), hat_b, inv_b)
        dmid[rows_of[e], :] = d_middle
        dgate_a = dgate_a + jnp.sum(d_middle * bas[e][...], axis=0, keepdims=True)
        own_dba[rows_of[e], :] = (gate_a * d_middle).astype(BF)
    hand("dba", own_dba, got_dba)
    wa_fetch.wait()
    for t in range(4):
        first = nt(own_dba[...], attn_rows(wa, t, 576, 704))
        second = nt(own_dba[...], attn_rows(wa, t, 640, 768))
        for e in range(2):
            sbuf[2 * t, e] = jnp.where(low, first[rows_of[e]], second[rows_of[e]]).astype(BF)
            sbuf[2 * t + 1, e] = second[rows_of[e]].astype(BF)
        for b in range(2):
            j = 2 * t + b
            deal(j, places[j][1], me, sbuf.at[j], rbuf.at[me], place_of(ss), place_of(rs))

    have("dbb", "nb", "act0", "dpre0", "act1", "dpre1")

    for h in range(2):
        t = 2 * h + c
        total = tn(own_nb[...], own_dpre[t]) + tn(got_nb[...], got_dpre[h])
        mlp_grads[h, 0:2] = total.astype(BF).reshape(2, 4, 2, 48, D)
        total = tn(own_act[t], own_dbb[...]) + tn(got_act[h], got_dbb[...])
        mlp_grads[h, 2:4] = total.astype(BF).reshape(2, 4, 2, 48, D)
    if layer == 0:
        mlp_first.begin()
    for j, where in places:
        dealt(j, where, me, sbuf.at[j], rbuf.at[j], place_of(ss), place_of(rs))

    if layer == 1:
        for s in range(4):
            scattered.send(s, ys.at[s], False)
            scattered.received(s)
        mlp_first.begin()
    state("qkv")
    state("lse")
    loaded("cosine", "sine")
    state("o")
    everyone = lanes((SEQ, 128)) < 64
    some = lanes((SEQ // 2, 128)) < 64
    row_of = lax.broadcasted_iota(jnp.int32, (8, 128), 0)
    picks = (row_of == jnp.where(lanes((8, 128)) < 64, 0, 1)).astype(F32)

    def shared_row(row):
        parts = []
        for a in range(4):
            first = row[:, 256 * a : 256 * a + 128]
            parts.append(jnp.where(c == 0, first, row[:, 256 * a + 128 : 256 * a + 256]))
        return jnp.concatenate(parts, axis=1)

    seg_own = segr[...]
    seg_sh = shared_row(seg_own)
    for e in range(2):
        qkv, lse = qkvs[e], lses[e]
        q_all = qkv[:, :, 0:128].reshape(SEQ, 128)
        g_all = rbuf[:, e].reshape(SEQ, 128)
        q_own[...] = jnp.where(everyone, q_all, 0).astype(BF)
        g_own[...] = jnp.where(everyone, g_all, 0).astype(BF)
        q_part = jnp.concatenate([qkv[2 * a + c, :, 0:128] for a in range(4)], axis=0)
        g_part = jnp.concatenate([rbuf[2 * a + c, e] for a in range(4)], axis=0)
        q_sh[...] = jnp.where(some, 0, q_part).astype(BF)
        g_sh[...] = jnp.where(some, 0, g_part).astype(BF)
        product = g_all.astype(F32) * outputs[e][...].reshape(SEQ, 128).astype(F32)
        centres = lax.dot_general(
            picks, product, (((1,), (1,)), ((), ())), precision=highest, preferred_element_type=F32
        )
        centre_own, centre_sh = centres[0:1, :], shared_row(centres[1:2, :])
        total_own = jnp.concatenate([lse[a, 0:1, 0:256] for a in range(4)], axis=1)
        total_sh = jnp.concatenate([lse[a, 0:1, 256:384] for a in range(4)], axis=1)

        for a in range(4):
            keys = qkv[2 * a : 2 * a + 2, :, 128:256].reshape(256, 128)
            values = qkv[2 * a : 2 * a + 2, :, 256:384].reshape(256, 128)
            seg_keys = segc[256 * a : 256 * (a + 1), :]

            def one(q, go, seg_q, total, centre, dq, keys=keys, values=values, seg_keys=seg_keys, a=a):
                scores = jnp.where(seg_keys == seg_q, nt(keys, q[...]), -1e30)
                p = jnp.exp(scores - total)
                d_s = (p * (nt(values, go[...]) - centre)).astype(BF)
                more = tn(d_s, keys)
                dq[...] = more if a == 0 else dq[...] + more
                return nn(d_s, q[...]), nn(p.astype(BF), go[...])

            dk1, dv1 = one(q_own, g_own, seg_own, total_own, centre_own, dq_own)
            dk2, dv2 = one(q_sh, g_sh, seg_sh, total_sh, centre_sh, dq_sh)
            dk, dv = dk1 + dk2, dv1 + dv2
            for b in range(2):
                j = 2 * a + b
                rows = slice(TOK * j, TOK * (j + 1))
                part = slice(TOK * b, TOK * (b + 1))
                sbig[j, e, :, 128:256] = turn(dk[part], cosine[rows, :], -sine[rows, :]).astype(BF)
                sbig[j, e, :, 256:384] = dv[part].astype(BF)
                deal(
                    j, places[j][1], me, sbig.at[j, e, :, pl.ds(128, 256)], rbig.at[me, e, :, pl.ds(128, 256)],
                    lambda i, e=e: ss2.at[e, i], lambda i, e=e: rs2.at[e, i],
                )
        for j, where in places:
            rows = slice(TOK * j, TOK * (j + 1))
            extra = dq_sh[TOK * (j // 2) : TOK * (j // 2 + 1), :]
            whole = jnp.where(low, dq_own[rows, :], jnp.where(c == j % 2, extra, 0.0)) * 0.125
            sbig[j, e, :, 0:128] = turn(whole, cosine[rows, :], -sine[rows, :]).astype(BF)
            deal(
                j, where, me, sbig.at[j, e, :, pl.ds(0, 128)], rbig.at[me, e, :, pl.ds(0, 128)],
                lambda i, e=e: ss3.at[e, i], lambda i, e=e: rs3.at[e, i],
            )
        if layer == 0 and e == 0:
            mlp_rest.sum_second()
            attn_first.sum()
            attn_rest.begin()
    for e in range(2):
        for j, where in places:
            dealt(
                j, where, me, sbig.at[j, e, :, pl.ds(128, 256)], rbig.at[j, e, :, pl.ds(128, 256)],
                lambda i, e=e: ss2.at[e, i], lambda i, e=e: rs2.at[e, i],
            )
            dealt(
                j, where, me, sbig.at[j, e, :, pl.ds(0, 128)], rbig.at[j, e, :, pl.ds(0, 128)],
                lambda i, e=e: ss3.at[e, i], lambda i, e=e: rs3.at[e, i],
            )
        for t in range(4):
            q0, k0, v0 = (rbig[2 * t, e, :, 128 * i : 128 * (i + 1)].astype(F32) for i in range(3))
            q1, k1, v1 = (rbig[2 * t + 1, e, :, 128 * i : 128 * (i + 1)].astype(F32) for i in range(3))
            tiles = (
                jnp.where(low, q0, swap(k0)),
                jnp.where(low, v0, swap(q1)),
                jnp.where(low, k1, swap(v1)),
                jnp.where(low, swap(q0 + q1), k0 + k1),
                jnp.where(low, swap(v0 + v1), 0.0),
            )
            for i, tile in enumerate(tiles):
                own_dpj[t, rows_of[e], 128 * i : 128 * (i + 1)] = tile.astype(BF)
    for h in range(2):
        hand(f"dpj{h}", own_dpj.at[2 * h + 1 - c], got_dpj.at[h])
    if layer == 0:
        attn_rest.sum_second()
    dna = jnp.zeros((2 * TOK, D), F32)
    for t in range(4):
        dna = dna + nn(own_dpj[t], attn_rows(wa, t, 0, 640))
    dscale_a = jnp.zeros((1, D), F32)
    dshift_a = jnp.zeros((1, D), F32)
    for e in range(2):
        hat_a, inv_a = normalize(entry(e))
        g = dna[rows_of[e]]
        dscale_a = dscale_a + jnp.sum(g * hat_a, axis=0, keepdims=True)
        dshift_a = dshift_a + jnp.sum(g, axis=0, keepdims=True)
        total = dmid[rows_of[e], :] + norm_back(g * (1.0 + scale_a), hat_a, inv_a)
        din[e] = total
        dinb[e] = total.astype(BF)
    for i, part in enumerate((dshift_a, dscale_a, dgate_a, dshift_b, dscale_b, dgate_b)):
        dmod[i : i + 1, :] = part
    dmod[6:8, :] = jnp.zeros((2, D), F32)

    have("na", "at0", "at1", "dba", "dpj0", "dpj1")
    for h in range(2):
        t = 2 * h + c
        copy = pltpu.make_async_copy(stage_attn, grads.at[h], gsem.at[0])
        if h:
            copy.wait()
        total = tn(own_dpj[t], own_na[...]) + tn(got_dpj[h], got_na[...])
        stage_attn[0:3] = total[0:576].astype(BF).reshape(3, 4, 3, 16, D)
        parts = []
        for first in (0, 512):
            cols = pl.ds(pl.multiple_of(first + 128 * t, 128), 128)
            total = jnp.zeros((128, D), F32)
            for e in range(2):
                total = total + tn(atts[e][:, cols], own_dba[rows_of[e], :])
                total = total + tn(got_at[e, :, cols], got_dba[rows_of[e], :])
            parts.append(total)
        total = jnp.concatenate([parts[0], parts[1][64:128]], axis=0)
        stage_attn[3] = total.astype(BF).reshape(4, 3, 16, D)
        copy.start()
    if layer == 0:
        mlp_rest.sum_third(fin_mlp)
        attn_rest.sum_third(fin_attn)
    mlp_first.sum()
    pltpu.make_async_copy(stage_attn, grads.at[1], gsem.at[0]).wait()


def backward(layer, *operands):
    dma = pltpu.SemaphoreType.DMA
    both = 2 * TOK

    def buf(*dims, dtype=BF):
        return pltpu.VMEM(dims, dtype)

    outs = [
        jax.ShapeDtypeStruct((2, TOK, D), F32),
        jax.ShapeDtypeStruct((2, TOK, D), BF),
        jax.ShapeDtypeStruct((8, D), F32),
        jax.ShapeDtypeStruct((2,) + ATTN, BF),
    ]
    outs += [jax.ShapeDtypeStruct(dims, BF) for dims in ReduceFirst.shapes(MLP_SUM, MLP_ROWS)]
    out_specs = [VM, VM, VM, ANY, VM, VM]
    if layer == 0:
        outs += [jax.ShapeDtypeStruct(dims, BF) for dims in ((3, 16, HALF), (2, 48, HALF))]
        out_specs += [VM, VM]
    else:
        outs.append(jax.ShapeDtypeStruct((2, 2, TOK, D), BF))
        out_specs.append(ANY)
    scratch = [buf(2, *dims, dtype=dtype) for dims, dtype in state_shapes()]
    scratch += [buf(SEQ, 128, dtype=F32)] * 2 + [buf(TOK, D), buf(2, TOK, D), dma((24,))]
    scratch += [buf(both, D)] * 4 + [buf(4, both, D)] * 2 + [buf(4, both, 640)]
    scratch += [buf(both, D)] * 4 + [buf(2, TOK, 1024)] + [buf(2, both, D)] * 2 + [buf(2, both, 640)]
    scratch += [buf(8, 2, TOK, 128)] * 2 + [buf(8, 2, TOK, 384)] * 2
    scratch += [buf(both, D, dtype=F32)] * 2 + [buf(SEQ, 128)] * 2 + [buf(SEQ // 2, 128)] * 2
    scratch += [buf(SEQ, 128, dtype=F32), buf(SEQ // 2, 128, dtype=F32)]
    scratch += [buf(4, *ATTN), buf(2, *MLP), buf(2, *MLP), buf(*ATTN)]
    scratch += [dma((5,)), dma((1,)), dma((8,)), dma((8,)), dma((2, 8)), dma((2, 8)), dma((2, 8)), dma((2, 8)), dma((12,)), dma((12,))]
    scratch += ReduceFirst.scratch(MLP_SUM, MLP_ROWS)
    if layer == 1:
        scratch += [buf(4, TOK, D), dma((4,)), dma((4,))]
    if layer == 0:
        scratch += ReduceRest.scratch(MLP_SUM, MLP_ROWS)
        scratch += [pltpu.VMEM(dims, BF) for dims in ReduceFirst.shapes(ATTN_SUM, ATTN_ROWS)]
        scratch += ReduceFirst.scratch(ATTN_SUM, ATTN_ROWS)
        scratch += ReduceRest.scratch(ATTN_SUM, ATTN_ROWS)
    vmem_in = 6 if layer == 0 else 3
    return pl.pallas_call(
        functools.partial(backward_kernel, layer),
        out_shape=tuple(outs),
        in_specs=[VM] * vmem_in + [ANY] * (len(operands) - vmem_in),
        out_specs=tuple(out_specs),
        scratch_shapes=scratch,
        compiler_params=pltpu.CompilerParams(
            collective_id=2 + layer, has_side_effects=True, vmem_limit_bytes=62 * 2**20
        ),
        name=f"backward_{layer}",
    )(*operands)


def finish_kernel(*refs):
    refs = list(refs)

    def take(count):
        got = refs[:count]
        del refs[:count]
        return got

    shares = take(2)
    fin_a1, fin_m1, dm0, dm1, feat, db0, db1 = take(7)
    (attn_grads,) = take(1)
    out_a0, out_m0, out_a1, out_m1, g_out, rows_out = take(6)
    fin_a0, fin_m0, dm_in, dsum = take(4)
    mlp_rest = ReduceRest(MLP_SUM, shares, take(ReduceRest.count(MLP_SUM)))
    attn_first = ReduceFirst(attn_grads, ATTN_SUM, take(3), take(3), *take(3))
    attn_rest = ReduceRest(ATTN_SUM, attn_first.own, take(ReduceRest.count(ATTN_SUM)))
    ag_a0 = Spread(out_a0, ("xzy", "xyz", "xzy"), *take(2), ring=True)
    ag_m0 = Spread(out_m0, ("zyx", "xzy"), *take(2), ring=True)
    ag_a1 = Spread(out_a1, ("xyz", "xzy", "xyz"), *take(2), ring=True)
    ag_m1 = Spread(out_m1, ("zyx", "yxz"), *take(2), ring=True)
    scattered = Scatter(g_out, *take(2))
    ms, mr, ms2, mr2, fsem = take(5)
    x, ylo, z, yhi, c = here()
    dp = 2 * x + ylo
    places, me = row_places()
    row = 2 * dp + yhi
    others = []
    for o in range(1, 16):
        r = (row + o) % 16
        others.append(dev(r // 4, (r // 2) % 2, z, r % 2, c))
    far = []
    for o in range(1, 8):
        g = (dp + o) % 8
        far += [(g, z, 2 * b + c) for b in range(2)]
    greet(dp_group() + far)()

    def place_in(n, fin, out):
        return pltpu.make_async_copy(fin, out.at[x, z, :, :, half(ylo)], fsem.at[n])

    settled = [place_in(0, fin_m1, out_m1), place_in(1, fin_a1, out_a1)]
    for cp in settled:
        cp.start()
    mlp_rest.begin()
    attn_first.begin()
    for cp in settled:
        cp.wait()
    ag_m1.start(0)
    ag_a1.start(0)
    for j, where in places:

        @pl.when(me != j)
        def _(j=j, where=where):
            push(dm0, dm_in.at[me, 0], ms.at[0, j], mr.at[0, me], where).start()
            push(dm1, dm_in.at[me, 1], ms.at[1, j], mr.at[1, me], where).start()

    mlp_rest.sum_second()
    attn_first.sum()
    attn_rest.begin()

    for j, where in places:

        @pl.when(me != j)
        def _(j=j, where=where):
            for l, ref in enumerate((dm0, dm1)):
                cp = push(ref, dm_in.at[j, l], ms.at[l, j], mr.at[l, j], where)
                cp.wait_send()
                cp.wait_recv()

        @pl.when(me == j)
        def _(j=j):
            dm_in[j, 0] = dm0[...]
            dm_in[j, 1] = dm1[...]

    total = dm_in[0]
    for j in range(1, 8):
        total = total + dm_in[j]
    lane = lax.broadcasted_iota(jnp.int32, (2, 8, D), 1)
    wide = jnp.concatenate([feat[...]] * 6, axis=1)
    high = wide.astype(BF).astype(F32)
    total = jnp.where(lane == 6, high, jnp.where(lane == 7, wide - high, total))
    dsum[...] = total.astype(BF)
    mlp_rest.sum_third(fin_m0)
    done = place_in(0, fin_m0, out_m0)
    done.start()
    attn_rest.sum_second()
    done.wait()
    ag_m0.start(0)
    moved = [push(dsum, rows_out.at[row], ms2.at[o], mr2.at[o], where) for o, where in enumerate(others)]
    for cp in moved:
        cp.start()
    keep = pltpu.make_async_copy(dsum, rows_out.at[row], fsem.at[2])
    keep.start()
    ag_m1.finish()
    ag_m1.start(1)
    ag_a1.finish()
    ag_a1.start(1)
    attn_rest.sum_third(fin_a0)
    done = place_in(1, fin_a0, out_a0)
    done.start()
    done.wait()
    ag_a0.start(0)
    ag_m0.finish()
    ag_m0.start(1)
    ag_a0.finish()
    ag_a0.start(1)
    ag_m1.finish()
    ag_m1.start(2)
    ag_a1.finish()
    ag_a1.start(2)
    ag_m0.finish()
    ag_m0.start(2)
    ag_a0.finish()
    ag_a0.start(2)
    for ag in (ag_m1, ag_a1, ag_m0, ag_a0):
        ag.relay()
    results = (db0.at[0], db1.at[0], db0.at[1], db1.at[1])
    for s in range(4):
        scattered.send(s, results[s], True)
    for ag in (ag_m1, ag_a1, ag_m0, ag_a0):
        ag.finish()
    keep.wait()
    for cp in moved:
        cp.wait()
    for s in range(4):
        scattered.send(s, results[s], False)
        scattered.received(s)


def finish(*operands):
    dma = pltpu.SemaphoreType.DMA
    shapes = [ATTN, MLP, ATTN, MLP, (2, 2, TOK, D)]
    scratch = [
        pltpu.VMEM((3, 16, HALF), BF),
        pltpu.VMEM((2, 48, HALF), BF),
        pltpu.VMEM((8, 2, 8, D), F32),
        pltpu.VMEM((2, 8, D), BF),
    ]
    scratch += ReduceRest.scratch(MLP_SUM, MLP_ROWS)
    scratch += [pltpu.VMEM(dims, BF) for dims in ReduceFirst.shapes(ATTN_SUM, ATTN_ROWS)]
    scratch += ReduceFirst.scratch(ATTN_SUM, ATTN_ROWS)
    scratch += ReduceRest.scratch(ATTN_SUM, ATTN_ROWS)
    scratch += [dma((30,))] * 8 + [dma((4,))] * 2
    scratch += [dma((2, 8)), dma((2, 8)), dma((15,)), dma((15,)), dma((3,))]
    return pl.pallas_call(
        finish_kernel,
        out_shape=tuple(
            [jax.ShapeDtypeStruct(dims, BF) for dims in shapes] + [jax.ShapeDtypeStruct((16, 2, 8, D), BF)]
        ),
        in_specs=[VM] * 9 + [ANY],
        out_specs=(ANY,) * 6,
        scratch_shapes=scratch,
        compiler_params=pltpu.CompilerParams(
            collective_id=4, has_side_effects=True, vmem_limit_bytes=62 * 2**20
        ),
        name="finish",
    )(*operands)


def modulation_kernel(rows, grad_mod, grad_bias):
    features = jnp.concatenate([rows[:, 0, 6, 0:128], rows[:, 0, 7, 0:128]], axis=0)
    for l in range(2):
        for i in range(6):
            cols = slice(D * i, D * (i + 1))
            d = rows[:, l, i, :]
            grad_mod[l, :, cols] = tn(features, jnp.concatenate([d, d], axis=0))
            grad_bias[l : l + 1, cols] = jnp.sum(d.astype(F32), axis=0, keepdims=True)


def modulation_grads(rows):
    return pl.pallas_call(
        modulation_kernel,
        out_shape=(
            jax.ShapeDtypeStruct((2, 128, 6 * D), F32),
            jax.ShapeDtypeStruct((2, 6 * D), F32),
        ),
        in_specs=[VM],
        out_specs=(VM, VM),
        compiler_params=pltpu.CompilerParams(vmem_limit_bytes=30 * 2**20),
        name="modulation_grads",
    )(rows)


def rotary(count):
    frequency = np.exp(-np.log(10000.0) * np.arange(32) / 32)
    angles = np.arange(count)[:, None] * frequency[None, :]
    cos, sin = np.cos(angles), np.sin(angles)
    return (
        np.concatenate([cos] * 4, axis=1).astype(np.float32),
        np.concatenate([-sin, sin, -sin, sin], axis=1).astype(np.float32),
    )


def time_features(step_values, feature_count):
    half_count = feature_count // 2
    frequency = jnp.exp(-np.log(10000.0) * jnp.arange(half_count, dtype=F32) / half_count)
    angles = step_values.astype(F32)[:, None] * frequency[None, :]
    return jnp.concatenate([jnp.cos(angles), jnp.sin(angles)], axis=1)


def on_device(hidden_in, segments, timestep, w_qkv, w_out, w_up, w_down, w_mod, b_mod, cotangent):
    x, ylo, z, yhi, c = here()
    attn_loc = jnp.concatenate([jnp.swapaxes(w_qkv, 1, 2), w_out], axis=1).reshape((2,) + ATTN)
    up_loc = w_up.reshape(2, 2, 4, 2, 48, D)
    down_loc = w_down.reshape(2, 2, 4, 2, 48, D)

    mine = lax.dynamic_slice_in_dim(timestep, yhi, 1, 0)
    features = time_features(mine, w_mod.shape[1])
    modulation = jnp.einsum(
        "rf,lfm->lrm", features, w_mod.astype(F32), precision=highest
    ) + b_mod.astype(F32)[:, None, :]
    modulation = modulation.reshape(2, 6, D)
    seg = lax.dynamic_slice_in_dim(segments, yhi, 1, 0)
    segc, segr = seg.reshape(SEQ, 1), seg
    cosine, sine = (jnp.asarray(v) for v in rotary(SEQ))

    *state, x0, cots, wa0, wm0, wa1, wm1 = forward(
        hidden_in.reshape(2, 2, TOK, D),
        cotangent.reshape(2, 2, TOK, D),
        modulation,
        segc,
        segr,
        cosine,
        sine,
        attn_loc,
        up_loc,
        down_loc,
    )
    known = (cosine, sine, x0, cots, *state)
    din1, dinb1, dm1, ga1, *shares1, y_out = backward(1, modulation, segc, segr, *known, wa1, wm1)
    _, dinb0, dm0, ga0, *shares0, fin_a1, fin_m1 = backward(
        0, modulation, segc, segr, din1, *shares1, *known, wa0, wm0, ga1
    )
    out_a0, out_m0, out_a1, out_m1, g_out, rows = finish(
        *shares0, fin_a1, fin_m1, dm0, dm1, features, dinb0, dinb1, ga0
    )
    grad_mod, grad_bias = modulation_grads(rows)

    attn = jnp.stack([out_a0, out_a1]).reshape(2, D, D)
    mlp = jnp.stack([out_m0, out_m1]).reshape(2, 2 * D, D)
    return (
        y_out.reshape(1, 2, 2 * TOK, D),
        g_out.reshape(1, 2, 2 * TOK, D).astype(F32),
        attn[:, 0:576].swapaxes(1, 2).astype(F32),
        attn[:, 576:768].astype(F32),
        mlp[:, 0:768].astype(F32),
        mlp[:, 768:1536].astype(F32),
        grad_mod,
        grad_bias,
    )


def solution(mesh):
    placed = (
        P("dp", "tensor", None),
        P("dp", None),
        P("dp"),
        P(None, None, "tensor"),
        P(None, "tensor", None),
        P(None, None, "tensor"),
        P(None, "tensor", None),
        P(),
        P(),
        P("section", "dp", "tensor", None),
    )
    return jax.shard_map(
        on_device,
        mesh=mesh,
        in_specs=placed,
        out_specs=(
            P("section", "dp", "tensor", None),
            P("section", "dp", "tensor", None),
            P(None, None, "tensor"),
            P(None, "tensor", None),
            P(None, None, "tensor"),
            P(None, "tensor", None),
            P(),
            P(),
        ),
        check_vma=False,
    )
```

```python
import functools

import jax
import jax.numpy as jnp
import numpy as np
from jax import lax
from jax.experimental import pallas as pl
from jax.experimental.pallas import tpu as pltpu
from jax.sharding import PartitionSpec as P

MESH = pl.DeviceIdType.MESH
BF = jnp.bfloat16
F32 = jnp.float32
highest = lax.Precision.HIGHEST
EPS = 1e-06
D = 768
TOK = 128
SEQ = 1024
ANY = pl.BlockSpec(memory_space=pl.ANY)
VM = pl.BlockSpec(memory_space=pltpu.VMEM)
HALF = 384
ATTN = (4, 4, 3, 16, D)
MLP = (4, 4, 2, 48, D)


def here():
    dp = lax.axis_index("dp")
    t = lax.axis_index("tensor")
    return dp // 2, dp % 2, lax.axis_index("section"), t // 2, t % 2


def dev(x, ylo, z, yhi, c):
    return (2 * x + ylo, z, 2 * yhi + c)


def push(src, dst, send_sem, recv_sem, where):
    return pltpu.make_async_remote_copy(
        src_ref=src,
        dst_ref=dst,
        send_sem=send_sem,
        recv_sem=recv_sem,
        device_id=where,
        device_id_type=MESH,
    )


def greet(devices):
    barrier = pltpu.get_barrier_semaphore()
    for where in devices:
        pl.semaphore_signal(barrier, inc=1, device_id=where, device_id_type=MESH)
    return lambda: pl.semaphore_wait(barrier, len(devices))


def nn(a, b):
    return lax.dot_general(a, b, (((1,), (0,)), ((), ())), preferred_element_type=F32)


def nt(a, b):
    return lax.dot_general(a, b, (((1,), (1,)), ((), ())), preferred_element_type=F32)


def tn(a, b):
    return lax.dot_general(a, b, (((0,), (0,)), ((), ())), preferred_element_type=F32)


def normalize(values):
    centred = values - jnp.mean(values, axis=-1, keepdims=True)
    inverse = lax.rsqrt(jnp.mean(centred * centred, axis=-1, keepdims=True) + EPS)
    return centred * inverse, inverse


def norm_back(gradient, normed, inverse):
    return inverse * (
        gradient
        - jnp.mean(gradient, axis=-1, keepdims=True)
        - normed * jnp.mean(gradient * normed, axis=-1, keepdims=True)
    )


def lanes(shape):
    return lax.broadcasted_iota(jnp.int32, shape, len(shape) - 1)


def swap(x):
    return pltpu.roll(x, 64, 1)


def turn(x, cosine, sine):
    low = (lanes(x.shape) % 64) < 32
    other = jnp.where(low, pltpu.roll(x, 96, 1), pltpu.roll(x, 32, 1))
    return x * cosine + other * sine


def half(ylo):
    return pl.ds(pl.multiple_of(HALF * ylo, 128), HALF)


class Spread:
    def __init__(self, buf, orders, ss, rs, ring=False):
        self.buf, self.orders, self.ss, self.rs, self.ring = buf, orders, ss, rs, ring
        self.sent, self.rest, self.relays = [], [], []

    def at(self, dims, part, by, cols=None):
        x, ylo, z, yhi, c = here()
        everything = slice(None)
        i = everything if "x" in dims else by.get("x", x)
        j = everything if "z" in dims else by.get("z", z)
        k = cols if cols is not None else everything if "y" in dims else half(by.get("y", ylo))
        return self.buf.at[i, j, part, :, k]

    def peer(self, dim, o):
        x, ylo, z, yhi, c = here()
        if dim == "y":
            return dev(x, 1 - ylo, z, yhi, c), 1 - ylo
        if dim == "x":
            return dev((x + o) % 4, ylo, z, yhi, c), (x - o + 4) % 4
        return dev(x, ylo, (z + o) % 4, yhi, c), (z - o + 4) % 4

    def start(self, phase):
        self.sent, self.rest, self.relays = [], [], []
        for part in range(len(self.orders)):
            dim, done = self.orders[part][phase], self.orders[part][:phase]
            ring = self.ring and phase == 2 and dim != "y"
            for o in (1, 3) if ring else (1,) if dim == "y" else (2, 1, 3):
                where, origin = self.peer(dim, o)
                n = (phase * 3 + part) * 3 + o - 1
                here_now = self.at(done, part, {})
                cp = push(here_now, here_now, self.ss.at[n], self.rs.at[n], where)
                cp.start()
                self.sent.append(cp)
                back = self.at(done, part, {dim: origin})
                got = push(back, back, self.ss.at[n], self.rs.at[n], where), back
                if ring:
                    self.relays.append((part, dim, done, o, got))
                else:
                    self.rest.append(got)

    def relay(self, each=None):
        x, ylo, z, yhi, c = here()
        for part, dim, done, o, (cp, back) in self.relays:
            cp.wait_recv()
            if each is not None:
                each(back)
            where, origin = self.peer(dim, o)
            cols = pl.ds(0 if o == 1 else HALF, HALF)
            n = (2 * 3 + part) * 3 + 1 if o == 1 else 27 + part
            ref = self.at(done, part, {dim: origin}, cols)
            cp = push(ref, ref, self.ss.at[n], self.rs.at[n], where)
            cp.start()
            self.sent.append(cp)
            far = self.at(done, part, {dim: ((x if dim == "x" else z) + 2) % 4}, cols)
            self.rest.append((push(far, far, self.ss.at[n], self.rs.at[n], where), far))
        self.relays = []

    def finish(self, each=None):
        self.relay(each)
        for cp, back in self.rest:
            cp.wait_recv()
            if each is not None:
                each(back)
        for cp in self.sent:
            cp.wait_send()

    def held(self):
        return [self.at(self.orders[p][:2], p, {}) for p in range(len(self.orders))]


class Gather:
    def __init__(self, wv, pieces, orders, ss, rs, ps, pr, ls):
        x, ylo, z, yhi, c = here()
        self.wv, self.pieces = wv, pieces
        self.ps, self.pr, self.ls = ps, pr, ls
        self.t = 2 * yhi + c
        self.other = 2 * (1 - yhi) + c
        self.partner = dev(x, ylo, z, yhi, 1 - c)
        self.cross = dev(x, 1 - ylo, z, 1 - yhi, c)
        self.spread = Spread(wv.at[self.other], orders, ss, rs)
        self.handed = []

    def side(self, n):
        ref, first = self.pieces[n]
        spot = self.wv.at[self.t, pl.ds(first, ref.shape[0])]
        return (
            pltpu.make_async_copy(ref, spot, self.ls.at[n]),
            push(ref, spot, self.ps.at[n], self.pr.at[n], self.partner),
        )

    def s0(self):
        x, ylo, z, yhi, c = here()
        for ref, first in self.pieces:

            @pl.when((x >= first) & (x < first + ref.shape[0]))
            def _(ref=ref, first=first):
                push(
                    ref.at[x - first, z, :, :, half(1 - ylo)],
                    self.wv.at[self.t, x, z, :, :, half(1 - ylo)],
                    self.ps.at[2],
                    self.pr.at[2],
                    self.cross,
                ).start()

    def beside(self):
        for n in range(len(self.pieces)):
            for cp in self.side(n):
                cp.start()

    def s1(self):
        x, ylo, z, yhi, c = here()
        landed = self.wv.at[self.other, x, z, :, :, half(ylo)]
        cp = push(landed, landed, self.ps.at[2], self.pr.at[2], self.cross)
        cp.wait_recv()
        cp.wait_send()
        self.spread.start(0)

    def s2(self):
        self.spread.finish()
        self.spread.start(1)

    def hand(self, ref):
        n = 3 + len(self.handed)
        cp = push(ref, ref, self.ps.at[n], self.pr.at[n], self.partner)
        cp.start()
        self.handed.append(cp)

    def s3(self):
        self.spread.finish()
        self.spread.start(2)
        for ref in self.spread.held():
            self.hand(ref)

    def s4(self):
        self.spread.finish(self.hand)

    def own(self):
        for n in range(len(self.pieces)):
            local, cp = self.side(n)
            local.wait()
            cp.wait_send()
            cp.wait_recv()

    def s5(self):
        for cp in self.handed:
            cp.wait_send()
            cp.wait_recv()


def gather_scratch():
    dma = pltpu.SemaphoreType.DMA
    return [dma((30,)), dma((30,)), dma((16,)), dma((16,)), dma((2,))]


def chips_around():
    x, ylo, z, yhi, c = here()
    return [dev((x + o) % 4, ylo, z, yhi, c) for o in (1, 2, 3)] + [
        dev(x, 1 - ylo, z, yhi, c),
        dev(x, 1 - ylo, z, 1 - yhi, c),
    ]


def dp_group():
    x, ylo, z, yhi, c = here()
    t = 2 * yhi + c
    return [(2 * x + ylo, (z + a) % 4, (t + b) % 4) for a in range(4) for b in range(4) if a or b]


def row_places():
    x, ylo, z, yhi, c = here()
    return [(2 * a + b, dev(x, ylo, a, yhi, b)) for a in range(4) for b in range(2)], 2 * z + c


def row_mates():
    x, ylo, z, yhi, c = here()
    me = 2 * z + c
    return [dev(x, ylo, ((me + o) % 8) // 2, yhi, (me + o) % 2) for o in range(1, 8)]


def deal(j, where, me, src, dst, s, r):
    @pl.when(me != j)
    def _():
        push(src, dst, s(j), r(me), where).start()

    @pl.when(me == j)
    def _():
        dst[...] = src[...]


def dealt(j, where, me, src, dst, s, r):
    @pl.when(me != j)
    def _():
        cp = push(src, dst, s(j), r(j), where)
        cp.wait_send()
        cp.wait_recv()


def place_of(sem):
    return lambda j: sem.at[j]


def attn_rows(wa, t, low, high):
    first, last = low // 192, -(-high // 192)
    whole = wa[t, first:last].reshape(192 * (last - first), D)
    return whole[low - 192 * first : high - 192 * first]


def up_rows(wt):
    return wt[0:2].reshape(D, D)


def down_rows(wt):
    return wt[2:4].reshape(D, D)


def holder():
    x, ylo, z, yhi, c = here()
    return 2 * c + z // 2


class Tokens:
    def __init__(self, hid, x0, hs, hr, ls):
        self.refs = hid, x0, hs, hr, ls

    def start(self):
        hid, x0, hs, hr, ls = self.refs
        x, ylo, z, yhi, c = here()
        t = 2 * yhi + c
        for b in range(2):
            to = 2 * b + yhi

            @pl.when((c == z // 2) & (t != to))
            def _(b=b, to=to):
                push(hid.at[b, z % 2], x0, hs.at[b], hr.at[0], (2 * x + ylo, z, to)).start()

            @pl.when((c == z // 2) & (t == to))
            def _(b=b):
                pltpu.make_async_copy(hid.at[b, z % 2], x0, ls.at[0]).start()

    def arrive(self):
        hid, x0, hs, hr, ls = self.refs
        x, ylo, z, yhi, c = here()
        t = 2 * yhi + c

        @pl.when(t != holder())
        def _():
            push(x0, x0, hs.at[0], hr.at[0], (2 * x + ylo, z, (t + 1) % 4)).wait_recv()

        @pl.when(t == holder())
        def _():
            pltpu.make_async_copy(hid.at[0, 0], x0, ls.at[0]).wait()

    def sent(self):
        hid, x0, hs, hr, ls = self.refs
        x, ylo, z, yhi, c = here()
        t = 2 * yhi + c
        for b in range(2):
            to = 2 * b + yhi

            @pl.when((c == z // 2) & (t != to))
            def _(b=b, to=to):
                push(hid.at[b, z % 2], x0, hs.at[b], hr.at[0], (2 * x + ylo, z, to)).wait_send()


class Cotangents:
    def __init__(self, cot, cots, over, cs, cr, ls):
        self.refs = cot, cots, over, cs, cr, ls

    def load(self, begin):
        cot, cots, over, cs, cr, ls = self.refs
        x, ylo, z, yhi, c = here()

        @pl.when(2 * yhi + c == holder())
        def _():
            cp = pltpu.make_async_copy(cot.at[yhi, z % 2], over, ls.at[0])
            if begin:
                cp.start()
            else:
                cp.wait()

    def move(self, step, begin):
        cot, cots, over, cs, cr, ls = self.refs
        x, ylo, z, yhi, c = here()
        t = 2 * yhi + c
        dp = 2 * x + ylo
        b, h = (step + z) % 4 // 2, (step + z) % 2
        section, to = 2 * c + h, 2 * b + yhi

        @pl.when((section != z) | (to != t))
        def _():
            cp = push(cot.at[b, h], cots.at[z], cs.at[step], cr.at[z], (dp, section, to))
            if begin:
                cp.start()
            else:
                cp.wait_send()

        @pl.when((section == z) & (to == t))
        def _():
            cp = pltpu.make_async_copy(over, cots.at[z], ls.at[1])
            if begin:
                cp.start()
            else:
                cp.wait()

        if not begin:

            @pl.when((holder() != t) | (z != step))
            def _():
                spot = cots.at[step]
                push(spot, spot, cs.at[step], cr.at[step], (dp, z, (t + 1) % 4)).wait_recv()


class Scatter:
    def __init__(self, dst, s_sem, r_sem):
        self.dst, self.s_sem, self.r_sem = dst, s_sem, r_sem

    def send(self, s, src, begin):
        x, ylo, z, yhi, c = here()
        t = 2 * yhi + c
        mine = (z == s) & (t == holder())
        spot = self.dst.at[yhi, z % 2]

        @pl.when(jnp.logical_not(mine))
        def _():
            where = (2 * x + ylo, s, holder())
            cp = push(src, spot, self.s_sem.at[s], self.r_sem.at[2 * yhi + z % 2], where)
            if begin:
                cp.start()
            else:
                cp.wait_send()

        @pl.when(mine)
        def _():
            cp = pltpu.make_async_copy(src, spot, self.s_sem.at[s])
            if begin:
                cp.start()
            else:
                cp.wait()

    def received(self, s):
        x, ylo, z, yhi, c = here()
        t = 2 * yhi + c
        for b in range(2):
            for h in range(2):

                @pl.when((z == s) & ((yhi != b) | (c != yhi) | (z != 2 * c + h)))
                def _(b=b, h=h):
                    spot = self.dst.at[b, h]
                    where = (2 * x + ylo, z, (t + 1) % 4)
                    n = 2 * b + h
                    push(spot, spot, self.s_sem.at[n], self.r_sem.at[n], where).wait_recv()


STATE = ("y", "qkv", "lse", "att", "ba", "mid", "pre", "bb", "o")


def state_shapes():
    return (
        ((TOK, D), BF),
        ((8, TOK, 384), BF),
        ((4, 8, 384), F32),
        ((TOK, 1024), BF),
        ((TOK, D), F32),
        ((TOK, D), F32),
        ((TOK, 4 * D), F32),
        ((TOK, D), F32),
        ((8, TOK, 128), BF),
    )


def forward_kernel(*refs):
    refs = list(refs)

    def take(count):
        got = refs[:count]
        del refs[:count]
        return got

    hid, cot, mods, segc, segr, cosine, sine, attn_loc, up_loc, down_loc = take(10)
    outs = dict(zip(STATE, take(9)))
    x0, cots, *weights_out = take(6)
    held = dict(zip(STATE, take(9)))
    sbuf, rbuf, cos_ref, sin_ref, wa0, wa1, wm0, wm1 = take(8)
    wsem, ksem, ss, rs, ss2, rs2 = take(6)
    x, ylo, z, yhi, c = here()
    places, me = row_places()
    saved = []

    def save(src, dst):
        cp = pltpu.make_async_copy(src, dst, wsem.at[len(saved)])
        cp.start()
        saved.append(cp)

    beside = ("zyx", "zxy")
    a0 = Gather(wa0, [(attn_loc.at[0], 0)], ("zyx", "xzy", "yxz"), *take(5))
    m0 = Gather(wm0, [(up_loc.at[0], 0), (down_loc.at[0], 2)], beside, *take(5))
    a1 = Gather(wa1, [(attn_loc.at[1], 0)], ("zyx", "zxy", "zyx"), *take(5))
    m1 = Gather(wm1, [(up_loc.at[1], 0), (down_loc.at[1], 2)], beside, *take(5))
    tokens = Tokens(hid, x0, *take(3))
    cotangents = Cotangents(cot, cots, *take(4))
    mine = pl.ds(pl.multiple_of(TOK * me, TOK), TOK)
    tables = [
        pltpu.make_async_copy(cosine.at[mine], cos_ref, wsem.at[4]),
        pltpu.make_async_copy(sine.at[mine], sin_ref, wsem.at[5]),
    ]
    for cp in tables:
        cp.start()
    greet(dp_group() + chips_around())()
    for gather in (a0, m0, a1, m1):
        gather.s0()
    a0.beside()
    tokens.start()
    cotangents.load(True)
    a0.s1()
    a0.s2()
    m0.s1()
    a0.s3()
    m0.beside()
    tokens.arrive()

    for cp in tables:
        cp.wait()
    cos_here, sin_here = cos_ref[...], sin_ref[...]
    low = lanes((TOK, 128)) < 64
    seg_keys = segr[...]

    def flat(column):
        wide = jnp.broadcast_to(column, (column.shape[0], 128))
        return jnp.transpose(wide)[0:8, :]

    def keeping(app):
        slot = app % 2
        return [
            pltpu.make_async_copy(held[name].at[app if name == "y" else slot], outs[name].at[app], ksem.at[slot, n])
            for n, name in enumerate(STATE)
        ]

    for app in range(4):
        slot = app % 2
        wa, wm = ((wa0, wm0), (wa1, wm1))[slot]
        mod = mods.at[slot]
        qkv, lse, att, ba, mid, pre, bb, obuf = (held[name].at[slot] for name in STATE[1:])
        if app == 0:
            v = x0[...].astype(F32)
        else:
            v = held["y"][app - 1].astype(F32)
            if app == 2:
                v = v + x0[...].astype(F32)
        hat, _ = normalize(v)
        normed = (hat * (1.0 + mod[1:2, :]) + mod[0:1, :]).astype(BF)
        if app == 0:
            a0.own()
        if app == 1:
            a1.s4()
            m1.s2()
            a1.own()
            a1.s5()
            save(wa1, weights_out[2])
        for i in range(4):
            if app == 0 and i == 2:
                a0.s4()
                m0.s2()
                a0.s5()
                save(wa0, weights_out[0])
            t = (2 * yhi + i) % 4
            got = nt(normed, attn_rows(wa, t, 0, 640))
            t0, t1, t2, t3, t4 = (got[:, 128 * n : 128 * (n + 1)] for n in range(5))
            s0, s1, s2, s3, s4 = (swap(u) for u in (t0, t1, t2, t3, t4))
            for head, (q, k, w) in enumerate(
                (
                    (jnp.where(low, t0, s3), jnp.where(low, s0, t3), jnp.where(low, t1, s4)),
                    (jnp.where(low, s1, s3), jnp.where(low, t2, t3), jnp.where(low, s2, s4)),
                )
            ):
                j = 2 * t + head
                sbuf[j, :, 0:128] = (turn(q, cos_here, sin_here).astype(BF).astype(F32) * 0.125).astype(BF)
                sbuf[j, :, 128:256] = turn(k, cos_here, sin_here).astype(BF)
                sbuf[j, :, 256:384] = w.astype(BF)
                where = dev(x, ylo, t, yhi, head)
                deal(j, where, me, sbuf.at[j], qkv.at[me], place_of(ss.at[app]), place_of(rs.at[app]))
        if app == 0:
            a1.beside()
            m0.s3()
            a1.s1()
        if app == 1:
            m1.s3()
        for j, where in places:
            dealt(j, where, me, sbuf.at[j], qkv.at[j], place_of(ss.at[app]), place_of(rs.at[app]))
        if app:
            for cp in keeping(app - 1):
                cp.wait()

        if app == 0:
            a1.s2()
            m1.beside()

        keys = qkv[:, :, 128:256].reshape(SEQ, 128)
        values = qkv[:, :, 256:384].reshape(SEQ, 128)

        def softmax(q, seg_q, keys=keys, values=values):
            scores = jnp.where(seg_q == seg_keys, nt(q, keys), -1e30)
            largest = jnp.max(scores, axis=-1, keepdims=True)
            raised = jnp.exp(scores - largest)
            total = jnp.sum(raised, axis=-1, keepdims=True)
            mixed = nn(raised.astype(BF), values) * (1.0 / total)
            return mixed, largest + jnp.log(total)

        for a in range(4):
            q = qkv[2 * a : 2 * a + 2, :, 0:128].reshape(256, 128)
            q = jnp.where(lanes((256, 128)) < 64, q, 0).astype(BF)
            mixed, total = softmax(q, segc[256 * a : 256 * (a + 1), :])
            q2 = jnp.where(low, 0, qkv[2 * a + c, :, 0:128]).astype(BF)
            mixed2, total2 = softmax(q2, segc[pl.ds(256 * a + TOK * c, TOK), :])
            lse[a, :, 0:256] = flat(total)
            lse[a, :, 256:384] = flat(total2)
            for b in range(2):
                j = 2 * a + b
                part = mixed[TOK * b : TOK * (b + 1)]
                obuf[j] = jnp.where(low | (c != b), part, mixed2).astype(BF)
                deal(j, places[j][1], me, obuf.at[j], rbuf.at[me], place_of(ss2.at[app]), place_of(rs2.at[app]))
        if app == 0:
            a1.s3()
        for j, where in places:
            dealt(j, where, me, obuf.at[j], rbuf.at[j], place_of(ss2.at[app]), place_of(rs2.at[app]))

        if app == 0:
            cotangents.load(False)
        cotangents.move(app, True)
        branch_a = jnp.zeros((TOK, D), F32)
        for t in range(4):
            first, second = rbuf[2 * t], rbuf[2 * t + 1]
            own = jnp.where(low, first.astype(F32), swap(second.astype(F32))).astype(BF)
            extra = jnp.where(low, 0, rbuf[2 * t + c]).astype(BF)
            att[:, 128 * t : 128 * (t + 1)] = own
            att[:, 512 + 128 * t : 512 + 128 * (t + 1)] = extra
            branch_a = branch_a + nn(own, attn_rows(wa, t, 576, 704)) + nn(extra, attn_rows(wa, t, 640, 768))
        ba[...] = branch_a
        middle = v + mod[2:3, :] * branch_a
        mid[...] = middle
        hat_b, _ = normalize(middle)
        normed_b = (hat_b * (1.0 + mod[4:5, :]) + mod[3:4, :]).astype(BF)
        if app == 0:
            m0.s4()
            m0.own()
            m0.s5()
            save(wm0, weights_out[1])
            m1.s1()
        if app == 1:
            m1.s4()
            m1.own()
            m1.s5()
            save(wm1, weights_out[3])
        total_b = jnp.zeros((TOK, D), F32)
        for t in range(4):
            before = nn(normed_b, up_rows(wm.at[t]))
            pre[:, D * t : D * (t + 1)] = before
            total_b = total_b + nn(jax.nn.gelu(before, approximate=True).astype(BF), down_rows(wm.at[t]))
        bb[...] = total_b
        held["y"][app] = (middle + mod[5:6, :] * total_b).astype(BF)
        for cp in keeping(app):
            cp.start()
    for b in range(4):
        cotangents.move(b, False)
    tokens.sent()
    for cp in keeping(3) + saved:
        cp.wait()


def forward(*operands):
    dma = pltpu.SemaphoreType.DMA
    outs = [jax.ShapeDtypeStruct((4,) + dims, dtype) for dims, dtype in state_shapes()]
    outs += [jax.ShapeDtypeStruct(dims, BF) for dims in ((TOK, D), (4, TOK, D))]
    outs += [jax.ShapeDtypeStruct((4,) + group, BF) for group in (ATTN, MLP, ATTN, MLP)]
    scratch = [pltpu.VMEM((2,) + dims, dtype) for dims, dtype in state_shapes()]
    scratch[0] = pltpu.VMEM((4, TOK, D), BF)
    scratch += [
        pltpu.VMEM((8, TOK, 384), BF),
        pltpu.VMEM((8, TOK, 128), BF),
        pltpu.VMEM((TOK, 128), F32),
        pltpu.VMEM((TOK, 128), F32),
    ]
    scratch += [pltpu.VMEM((4,) + group, BF) for group in (ATTN, ATTN, MLP, MLP)]
    scratch += [dma((6,)), dma((2, 9))] + [dma((4, 8))] * 4
    for _ in range(4):
        scratch += gather_scratch()
    scratch += [dma((4,)), dma((1,)), dma((1,))]
    scratch += [pltpu.VMEM((TOK, D), BF), dma((4,)), dma((4,)), dma((2,))]
    return pl.pallas_call(
        forward_kernel,
        out_shape=tuple(outs),
        in_specs=[ANY] * 2 + [VM] * 3 + [ANY] * 5,
        out_specs=tuple([ANY] * 9 + [VM] + [ANY] * 5),
        scratch_shapes=scratch,
        compiler_params=pltpu.CompilerParams(
            collective_id=1, has_side_effects=True, vmem_limit_bytes=62 * 2**20
        ),
        name="forward",
    )(*operands)


def across(dim, o):
    x, ylo, z, yhi, c = here()
    if dim == "x":
        to = (x + o) % 4
        return dev(to, ylo, z, yhi, c), to
    if dim == "z":
        to = (z + o) % 4
        return dev(x, ylo, to, yhi, c), to
    to = (2 * yhi + ylo + o) % 4
    return dev(x, to % 2, z, to // 2, c), to


def own_place(dim):
    x, ylo, z, yhi, c = here()
    return {"x": x, "z": z, "y": 2 * yhi + ylo}[dim]


def reduce_greeted():
    return [across(dim, o)[0] for dim in "xy" for o in (1, 2, 3)]


def left(order, steps):
    return [label for label in "Yxz" if label.lower() not in order[:steps]]


def block(order, steps, rows):
    sizes = {"Y": 2, "x": 4, "z": 4}
    lane_count = HALF if "y" in order[:steps] else D
    return tuple(sizes[label] for label in left(order, steps)) + (rows, lane_count)


def pick(labels, dim, to):
    index = [slice(None)] * len(labels)
    if dim == "y":
        index[labels.index("Y")] = to // 2
        return tuple(index), half(to % 2)
    index[labels.index(dim)] = to
    return tuple(index), slice(None)


def each_unit(dims, body):
    count = 1
    for size in dims:
        count *= size

    def step(i, carry):
        index, rest = [], i
        for size in reversed(dims):
            index.append(rest % size)
            rest = rest // size
        body(tuple(reversed(index)))
        return carry

    lax.fori_loop(0, count, step, 0)


class ReduceFirst:
    def __init__(self, grads, orders, own, arrived, ls, ss, rs):
        self.grads, self.orders, self.own, self.arrived = grads, orders, own, arrived
        self.ls, self.ss, self.rs = ls, ss, rs

    def source(self, p, to):
        index, cols = pick(["Y", "x", "z"], self.orders[p][0], to)
        return self.grads.at[index + (p, slice(None), cols)]

    def copies(self):
        found = []
        if self.ls is not None:
            for p, order in enumerate(self.orders):
                found.append(pltpu.make_async_copy(self.source(p, own_place(order[0])), self.own[p], self.ls.at[p]))
        for o in (2, 1, 3):
            for p, order in enumerate(self.orders):
                where, to = across(order[0], o)
                n = 3 * p + o - 1
                found.append(push(self.source(p, to), self.arrived[p].at[o - 1], self.ss.at[n], self.rs.at[n], where))
        return found

    def begin(self):
        for cp in self.copies():
            cp.start()

    def sum(self):
        for cp in self.copies():
            cp.wait()
        for p in range(len(self.orders)):
            own, arrived = self.own[p], self.arrived[p]
            mine = own if self.ls is not None else self.source(p, own_place(self.orders[p][0]))

            def body(index, own=own, arrived=arrived, mine=mine):
                total = mine[index].astype(F32)
                for n in range(3):
                    total = total + arrived[(n,) + index].astype(F32)
                own[index] = total.astype(BF)

            each_unit(own.shape[:-2], body)

    @staticmethod
    def shapes(orders, rows):
        return [block(order, 1, rows) for order in orders]

    @staticmethod
    def scratch(orders, rows):
        dma = pltpu.SemaphoreType.DMA
        arrived = [pltpu.VMEM((3,) + dims, BF) for dims in ReduceFirst.shapes(orders, rows)]
        return arrived + [dma((3,)), dma((9,)), dma((9,))]


class ReduceRest:
    def __init__(self, orders, own, refs):
        refs = list(refs)
        count = len(orders)
        self.orders, self.own = orders, own
        self.mid, self.tot, self.end = refs[:count], refs[count : 2 * count], refs[2 * count : 3 * count]
        self.ss2, self.rs2, self.ss3, self.rs3 = refs[3 * count :]

    @staticmethod
    def scratch(orders, rows):
        dma = pltpu.SemaphoreType.DMA
        shapes = [pltpu.VMEM((3,) + block(order, 2, rows), BF) for order in orders]
        shapes += [pltpu.VMEM(block(order, 2, rows), BF) for order in orders]
        shapes += [pltpu.VMEM((3,) + block(order, 3, rows), BF) for order in orders]
        return shapes + [dma((9,))] * 4

    @staticmethod
    def count(orders):
        return 3 * len(orders) + 4

    def copies(self, step):
        found = []
        sources, targets = (self.own, self.mid) if step == 1 else (self.tot, self.end)
        send, recv = (self.ss2, self.rs2) if step == 1 else (self.ss3, self.rs3)
        for o in (2, 1, 3):
            for p, order in enumerate(self.orders):
                where, to = across(order[step], o)
                index, cols = pick(left(order, step), order[step], to)
                n = 3 * p + o - 1
                found.append(
                    push(sources[p].at[index + (slice(None), cols)], targets[p].at[o - 1], send.at[n], recv.at[n], where)
                )
        return found

    def begin(self):
        for cp in self.copies(1):
            cp.start()

    def sum_second(self):
        for cp in self.copies(1):
            cp.wait()
        for p, order in enumerate(self.orders):
            own, mid, tot = self.own[p], self.mid[p], self.tot[p]
            labels = left(order, 1)
            index, cols = pick(labels, order[1], own_place(order[1]))
            free = [n for n, value in enumerate(index) if isinstance(value, slice)]
            for i in range(tot.shape[0]):
                spot = list(index)
                spot[free[0]] = i
                total = own[tuple(spot) + (slice(None), cols)].astype(F32)
                for n in range(3):
                    total = total + mid[n, i].astype(F32)
                tot[i] = total.astype(BF)
        for cp in self.copies(2):
            cp.start()

    def sum_third(self, fin):
        for cp in self.copies(2):
            cp.wait()
        for p, order in enumerate(self.orders):
            index, cols = pick(left(order, 2), order[2], own_place(order[2]))
            total = self.tot[p][index + (slice(None), cols)].astype(F32)
            for n in range(3):
                total = total + self.end[p][n].astype(F32)
            fin[p] = total.astype(BF)


MLP_SUM = ("xyz", "yxz")
ATTN_SUM = ("xyz", "yzx", "zxy")
MLP_ROWS, ATTN_ROWS = 48, 16


def gelu_parts(u):
    k = 0.7978845608028654
    square = u * u
    th = jnp.tanh(k * u * (1.0 + 0.044715 * square))
    half_up = 0.5 * (1.0 + th)
    slope = half_up + 0.5 * u * (1.0 - th * th) * (k * (1.0 + 0.134145 * square))
    return u * half_up, slope


def backward_kernel(layer, *refs):
    refs = list(refs)

    def take(count):
        got = refs[:count]
        del refs[:count]
        return got

    mods, segc, segr = take(3)
    more_dy, *last_shares = take(3) if layer == 0 else [None]
    cosine_in, sine_in, x0_in, cots_in = take(4)
    outer = dict(zip(STATE, take(9)))
    wa_in, wm_in = take(2)
    before = take(1)[0] if layer == 0 else None
    din, dinb, dmod, grads, *shares = take(6)
    if layer == 0:
        fin_attn, fin_mlp = take(2)
    else:
        (y_out,) = take(1)
    held = dict(zip(STATE, take(9)))
    cosine, sine, x0, cots, lsem = take(5)
    mod = mods.at[layer]
    own_na, own_nb, own_dba, own_dbb, own_act, own_dpre, own_dpj = take(7)
    got_na, got_nb, got_dba, got_dbb, got_at, got_act, got_dpre, got_dpj = take(8)
    sbuf, rbuf, sbig, rbig, dmid, dnb, q_own, g_own, q_sh, g_sh, dq_own, dq_sh = take(12)
    wa, wm, mlp_grads, stage_attn = take(4)
    wsem, gsem, ss, rs, ss2, rs2, ss3, rs3, xs, xr = take(10)
    mlp_first = ReduceFirst(mlp_grads, MLP_SUM, shares, take(2), None, *take(3)[1:])
    rows_of = [slice(TOK * e, TOK * (e + 1)) for e in range(2)]
    x, ylo, z, yhi, c = here()
    places, me = row_places()
    partner = dev(x, ylo, z, yhi, 1 - c)
    if layer == 1:
        (ys,) = take(1)
        scattered = Scatter(y_out, *take(2))
    if layer == 0:
        mlp_rest = ReduceRest(MLP_SUM, last_shares, take(ReduceRest.count(MLP_SUM)))
        attn_first = ReduceFirst(before, ATTN_SUM, take(3), take(3), *take(3))
        attn_rest = ReduceRest(ATTN_SUM, attn_first.own, take(ReduceRest.count(ATTN_SUM)))
    entered = greet(dp_group() + reduce_greeted())
    loads = {}

    def load(name, src, dst):
        cp = pltpu.make_async_copy(src, dst, lsem.at[len(loads)])
        cp.start()
        loads[name] = cp

    def loaded(*names):
        for name in names:
            loads[name].wait()

    def load_state(name):
        for e in range(2):
            load((name, e), outer[name].at[layer + 2 * e], held[name].at[e])

    def state(name):
        loaded((name, 0), (name, 1))

    for e in range(2):
        load(("cots", e), cots_in.at[layer + 2 * e], cots.at[e])
    load_state("mid")
    load_state("bb")
    if layer == 0:
        load("x0", x0_in, x0)
        load(("y", 1), outer["y"].at[1], held["y"].at[1])
    else:
        load("y", outer["y"], ys)
    load_state("att")

    def wm_fetch(t):
        return pltpu.make_async_copy(wm_in.at[t], wm.at[t % 2], wsem.at[1 + t])

    wm_fetch(0).start()
    load_state("pre")
    wm_fetch(1).start()
    wa_fetch = pltpu.make_async_copy(wa_in, wa, wsem.at[0])
    wa_fetch.start()
    for name in ("ba", "qkv", "lse", "o"):
        load_state(name)
    load("cosine", cosine_in, cosine)
    load("sine", sine_in, sine)
    qkvs, lses, atts, bas, mids, pres, bbs, outputs = ([held[name].at[e] for e in range(2)] for name in STATE[1:])
    scale_a, gate_a = mod[1:2, :], mod[2:3, :]
    scale_b, gate_b = mod[4:5, :], mod[5:6, :]
    low = lanes((TOK, 128)) < 64
    exchanged = {}

    def hand(name, src, dst):
        n = len(exchanged)
        cp = push(src, dst, xs.at[n], xr.at[n], partner)
        cp.start()
        exchanged[name] = cp

    def have(*names):
        for name in names:
            exchanged[name].wait_send()
            exchanged[name].wait_recv()

    def gradient(e):
        dy = cots[e].astype(F32)
        return dy if more_dy is None else dy + more_dy[e]

    def entry(e):
        if layer == 1:
            return ys[2 * e].astype(F32)
        v = x0[...].astype(F32)
        return v + held["y"][1].astype(F32) if e else v

    loaded(("cots", 0), ("cots", 1))
    state("mid")
    state("bb")
    loaded(*(["x0", ("y", 1)] if layer == 0 else ["y"]))
    dgate_b = jnp.zeros((1, D), F32)
    for e in range(2):
        dy = gradient(e)
        dgate_b = dgate_b + jnp.sum(dy * bbs[e][...], axis=0, keepdims=True)
        own_dbb[rows_of[e], :] = (gate_b * dy).astype(BF)
        hat_b, _ = normalize(mids[e][...])
        own_nb[rows_of[e], :] = (hat_b * (1.0 + scale_b) + mod[3:4, :]).astype(BF)
        hat_a, _ = normalize(entry(e))
        own_na[rows_of[e], :] = (hat_a * (1.0 + scale_a) + mod[0:1, :]).astype(BF)
    entered()
    if layer == 1:
        for s in range(4):
            scattered.send(s, ys.at[s], True)
    hand("dbb", own_dbb, got_dbb)
    hand("nb", own_nb, got_nb)
    if layer == 0:
        mlp_rest.begin()
        attn_first.begin()
    state("pre")

    for t in range(4):
        wm_fetch(t).wait()
        d_act = nt(own_dbb[...], down_rows(wm.at[t % 2]))
        for e in range(2):
            act, slope = gelu_parts(pres[e][:, D * t : D * (t + 1)])
            own_act[t, rows_of[e], :] = act.astype(BF)
            own_dpre[t, rows_of[e], :] = (d_act[rows_of[e]] * slope).astype(BF)
        more = nt(own_dpre[t], up_rows(wm.at[t % 2]))
        dnb[...] = more if t == 0 else dnb[...] + more
        if t < 2:
            wm_fetch(t + 2).start()
    for h in range(2):
        hand(f"act{h}", own_act.at[2 * h + 1 - c], got_act.at[h])
        hand(f"dpre{h}", own_dpre.at[2 * h + 1 - c], got_dpre.at[h])

    hand("na", own_na, got_na)
    state("att")
    for e in range(2):
        hand(f"at{e}", atts[e], got_at.at[e])
    state("ba")
    dgate_a = jnp.zeros((1, D), F32)
    dscale_b = jnp.zeros((1, D), F32)
    dshift_b = jnp.zeros((1, D), F32)
    for e in range(2):
        hat_b, inv_b = normalize(mids[e][...])
        g = dnb[rows_of[e], :]
        dscale_b = dscale_b + jnp.sum(g * hat_b, axis=0, keepdims=True)
        dshift_b = dshift_b + jnp.sum(g, axis=0, keepdims=True)
        d_middle = gradient(e) + norm_back(g * (1.0 + scale_b), hat_b, inv_b)
        dmid[rows_of[e], :] = d_middle
        dgate_a = dgate_a + jnp.sum(d_middle * bas[e][...], axis=0, keepdims=True)
        own_dba[rows_of[e], :] = (gate_a * d_middle).astype(BF)
    hand("dba", own_dba, got_dba)
    wa_fetch.wait()
    for t in range(4):
        first = nt(own_dba[...], attn_rows(wa, t, 576, 704))
        second = nt(own_dba[...], attn_rows(wa, t, 640, 768))
        for e in range(2):
            sbuf[2 * t, e] = jnp.where(low, first[rows_of[e]], second[rows_of[e]]).astype(BF)
            sbuf[2 * t + 1, e] = second[rows_of[e]].astype(BF)
        for b in range(2):
            j = 2 * t + b
            deal(j, places[j][1], me, sbuf.at[j], rbuf.at[me], place_of(ss), place_of(rs))

    have("dbb", "nb", "act0", "dpre0", "act1", "dpre1")

    for h in range(2):
        t = 2 * h + c
        total = tn(own_nb[...], own_dpre[t]) + tn(got_nb[...], got_dpre[h])
        mlp_grads[h, 0:2] = total.astype(BF).reshape(2, 4, 2, 48, D)
        total = tn(own_act[t], own_dbb[...]) + tn(got_act[h], got_dbb[...])
        mlp_grads[h, 2:4] = total.astype(BF).reshape(2, 4, 2, 48, D)
    if layer == 0:
        mlp_first.begin()
    for j, where in places:
        dealt(j, where, me, sbuf.at[j], rbuf.at[j], place_of(ss), place_of(rs))

    if layer == 1:
        for s in range(4):
            scattered.send(s, ys.at[s], False)
            scattered.received(s)
        mlp_first.begin()
    state("qkv")
    state("lse")
    loaded("cosine", "sine")
    state("o")
    everyone = lanes((SEQ, 128)) < 64
    some = lanes((SEQ // 2, 128)) < 64
    row_of = lax.broadcasted_iota(jnp.int32, (8, 128), 0)
    picks = (row_of == jnp.where(lanes((8, 128)) < 64, 0, 1)).astype(F32)

    def shared_row(row):
        parts = []
        for a in range(4):
            first = row[:, 256 * a : 256 * a + 128]
            parts.append(jnp.where(c == 0, first, row[:, 256 * a + 128 : 256 * a + 256]))
        return jnp.concatenate(parts, axis=1)

    seg_own = segr[...]
    seg_sh = shared_row(seg_own)
    for e in range(2):
        qkv, lse = qkvs[e], lses[e]
        q_all = qkv[:, :, 0:128].reshape(SEQ, 128)
        g_all = rbuf[:, e].reshape(SEQ, 128)
        q_own[...] = jnp.where(everyone, q_all, 0).astype(BF)
        g_own[...] = jnp.where(everyone, g_all, 0).astype(BF)
        q_part = jnp.concatenate([qkv[2 * a + c, :, 0:128] for a in range(4)], axis=0)
        g_part = jnp.concatenate([rbuf[2 * a + c, e] for a in range(4)], axis=0)
        q_sh[...] = jnp.where(some, 0, q_part).astype(BF)
        g_sh[...] = jnp.where(some, 0, g_part).astype(BF)
        product = g_all.astype(F32) * outputs[e][...].reshape(SEQ, 128).astype(F32)
        centres = lax.dot_general(
            picks, product, (((1,), (1,)), ((), ())), precision=highest, preferred_element_type=F32
        )
        centre_own, centre_sh = centres[0:1, :], shared_row(centres[1:2, :])
        total_own = jnp.concatenate([lse[a, 0:1, 0:256] for a in range(4)], axis=1)
        total_sh = jnp.concatenate([lse[a, 0:1, 256:384] for a in range(4)], axis=1)

        for a in range(4):
            keys = qkv[2 * a : 2 * a + 2, :, 128:256].reshape(256, 128)
            values = qkv[2 * a : 2 * a + 2, :, 256:384].reshape(256, 128)
            seg_keys = segc[256 * a : 256 * (a + 1), :]

            def one(q, go, seg_q, total, centre, dq, keys=keys, values=values, seg_keys=seg_keys, a=a):
                scores = jnp.where(seg_keys == seg_q, nt(keys, q[...]), -1e30)
                p = jnp.exp(scores - total)
                d_s = (p * (nt(values, go[...]) - centre)).astype(BF)
                more = tn(d_s, keys)
                dq[...] = more if a == 0 else dq[...] + more
                return nn(d_s, q[...]), nn(p.astype(BF), go[...])

            dk1, dv1 = one(q_own, g_own, seg_own, total_own, centre_own, dq_own)
            dk2, dv2 = one(q_sh, g_sh, seg_sh, total_sh, centre_sh, dq_sh)
            dk, dv = dk1 + dk2, dv1 + dv2
            for b in range(2):
                j = 2 * a + b
                rows = slice(TOK * j, TOK * (j + 1))
                part = slice(TOK * b, TOK * (b + 1))
                sbig[j, e, :, 128:256] = turn(dk[part], cosine[rows, :], -sine[rows, :]).astype(BF)
                sbig[j, e, :, 256:384] = dv[part].astype(BF)
                deal(
                    j, places[j][1], me, sbig.at[j, e, :, pl.ds(128, 256)], rbig.at[me, e, :, pl.ds(128, 256)],
                    lambda i, e=e: ss2.at[e, i], lambda i, e=e: rs2.at[e, i],
                )
        for j, where in places:
            rows = slice(TOK * j, TOK * (j + 1))
            extra = dq_sh[TOK * (j // 2) : TOK * (j // 2 + 1), :]
            whole = jnp.where(low, dq_own[rows, :], jnp.where(c == j % 2, extra, 0.0)) * 0.125
            sbig[j, e, :, 0:128] = turn(whole, cosine[rows, :], -sine[rows, :]).astype(BF)
            deal(
                j, where, me, sbig.at[j, e, :, pl.ds(0, 128)], rbig.at[me, e, :, pl.ds(0, 128)],
                lambda i, e=e: ss3.at[e, i], lambda i, e=e: rs3.at[e, i],
            )
        if layer == 0 and e == 0:
            mlp_rest.sum_second()
            attn_first.sum()
            attn_rest.begin()
    for e in range(2):
        for j, where in places:
            dealt(
                j, where, me, sbig.at[j, e, :, pl.ds(128, 256)], rbig.at[j, e, :, pl.ds(128, 256)],
                lambda i, e=e: ss2.at[e, i], lambda i, e=e: rs2.at[e, i],
            )
            dealt(
                j, where, me, sbig.at[j, e, :, pl.ds(0, 128)], rbig.at[j, e, :, pl.ds(0, 128)],
                lambda i, e=e: ss3.at[e, i], lambda i, e=e: rs3.at[e, i],
            )
        for t in range(4):
            q0, k0, v0 = (rbig[2 * t, e, :, 128 * i : 128 * (i + 1)].astype(F32) for i in range(3))
            q1, k1, v1 = (rbig[2 * t + 1, e, :, 128 * i : 128 * (i + 1)].astype(F32) for i in range(3))
            tiles = (
                jnp.where(low, q0, swap(k0)),
                jnp.where(low, v0, swap(q1)),
                jnp.where(low, k1, swap(v1)),
                jnp.where(low, swap(q0 + q1), k0 + k1),
                jnp.where(low, swap(v0 + v1), 0.0),
            )
            for i, tile in enumerate(tiles):
                own_dpj[t, rows_of[e], 128 * i : 128 * (i + 1)] = tile.astype(BF)
    for h in range(2):
        hand(f"dpj{h}", own_dpj.at[2 * h + 1 - c], got_dpj.at[h])
    if layer == 0:
        attn_rest.sum_second()
    dna = jnp.zeros((2 * TOK, D), F32)
    for t in range(4):
        dna = dna + nn(own_dpj[t], attn_rows(wa, t, 0, 640))
    dscale_a = jnp.zeros((1, D), F32)
    dshift_a = jnp.zeros((1, D), F32)
    for e in range(2):
        hat_a, inv_a = normalize(entry(e))
        g = dna[rows_of[e]]
        dscale_a = dscale_a + jnp.sum(g * hat_a, axis=0, keepdims=True)
        dshift_a = dshift_a + jnp.sum(g, axis=0, keepdims=True)
        total = dmid[rows_of[e], :] + norm_back(g * (1.0 + scale_a), hat_a, inv_a)
        din[e] = total
        dinb[e] = total.astype(BF)
    for i, part in enumerate((dshift_a, dscale_a, dgate_a, dshift_b, dscale_b, dgate_b)):
        dmod[i : i + 1, :] = part
    dmod[6:8, :] = jnp.zeros((2, D), F32)

    have("na", "at0", "at1", "dba", "dpj0", "dpj1")
    for h in range(2):
        t = 2 * h + c
        copy = pltpu.make_async_copy(stage_attn, grads.at[h], gsem.at[0])
        if h:
            copy.wait()
        total = tn(own_dpj[t], own_na[...]) + tn(got_dpj[h], got_na[...])
        stage_attn[0:3] = total[0:576].astype(BF).reshape(3, 4, 3, 16, D)
        parts = []
        for first in (0, 512):
            cols = pl.ds(pl.multiple_of(first + 128 * t, 128), 128)
            total = jnp.zeros((128, D), F32)
            for e in range(2):
                total = total + tn(atts[e][:, cols], own_dba[rows_of[e], :])
                total = total + tn(got_at[e, :, cols], got_dba[rows_of[e], :])
            parts.append(total)
        total = jnp.concatenate([parts[0], parts[1][64:128]], axis=0)
        stage_attn[3] = total.astype(BF).reshape(4, 3, 16, D)
        copy.start()
    if layer == 0:
        mlp_rest.sum_third(fin_mlp)
        attn_rest.sum_third(fin_attn)
    mlp_first.sum()
    pltpu.make_async_copy(stage_attn, grads.at[1], gsem.at[0]).wait()


def backward(layer, *operands):
    dma = pltpu.SemaphoreType.DMA
    both = 2 * TOK

    def buf(*dims, dtype=BF):
        return pltpu.VMEM(dims, dtype)

    outs = [
        jax.ShapeDtypeStruct((2, TOK, D), F32),
        jax.ShapeDtypeStruct((2, TOK, D), BF),
        jax.ShapeDtypeStruct((8, D), F32),
        jax.ShapeDtypeStruct((2,) + ATTN, BF),
    ]
    outs += [jax.ShapeDtypeStruct(dims, BF) for dims in ReduceFirst.shapes(MLP_SUM, MLP_ROWS)]
    out_specs = [VM, VM, VM, ANY, VM, VM]
    if layer == 0:
        outs += [jax.ShapeDtypeStruct(dims, BF) for dims in ((3, 16, HALF), (2, 48, HALF))]
        out_specs += [VM, VM]
    else:
        outs.append(jax.ShapeDtypeStruct((2, 2, TOK, D), BF))
        out_specs.append(ANY)
    scratch = [buf(2, *dims, dtype=dtype) for dims, dtype in state_shapes()]
    scratch += [buf(SEQ, 128, dtype=F32)] * 2 + [buf(TOK, D), buf(2, TOK, D), dma((24,))]
    scratch += [buf(both, D)] * 4 + [buf(4, both, D)] * 2 + [buf(4, both, 640)]
    scratch += [buf(both, D)] * 4 + [buf(2, TOK, 1024)] + [buf(2, both, D)] * 2 + [buf(2, both, 640)]
    scratch += [buf(8, 2, TOK, 128)] * 2 + [buf(8, 2, TOK, 384)] * 2
    scratch += [buf(both, D, dtype=F32)] * 2 + [buf(SEQ, 128)] * 2 + [buf(SEQ // 2, 128)] * 2
    scratch += [buf(SEQ, 128, dtype=F32), buf(SEQ // 2, 128, dtype=F32)]
    scratch += [buf(4, *ATTN), buf(2, *MLP), buf(2, *MLP), buf(*ATTN)]
    scratch += [dma((5,)), dma((1,)), dma((8,)), dma((8,)), dma((2, 8)), dma((2, 8)), dma((2, 8)), dma((2, 8)), dma((12,)), dma((12,))]
    scratch += ReduceFirst.scratch(MLP_SUM, MLP_ROWS)
    if layer == 1:
        scratch += [buf(4, TOK, D), dma((4,)), dma((4,))]
    if layer == 0:
        scratch += ReduceRest.scratch(MLP_SUM, MLP_ROWS)
        scratch += [pltpu.VMEM(dims, BF) for dims in ReduceFirst.shapes(ATTN_SUM, ATTN_ROWS)]
        scratch += ReduceFirst.scratch(ATTN_SUM, ATTN_ROWS)
        scratch += ReduceRest.scratch(ATTN_SUM, ATTN_ROWS)
    vmem_in = 6 if layer == 0 else 3
    return pl.pallas_call(
        functools.partial(backward_kernel, layer),
        out_shape=tuple(outs),
        in_specs=[VM] * vmem_in + [ANY] * (len(operands) - vmem_in),
        out_specs=tuple(out_specs),
        scratch_shapes=scratch,
        compiler_params=pltpu.CompilerParams(
            collective_id=2 + layer, has_side_effects=True, vmem_limit_bytes=62 * 2**20
        ),
        name=f"backward_{layer}",
    )(*operands)


def finish_kernel(*refs):
    refs = list(refs)

    def take(count):
        got = refs[:count]
        del refs[:count]
        return got

    shares = take(2)
    fin_a1, fin_m1, dm0, dm1, feat, db0, db1 = take(7)
    (attn_grads,) = take(1)
    out_a0, out_m0, out_a1, out_m1, g_out, rows_out = take(6)
    fin_a0, fin_m0, dm_in, dsum = take(4)
    mlp_rest = ReduceRest(MLP_SUM, shares, take(ReduceRest.count(MLP_SUM)))
    attn_first = ReduceFirst(attn_grads, ATTN_SUM, take(3), take(3), *take(3))
    attn_rest = ReduceRest(ATTN_SUM, attn_first.own, take(ReduceRest.count(ATTN_SUM)))
    ag_a0 = Spread(out_a0, ("xzy", "xyz", "xzy"), *take(2), ring=True)
    ag_m0 = Spread(out_m0, ("zyx", "xzy"), *take(2), ring=True)
    ag_a1 = Spread(out_a1, ("xyz", "xzy", "xyz"), *take(2), ring=True)
    ag_m1 = Spread(out_m1, ("zyx", "yxz"), *take(2), ring=True)
    scattered = Scatter(g_out, *take(2))
    ms, mr, ms2, mr2, fsem = take(5)
    x, ylo, z, yhi, c = here()
    dp = 2 * x + ylo
    places, me = row_places()
    row = 2 * dp + yhi
    others = []
    for o in range(1, 16):
        r = (row + o) % 16
        others.append(dev(r // 4, (r // 2) % 2, z, r % 2, c))
    far = []
    for o in range(1, 8):
        g = (dp + o) % 8
        far += [(g, z, 2 * b + c) for b in range(2)]
    greet(dp_group() + far)()

    def place_in(n, fin, out):
        return pltpu.make_async_copy(fin, out.at[x, z, :, :, half(ylo)], fsem.at[n])

    settled = [place_in(0, fin_m1, out_m1), place_in(1, fin_a1, out_a1)]
    for cp in settled:
        cp.start()
    mlp_rest.begin()
    attn_first.begin()
    for cp in settled:
        cp.wait()
    ag_m1.start(0)
    ag_a1.start(0)
    for j, where in places:

        @pl.when(me != j)
        def _(j=j, where=where):
            push(dm0, dm_in.at[me, 0], ms.at[0, j], mr.at[0, me], where).start()
            push(dm1, dm_in.at[me, 1], ms.at[1, j], mr.at[1, me], where).start()

    mlp_rest.sum_second()
    attn_first.sum()
    attn_rest.begin()

    for j, where in places:

        @pl.when(me != j)
        def _(j=j, where=where):
            for l, ref in enumerate((dm0, dm1)):
                cp = push(ref, dm_in.at[j, l], ms.at[l, j], mr.at[l, j], where)
                cp.wait_send()
                cp.wait_recv()

        @pl.when(me == j)
        def _(j=j):
            dm_in[j, 0] = dm0[...]
            dm_in[j, 1] = dm1[...]

    total = dm_in[0]
    for j in range(1, 8):
        total = total + dm_in[j]
    lane = lax.broadcasted_iota(jnp.int32, (2, 8, D), 1)
    wide = jnp.concatenate([feat[...]] * 6, axis=1)
    high = wide.astype(BF).astype(F32)
    total = jnp.where(lane == 6, high, jnp.where(lane == 7, wide - high, total))
    dsum[...] = total.astype(BF)
    mlp_rest.sum_third(fin_m0)
    done = place_in(0, fin_m0, out_m0)
    done.start()
    attn_rest.sum_second()
    done.wait()
    ag_m0.start(0)
    moved = [push(dsum, rows_out.at[row], ms2.at[o], mr2.at[o], where) for o, where in enumerate(others)]
    for cp in moved:
        cp.start()
    keep = pltpu.make_async_copy(dsum, rows_out.at[row], fsem.at[2])
    keep.start()
    ag_m1.finish()
    ag_m1.start(1)
    ag_a1.finish()
    ag_a1.start(1)
    attn_rest.sum_third(fin_a0)
    done = place_in(1, fin_a0, out_a0)
    done.start()
    done.wait()
    ag_a0.start(0)
    ag_m0.finish()
    ag_m0.start(1)
    ag_a0.finish()
    ag_a0.start(1)
    ag_m1.finish()
    ag_m1.start(2)
    ag_a1.finish()
    ag_a1.start(2)
    ag_m0.finish()
    ag_m0.start(2)
    ag_a0.finish()
    ag_a0.start(2)
    for ag in (ag_m1, ag_a1, ag_m0, ag_a0):
        ag.relay()
    results = (db0.at[0], db1.at[0], db0.at[1], db1.at[1])
    for s in range(4):
        scattered.send(s, results[s], True)
    for ag in (ag_m1, ag_a1, ag_m0, ag_a0):
        ag.finish()
    keep.wait()
    for cp in moved:
        cp.wait()
    for s in range(4):
        scattered.send(s, results[s], False)
        scattered.received(s)


def finish(*operands):
    dma = pltpu.SemaphoreType.DMA
    shapes = [ATTN, MLP, ATTN, MLP, (2, 2, TOK, D)]
    scratch = [
        pltpu.VMEM((3, 16, HALF), BF),
        pltpu.VMEM((2, 48, HALF), BF),
        pltpu.VMEM((8, 2, 8, D), F32),
        pltpu.VMEM((2, 8, D), BF),
    ]
    scratch += ReduceRest.scratch(MLP_SUM, MLP_ROWS)
    scratch += [pltpu.VMEM(dims, BF) for dims in ReduceFirst.shapes(ATTN_SUM, ATTN_ROWS)]
    scratch += ReduceFirst.scratch(ATTN_SUM, ATTN_ROWS)
    scratch += ReduceRest.scratch(ATTN_SUM, ATTN_ROWS)
    scratch += [dma((30,))] * 8 + [dma((4,))] * 2
    scratch += [dma((2, 8)), dma((2, 8)), dma((15,)), dma((15,)), dma((3,))]
    return pl.pallas_call(
        finish_kernel,
        out_shape=tuple(
            [jax.ShapeDtypeStruct(dims, BF) for dims in shapes] + [jax.ShapeDtypeStruct((16, 2, 8, D), BF)]
        ),
        in_specs=[VM] * 9 + [ANY],
        out_specs=(ANY,) * 6,
        scratch_shapes=scratch,
        compiler_params=pltpu.CompilerParams(
            collective_id=4, has_side_effects=True, vmem_limit_bytes=62 * 2**20
        ),
        name="finish",
    )(*operands)


def modulation_kernel(rows, grad_mod, grad_bias):
    features = jnp.concatenate([rows[:, 0, 6, 0:128], rows[:, 0, 7, 0:128]], axis=0)
    for l in range(2):
        for i in range(6):
            cols = slice(D * i, D * (i + 1))
            d = rows[:, l, i, :]
            grad_mod[l, :, cols] = tn(features, jnp.concatenate([d, d], axis=0))
            grad_bias[l : l + 1, cols] = jnp.sum(d.astype(F32), axis=0, keepdims=True)


def modulation_grads(rows):
    return pl.pallas_call(
        modulation_kernel,
        out_shape=(
            jax.ShapeDtypeStruct((2, 128, 6 * D), F32),
            jax.ShapeDtypeStruct((2, 6 * D), F32),
        ),
        in_specs=[VM],
        out_specs=(VM, VM),
        compiler_params=pltpu.CompilerParams(vmem_limit_bytes=30 * 2**20),
        name="modulation_grads",
    )(rows)


def rotary(count):
    frequency = np.exp(-np.log(10000.0) * np.arange(32) / 32)
    angles = np.arange(count)[:, None] * frequency[None, :]
    cos, sin = np.cos(angles), np.sin(angles)
    tables = np.concatenate([cos] * 4, axis=1), np.concatenate([-sin, sin, -sin, sin], axis=1)
    ordered = (v.reshape(2, 4, TOK, 128).transpose(1, 0, 2, 3).reshape(count, 128) for v in tables)
    return tuple(v.astype(np.float32) for v in ordered)


def time_features(step_values, feature_count):
    half_count = feature_count // 2
    frequency = jnp.exp(-np.log(10000.0) * jnp.arange(half_count, dtype=F32) / half_count)
    angles = step_values.astype(F32)[:, None] * frequency[None, :]
    return jnp.concatenate([jnp.cos(angles), jnp.sin(angles)], axis=1)


def on_device(hidden_in, segments, timestep, w_qkv, w_out, w_up, w_down, w_mod, b_mod, cotangent):
    x, ylo, z, yhi, c = here()
    attn_loc = jnp.concatenate([jnp.swapaxes(w_qkv, 1, 2), w_out], axis=1).reshape((2,) + ATTN)
    up_loc = w_up.reshape(2, 2, 4, 2, 48, D)
    down_loc = w_down.reshape(2, 2, 4, 2, 48, D)

    mine = lax.dynamic_slice_in_dim(timestep, yhi, 1, 0)
    features = time_features(mine, w_mod.shape[1])
    modulation = jnp.einsum(
        "rf,lfm->lrm", features, w_mod.astype(F32), precision=highest
    ) + b_mod.astype(F32)[:, None, :]
    modulation = modulation.reshape(2, 6, D)
    seg = lax.dynamic_slice_in_dim(segments, yhi, 1, 0)
    seg = seg.reshape(2, 4, TOK).transpose(1, 0, 2).reshape(1, SEQ)
    segc, segr = seg.reshape(SEQ, 1), seg
    cosine, sine = (jnp.asarray(v) for v in rotary(SEQ))

    *state, x0, cots, wa0, wm0, wa1, wm1 = forward(
        hidden_in.reshape(2, 2, TOK, D),
        cotangent.reshape(2, 2, TOK, D),
        modulation,
        segc,
        segr,
        cosine,
        sine,
        attn_loc,
        up_loc,
        down_loc,
    )
    known = (cosine, sine, x0, cots, *state)
    din1, dinb1, dm1, ga1, *shares1, y_out = backward(1, modulation, segc, segr, *known, wa1, wm1)
    _, dinb0, dm0, ga0, *shares0, fin_a1, fin_m1 = backward(
        0, modulation, segc, segr, din1, *shares1, *known, wa0, wm0, ga1
    )
    out_a0, out_m0, out_a1, out_m1, g_out, rows = finish(
        *shares0, fin_a1, fin_m1, dm0, dm1, features, dinb0, dinb1, ga0
    )
    grad_mod, grad_bias = modulation_grads(rows)

    attn = jnp.stack([out_a0, out_a1]).reshape(2, D, D)
    mlp = jnp.stack([out_m0, out_m1]).reshape(2, 2 * D, D)
    return (
        y_out.reshape(1, 2, 2 * TOK, D),
        g_out.reshape(1, 2, 2 * TOK, D).astype(F32),
        attn[:, 0:576].swapaxes(1, 2).astype(F32),
        attn[:, 576:768].astype(F32),
        mlp[:, 0:768].astype(F32),
        mlp[:, 768:1536].astype(F32),
        grad_mod,
        grad_bias,
    )


def solution(mesh):
    placed = (
        P("dp", "tensor", None),
        P("dp", None),
        P("dp"),
        P(None, None, "tensor"),
        P(None, "tensor", None),
        P(None, None, "tensor"),
        P(None, "tensor", None),
        P(),
        P(),
        P("section", "dp", "tensor", None),
    )
    return jax.shard_map(
        on_device,
        mesh=mesh,
        in_specs=placed,
        out_specs=(
            P("section", "dp", "tensor", None),
            P("section", "dp", "tensor", None),
            P(None, None, "tensor"),
            P(None, "tensor", None),
            P(None, None, "tensor"),
            P(None, "tensor", None),
            P(),
            P(),
        ),
        check_vma=False,
    )
```
